256 devices in a mesh: seq: 16 (over x, y_lo, core), head: 16 (over z, y_hi).
Axes of the slice: x: 4, y: 4 (y_hi: 2, y_lo: 2; y = y_hi * 2 + y_lo), z: 8, core: 2. Of those that a mesh axis runs over, the one named last changes fastest.
Arguments:
- attn_out: bfloat16 [4096, 8192], P('seq', 'head'), may hold values from -6 to 6
- out_weight: bfloat16 [8192, 7168], P('head'), may hold values from -0.0625 to 0.0625
- residual: bfloat16 [4096, 7168], P(('seq', 'head')), may hold values from -6 to 6
- norm_gain: bfloat16 [7168], replicated, may hold values from 0.25 to 1.75
- latent_weight: bfloat16 [7168, 1536], P(None, 'head'), may hold values from -0.0625 to 0.0625
- index_proj: bfloat16 [7168, 64], P(None, 'head'), may hold values from -0.25 to 0.25
- latent_gain: bfloat16 [1536], replicated, may hold values from 0.25 to 1.75
- index_weight: bfloat16 [1536, 8192], P(None, 'head'), may hold values from -0.15625 to 0.15625
- index_keys: bfloat16 [16384, 128], P('seq'), may hold values from -6 to 6
- positions: int32 [4096], replicated, may hold values from 0 to 16383
- cache_len: int32 [16], P('seq'), may hold values from 256 to 1024, as said below
Outputs:
- hidden: bfloat16 [4096, 7168], P(('seq', 'head'))
- latent: bfloat16 [4096, 1536], P('seq', 'head')
- index_scores: float32 [4096, 16384], P('head', 'seq')
The draws below stay inside these ranges and needn't reach their ends.
Inputs may be any that keep to these rules, and one draw needn't show every extreme that they name: Cache block b holds keys in its first cache_len[b] slots; some block is full in every draw.
All inputs are finite; a program needn't handle non-finite values.
Results may differ from the reference program's by a relative error of at most 0.035.
Values may be sent and summed in bfloat16 or wider, within the bound.
No kernel may reach another device: no remote copies, remote signals or barrier semaphores. Data moves between devices by JAX's collectives and lax.ppermute only.
A program may use at most 128 MiB of HBM per device.

```python
import jax
import jax.numpy as jnp
from jax import lax

D = 7168
HEADS = 64
VDIM = 128
QL = 1536
IHEADS = 64
IDIM = 128
CACHE_DEV = 1024
TOKENS = 4096
CACHE = 16384
N_SEQ = 16
N_HEAD = 16


def draw_cache_len(key, part):
    key = jax.random.fold_in(key, 7)
    key_len, key_pick = jax.random.split(key)
    drawn = jax.random.randint(key_len, (N_SEQ,), CACHE_DEV // 4, CACHE_DEV + 1)
    chosen = jax.random.randint(key_pick, (), 0, N_SEQ)
    return jnp.where(jnp.arange(N_SEQ) == chosen, CACHE_DEV, drawn).astype(jnp.int32)


def with_ends(values, key, low, top_value):
    longest = values.shape.index(max(values.shape))
    spots = []
    for shift in (0, 1):
        where = [jax.random.randint(jax.random.fold_in(key, axis), (), 0, length) for axis, length in enumerate(values.shape)]
        where[longest] = (where[longest] + shift) % values.shape[longest]
        spots.append(tuple(where))
    return values.at[spots[0]].set(low).at[spots[1]].set(top_value)


def steps_of(stream_key, shape, cuts, smallest, largest):
    level = 1.0
    for axis_at, blocks in cuts:
        steps = jax.random.uniform(jax.random.fold_in(jax.random.fold_in(stream_key, 6), axis_at), (blocks,), jnp.float32, smallest / len(cuts), largest / len(cuts))
        level = level * jnp.repeat(jnp.exp(steps), shape[axis_at] // blocks).reshape((-1,) + (1,) * (len(shape) - 1 - axis_at))
    return level


def noise(own_key, shape, deviation, bound, cuts=(), kind=jnp.bfloat16):
    level = steps_of(own_key, shape, cuts, -0.22, 0.18) if cuts else 1.0
    array = jax.random.normal(own_key, shape, jnp.float32) * deviation * level
    return jnp.minimum(jnp.maximum(array, -bound), bound).astype(kind)


def setup_inputs(seed: int = 0) -> dict:
    seeds = jax.random.split(jax.random.key(seed), 12)
    return {
        "attn_out": noise(seeds[0], (TOKENS, HEADS * VDIM), 1.0, 6.0, ((0, 16), (1, 16))),
        "out_weight": noise(seeds[1], (HEADS * VDIM, D), (HEADS * VDIM) ** -0.5, 0.0625, ((0, 16),)),
        "residual": noise(seeds[2], (TOKENS, D), 1.0, 6.0, ((0, 256),)),
        "norm_gain": jnp.clip(1.0 + 0.15 * jax.random.normal(seeds[3], (D,), jnp.float32), 0.25, 1.75).astype(jnp.bfloat16),
        "latent_weight": noise(seeds[4], (D, QL), D ** -0.5, 0.0625, ((1, 16),)),
        "index_proj": noise(seeds[5], (D, IHEADS), (D // 16) ** -0.5, 0.25, ((1, 16),)),
        "latent_gain": jnp.clip(1.0 + 0.15 * jax.random.normal(seeds[6], (QL,), jnp.float32), 0.25, 1.75).astype(jnp.bfloat16),
        "index_weight": noise(seeds[7], (QL, IHEADS * IDIM), QL ** -0.5, 0.15625, ((1, 16),)),
        "index_keys": noise(seeds[8], (CACHE, IDIM), 1.0, 6.0, ((0, 16),)),
        "positions": with_ends(jax.random.randint(seeds[9], (TOKENS,), 0, CACHE), jax.random.fold_in(seeds[9], 1), 0, CACHE - 1).astype(jnp.int32),
        "cache_len": draw_cache_len(jax.random.fold_in(seeds[11], 71), 0),
    }


EPSILON = 1e-06

def rms_round(values, gain):
    widened = values.astype(jnp.float32)
    inverse = lax.rsqrt(lax.optimization_barrier(jnp.mean(widened * widened, axis=-1, keepdims=True)) + EPSILON)
    return (widened * inverse * gain.astype(jnp.float32)).astype(jnp.bfloat16)

def score_block(query_rows, weight_rows, keys_all):
    count = query_rows.shape[0]
    group = 8 if IHEADS % 8 == 0 else 1
    scale = IDIM ** (-0.5)
    keys_wide = keys_all.astype(jnp.float32)

    def add_group(step, total):
        q_part = lax.dynamic_slice_in_dim(query_rows, step * group * IDIM, group * IDIM, 1)
        q_part = q_part.reshape(count, group, IDIM).astype(jnp.float32)
        w_part = lax.dynamic_slice_in_dim(weight_rows, step * group, group, 1).astype(jnp.float32)
        logits = jnp.einsum('njd,sd->njs', q_part, keys_wide, precision=lax.Precision.HIGHEST) * scale
        return total + jnp.einsum('njs,nj->ns', jnp.maximum(logits, 0.0), w_part, precision=lax.Precision.HIGHEST)
    return lax.fori_loop(0, IHEADS // group, add_group, jnp.zeros((count, keys_all.shape[0]), jnp.float32))

def reference(attn_out, out_weight, residual, norm_gain, latent_weight, index_proj, latent_gain, index_weight, index_keys, positions, cache_len):
    group_cols = HEADS * VDIM // N_HEAD

    def add_partial(index, total):
        cols = lax.dynamic_slice_in_dim(attn_out, index * group_cols, group_cols, 1)
        rows = lax.dynamic_slice_in_dim(out_weight, index * group_cols, group_cols, 0)
        part = jnp.dot(cols, rows, preferred_element_type=jnp.float32).astype(jnp.bfloat16)
        part = lax.optimization_barrier(part)
        return total + part.astype(jnp.float32)
    projected = lax.fori_loop(0, N_HEAD, add_partial, jnp.zeros((TOKENS, D), jnp.float32))
    hidden = (projected + residual.astype(jnp.float32)).astype(jnp.bfloat16)
    normed = rms_round(hidden, norm_gain)
    latent_raw = jnp.dot(normed, latent_weight, preferred_element_type=jnp.float32).astype(jnp.bfloat16)
    head_weights = (jnp.dot(normed, index_proj, preferred_element_type=jnp.float32) * IHEADS ** (-0.5)).astype(jnp.bfloat16)
    latent = rms_round(latent_raw, latent_gain)
    queries = jnp.dot(latent, index_weight, preferred_element_type=jnp.float32).astype(jnp.bfloat16)
    block_rows = 128 if TOKENS % 128 == 0 else TOKENS
    q_blocks = queries.reshape(TOKENS // block_rows, block_rows, IHEADS * IDIM)
    w_blocks = head_weights.reshape(TOKENS // block_rows, block_rows, IHEADS)

    def one_block(pair):
        return score_block(pair[0], pair[1], index_keys)
    scores = lax.map(one_block, (q_blocks, w_blocks)).reshape(TOKENS, CACHE)
    slot_all = jnp.arange(CACHE, dtype=jnp.int32)
    block_of = (slot_all // CACHE_DEV).astype(jnp.int32)
    filled = slot_all % CACHE_DEV < cache_len[block_of]
    visible = filled[None, :] & (slot_all[None, :] <= positions[:, None])
    index_scores = jnp.where(visible, scores, jnp.float32(0.0))
    return (hidden, latent, index_scores)
```

```python
import functools

import jax
import jax.numpy as jnp
from jax import lax
from jax.experimental import pallas as pl
from jax.experimental.pallas import tpu as pltpu
from jax.sharding import Mesh
from jax.sharding import PartitionSpec as P

D = 7168
QL = 1536
IHEADS = 64
IDIM = 128
N_SEQ = 16
N_HEAD = 16
NZ = 8
DZ = D // NZ
EPSILON = 1e-06
SEQ = ("x", "yl", "c")
HEAD = ("z", "yh")
WIDE = 512 + 128


def rms_round(values, gain):
    widened = values.astype(jnp.float32)
    inverse = lax.rsqrt(jnp.mean(widened * widened, axis=-1, keepdims=True) + EPSILON)
    return (widened * inverse * gain.astype(jnp.float32)).astype(jnp.bfloat16)


def swap(values, axis):
    return lax.ppermute(values, axis, [(0, 1), (1, 0)])


def in_order(mine, other, index, axis):
    first = jnp.where(index == 0, mine, other)
    second = jnp.where(index == 0, other, mine)
    return jnp.stack([first, second], axis=axis)


def project_kernel(a_ref, b_ref, o_ref):
    o_ref[0] = jnp.dot(a_ref[...], b_ref[...], preferred_element_type=jnp.float32).astype(o_ref.dtype)


def project(attn_out, out_weight):
    rows, depth = attn_out.shape
    return pl.pallas_call(
        project_kernel,
        grid=(NZ,),
        in_specs=[
            pl.BlockSpec((rows, depth), lambda i: (0, 0)),
            pl.BlockSpec((depth, DZ), lambda i: (0, i)),
        ],
        out_specs=pl.BlockSpec((1, rows, DZ), lambda i: (i, 0, 0)),
        out_shape=jax.ShapeDtypeStruct((NZ, rows, DZ), jnp.bfloat16),
        compiler_params=pltpu.CompilerParams(vmem_limit_bytes=32 * 1024 * 1024),
    )(attn_out, out_weight)


def query_kernel(latent_ref, weight_ref, heads_ref, pick_ref, o_ref):
    o_ref[:, :512] = jnp.dot(
        latent_ref[...], weight_ref[...], preferred_element_type=jnp.float32
    ).astype(jnp.bfloat16)
    o_ref[:, 512:] = jnp.dot(
        heads_ref[...], pick_ref[...], preferred_element_type=jnp.float32
    ).astype(jnp.bfloat16)


def make_queries(latent, weight, heads, pick):
    rows = latent.shape[0]
    return pl.pallas_call(
        query_kernel,
        out_shape=jax.ShapeDtypeStruct((rows, WIDE), jnp.bfloat16),
        compiler_params=pltpu.CompilerParams(vmem_limit_bytes=32 * 1024 * 1024),
    )(latent, weight, heads, pick)


def score_kernel(limits_ref, q_ref, k_ref, pos_ref, o_ref):
    step = pl.program_id(0)
    scale = IDIM ** (-0.5)
    rows, slots = o_ref.shape
    tile_rows, tile_slots = 64, 256

    @pl.when(step == 0)
    def _():
        o_ref[...] = jnp.zeros_like(o_ref)

    for at in range(0, rows, tile_rows):
        weights = [
            jnp.broadcast_to(
                q_ref[0, at : at + tile_rows, 512 : 640].astype(jnp.float32)[:, j : j + 1] * scale,
                (tile_rows, tile_slots),
            )
            for j in range(4)
        ]
        for slot in range(0, slots, tile_slots):
            total = o_ref[at : at + tile_rows, slot : slot + tile_slots]
            for j in range(4):
                logits = jnp.dot(
                    q_ref[0, at : at + tile_rows, j * IDIM : (j + 1) * IDIM],
                    k_ref[:, slot : slot + tile_slots],
                    preferred_element_type=jnp.float32,
                )
                total = total + jnp.maximum(logits, 0.0) * weights[j]
            o_ref[at : at + tile_rows, slot : slot + tile_slots] = total

    @pl.when(step == pl.num_programs(0) - 1)
    def _():
        local = lax.broadcasted_iota(jnp.int32, (tile_rows, slots), 1)
        for at in range(0, rows, tile_rows):
            reach = jnp.minimum(limits_ref[0], pos_ref[at : at + tile_rows, :] - limits_ref[1] + 1)
            o_ref[at : at + tile_rows, :] = jnp.where(
                local < reach, o_ref[at : at + tile_rows, :], 0.0
            )


def make_scores(limits, queries, keys_t, own_positions):
    chunks, rows, _ = queries.shape
    slots = keys_t.shape[1]
    return pl.pallas_call(
        score_kernel,
        grid=(chunks,),
        in_specs=[
            pl.BlockSpec(memory_space=pltpu.SMEM),
            pl.BlockSpec((1, rows, WIDE), lambda i: (i, 0, 0)),
            pl.BlockSpec((IDIM, slots), lambda i: (0, 0)),
            pl.BlockSpec((rows, 1), lambda i: (0, 0)),
        ],
        out_specs=pl.BlockSpec((rows, slots), lambda i: (0, 0)),
        out_shape=jax.ShapeDtypeStruct((rows, slots), jnp.float32),
        compiler_params=pltpu.CompilerParams(vmem_limit_bytes=32 * 1024 * 1024),
    )(limits, queries, keys_t, own_positions)


def down_weight_rows(latent_weight, index_proj, z, yl, yh, x, c):
    piece = c * 8 + x * 2 + yl
    share = DZ // N_SEQ

    def own_rows(weight):
        return lax.dynamic_slice_in_dim(weight.reshape(NZ, DZ, weight.shape[1]), piece * share, share, 1)

    own = jnp.concatenate([own_rows(latent_weight), own_rows(index_proj)], axis=2)
    mine = lax.all_to_all(own, "z", 0, 0)
    both = in_order(mine, swap(mine, "yh"), yh, 1)
    by_head = both.reshape(N_HEAD, share, own.shape[2]).transpose(1, 0, 2)
    local = latent_weight.shape[1]
    wide = jnp.concatenate(
        [by_head[:, :, :local].reshape(share, QL), by_head[:, :, local:].reshape(share, IHEADS)], axis=1
    )
    half = lax.all_to_all(jnp.broadcast_to(wide[None], (8,) + wide.shape), ("x", "yl"), 0, 0)
    half = half.reshape(8 * share, wide.shape[1])
    return in_order(half, swap(half, "c"), c, 0).reshape(DZ, wide.shape[1])


def shards(
    attn_out,
    out_weight,
    residual,
    norm_gain,
    latent_weight,
    index_proj,
    latent_gain,
    index_weight,
    index_keys,
    positions,
    cache_len,
):
    x, yl, c = (lax.axis_index(a) for a in SEQ)
    z, yh = (lax.axis_index(a) for a in HEAD)
    seq = (x * 2 + yl) * 2 + c
    head = z * 2 + yh
    rows = attn_out.shape[0]
    own = rows // N_HEAD

    partial = project(attn_out, out_weight)
    summed = lax.psum_scatter(partial, "z", scatter_dimension=0, tiled=False)

    down = down_weight_rows(latent_weight, index_proj, z, yl, yh, x, c)
    residual_cols = lax.all_to_all(residual.reshape(own, NZ, DZ).transpose(1, 0, 2), "z", 0, 0)

    halves = summed.reshape(NZ, 2, own, DZ)
    kept = lax.dynamic_index_in_dim(halves, yh, 1, keepdims=False)
    given = lax.dynamic_index_in_dim(halves, 1 - yh, 1, keepdims=False)
    got = swap(given, "yh")
    hidden = (
        kept.astype(jnp.float32) + got.astype(jnp.float32) + residual_cols.astype(jnp.float32)
    ).astype(jnp.bfloat16)
    wide_hidden = hidden.reshape(NZ * own, DZ).astype(jnp.float32)
    gain = lax.dynamic_slice_in_dim(norm_gain, z * DZ, DZ).astype(jnp.float32)
    squares = jnp.sum(wide_hidden * wide_hidden, axis=1, keepdims=True)
    high = lax.reduce_precision(squares, 8, 7)
    lifted = jnp.dot(
        (wide_hidden * gain).astype(jnp.bfloat16), down, preferred_element_type=jnp.float32
    )
    lifted = jnp.concatenate(
        [
            lifted.astype(jnp.bfloat16),
            high.astype(jnp.bfloat16),
            (squares - high).astype(jnp.bfloat16),
            jnp.zeros((NZ * own, 62), jnp.bfloat16),
        ],
        axis=1,
    )
    parts = lax.all_to_all(lifted.reshape(NZ, own, lifted.shape[1]), "z", 0, 0)
    total = jnp.sum(parts.astype(jnp.float32), axis=0)
    mean = (total[:, 1600:1601] + total[:, 1601:1602]) / D
    inverse = lax.rsqrt(mean + EPSILON)
    latent_raw = (total[:, :QL] * inverse).astype(jnp.bfloat16)
    head_weights = (total[:, QL:1600] * inverse * IHEADS ** (-0.5)).astype(jnp.bfloat16)
    latent = rms_round(latent_raw, latent_gain)
    packed = jnp.concatenate([latent, head_weights, jnp.zeros((own, 64), jnp.bfloat16)], axis=1)
    pair = in_order(packed, swap(packed, "yh"), yh, 0)
    everyone = lax.all_gather(pair, "z", axis=0, tiled=False).reshape(rows, packed.shape[1])
    latent_full = everyone[:, :QL]
    latent_out = lax.dynamic_slice_in_dim(latent_full, head * 96, 96, 1)
    pick = (
        lax.broadcasted_iota(jnp.int32, (128, 128), 0)
        == lax.broadcasted_iota(jnp.int32, (128, 128), 1) + head * 4
    ) & (lax.broadcasted_iota(jnp.int32, (128, 128), 1) < 4)
    queries = make_queries(latent_full, index_weight, everyone[:, QL:], pick.astype(jnp.bfloat16))
    turned = lax.ppermute(
        queries, SEQ + HEAD, [(s * N_HEAD + h, h * N_HEAD + s) for s in range(N_SEQ) for h in range(N_HEAD)]
    )
    hidden, turned = lax.optimization_barrier((hidden, turned))
    hidden_rows = lax.all_to_all(hidden, "z", 0, 0).transpose(1, 0, 2).reshape(own, D)
    all_queries = lax.all_gather(turned, SEQ, axis=0, tiled=False)
    own_positions = lax.dynamic_slice_in_dim(positions, head * rows, rows).reshape(rows, 1)
    limits = jnp.stack([cache_len[0], seq * index_keys.shape[0]]).astype(jnp.int32)
    scores = make_scores(limits, all_queries, index_keys.T, own_positions)
    return (hidden_rows, latent_out, scores)


def solution(mesh):
    fine = Mesh(mesh.devices.reshape(4, 2, 2, 8, 2), SEQ + HEAD)
    in_specs = (
        P(SEQ, HEAD),
        P(HEAD, None),
        P(SEQ + HEAD, None),
        P(),
        P(None, HEAD),
        P(None, HEAD),
        P(),
        P(None, HEAD),
        P(SEQ, None),
        P(),
        P(SEQ),
    )
    out_specs = (P(SEQ + HEAD, None), P(SEQ, HEAD), P(HEAD, SEQ))
    return jax.shard_map(shards, mesh=fine, in_specs=in_specs, out_specs=out_specs, check_vma=False)
```

```python
import functools

import jax
import jax.numpy as jnp
from jax import lax
from jax.experimental import pallas as pl
from jax.experimental.pallas import tpu as pltpu
from jax.sharding import Mesh
from jax.sharding import PartitionSpec as P

D = 7168
QL = 1536
IHEADS = 64
IDIM = 128
N_SEQ = 16
N_HEAD = 16
NZ = 8
DZ = D // NZ
EPSILON = 1e-06
SEQ = ("x", "yl", "c")
HEAD = ("z", "yh")
HALF = 128
SLOTS = 1024
WIDE = 1024 + 128


def rms_round(values, gain):
    widened = values.astype(jnp.float32)
    inverse = lax.rsqrt(jnp.mean(widened * widened, axis=-1, keepdims=True) + EPSILON)
    return (widened * inverse * gain.astype(jnp.float32)).astype(jnp.bfloat16)


def swap(values, axis):
    return lax.ppermute(values, axis, [(0, 1), (1, 0)])


def shift(values, axis, size, by):
    return lax.ppermute(values, axis, [(i, (i + by) % size) for i in range(size)])


def kernel_params():
    return pltpu.CompilerParams(vmem_limit_bytes=48 * 1024 * 1024)


def project_kernel(a_ref, b_ref, o_ref):
    product = jnp.dot(a_ref[...], b_ref[...], preferred_element_type=jnp.float32).astype(o_ref.dtype)
    for group in range(NZ):
        for half in range(2):
            o_ref[0, half, group * 16 : (group + 1) * 16, :] = product[
                group * 32 + half * 16 : group * 32 + (half + 1) * 16, :
            ]


def project(attn_out, out_weight):
    rows, depth = attn_out.shape
    return pl.pallas_call(
        project_kernel,
        grid=(NZ,),
        in_specs=[
            pl.BlockSpec((rows, depth), lambda i: (0, 0)),
            pl.BlockSpec((depth, DZ), lambda i: (0, i)),
        ],
        out_specs=pl.BlockSpec((1, 2, HALF, DZ), lambda i: (i, 0, 0, 0)),
        out_shape=jax.ShapeDtypeStruct((NZ, 2, HALF, DZ), jnp.bfloat16),
        compiler_params=pltpu.CompilerParams(vmem_limit_bytes=60 * 1024 * 1024),
    )(attn_out, out_weight)


def lift_kernel(core_ref, kept_ref, got_ref, res_ref, gain_ref, mine_ref, other_ref, hidden_ref, o_ref):
    hidden = (
        kept_ref[...].astype(jnp.float32)
        + got_ref[...].astype(jnp.float32)
        + res_ref[...].astype(jnp.float32)
    ).astype(jnp.bfloat16)
    hidden_ref[...] = hidden
    wide = hidden.astype(jnp.float32)
    squares = jnp.sum(wide * wide, axis=1, keepdims=True)
    high = squares.astype(jnp.bfloat16).astype(jnp.float32)
    scaled = wide * gain_ref[...].astype(jnp.float32)
    first, second = scaled[:, : DZ // 2], scaled[:, DZ // 2 :]
    is_first = core_ref[0] == 0
    mine = jnp.where(is_first, first, second).astype(jnp.bfloat16)
    other = jnp.where(is_first, second, first).astype(jnp.bfloat16)
    lifted = jnp.dot(mine, mine_ref[...], preferred_element_type=jnp.float32) + jnp.dot(
        other, other_ref[...], preferred_element_type=jnp.float32
    )
    lane = lax.broadcasted_iota(jnp.int32, (HALF, 128), 1)
    tail = jnp.where(lane == IHEADS, high, jnp.where(lane == IHEADS + 1, squares - high, 0.0))
    o_ref[:, :QL] = lifted[:, :QL].astype(jnp.bfloat16)
    o_ref[:, QL:] = jnp.where(lane < IHEADS, lifted[:, QL:], tail).astype(jnp.bfloat16)


def lift(core, kept, got, residual, gain, mine, other):
    whole = pl.BlockSpec(memory_space=pltpu.VMEM)
    return pl.pallas_call(
        lift_kernel,
        in_specs=[pl.BlockSpec(memory_space=pltpu.SMEM)] + [whole] * 6,
        out_specs=[whole, whole],
        out_shape=[
            jax.ShapeDtypeStruct((HALF, DZ), jnp.bfloat16),
            jax.ShapeDtypeStruct((HALF, QL + 128), jnp.bfloat16),
        ],
        compiler_params=kernel_params(),
    )(core, kept, got, residual, gain, mine, other)


def query_kernel(latent_ref, own_ref, other_ref, pick_ref, o_ref):
    latent = latent_ref[:, :QL]
    o_ref[:, :512] = jnp.dot(latent, own_ref[...], preferred_element_type=jnp.float32).astype(jnp.bfloat16)
    o_ref[:, 512:1024] = jnp.dot(latent, other_ref[...], preferred_element_type=jnp.float32).astype(
        jnp.bfloat16
    )
    o_ref[:, 1024:] = jnp.dot(
        latent_ref[:, QL:], pick_ref[...], preferred_element_type=jnp.float32
    ).astype(jnp.bfloat16)


def make_queries(latent, own, other, pick):
    whole = pl.BlockSpec(memory_space=pltpu.VMEM)
    return pl.pallas_call(
        query_kernel,
        in_specs=[whole] * 4,
        out_specs=whole,
        out_shape=jax.ShapeDtypeStruct((HALF, WIDE), jnp.bfloat16),
        compiler_params=kernel_params(),
    )(latent, own, other, pick)


def score_kernel(count, first, *refs):
    pieces, k_ref = refs[:count], refs[count]
    before, o_ref = (None if first else refs[count + 1]), refs[-1]
    scale = IDIM ** (-0.5)
    rows, slots = o_ref.shape
    tile_rows, tile_slots = 64, 256
    for at in range(0, rows, tile_rows):
        weights = [piece[at : at + tile_rows, 1024:].astype(jnp.float32) * scale for piece in pieces]
        for slot in range(0, slots, tile_slots):
            here = (slice(at, at + tile_rows), slice(slot, slot + tile_slots))
            total = jnp.zeros((tile_rows, tile_slots), jnp.float32) if first else before[here]
            for piece, weight in zip(pieces, weights):
                for j in range(8):
                    logits = jnp.dot(
                        piece[at : at + tile_rows, j * IDIM : (j + 1) * IDIM],
                        k_ref[:, slot : slot + tile_slots],
                        preferred_element_type=jnp.float32,
                    )
                    total = total + jnp.maximum(logits, 0.0) * weight[:, j : j + 1]
            o_ref[here] = total


def add_scores(pieces, keys_t, before):
    count, slots, block = len(pieces), keys_t.shape[1], 512
    tile = pl.BlockSpec((HALF, block), lambda i: (0, i))
    specs = [pl.BlockSpec((HALF, WIDE), lambda i: (0, 0))] * count
    specs += [pl.BlockSpec((IDIM, block), lambda i: (0, i))]
    args = list(pieces) + [keys_t]
    if before is not None:
        specs.append(tile)
        args.append(before)
    return pl.pallas_call(
        functools.partial(score_kernel, count, before is None),
        grid=(slots // block,),
        in_specs=specs,
        out_specs=tile,
        out_shape=jax.ShapeDtypeStruct((HALF, slots), jnp.float32),
        compiler_params=kernel_params(),
        cost_estimate=pl.CostEstimate(
            flops=2 * count * 8 * HALF * slots * IDIM * 2, bytes_accessed=2 * HALF * slots * 4, transcendentals=0
        ),
    )(*args)


def finish_kernel(numbers_ref, own_ref, got_ref, pos_ref, o_ref):
    local = lax.broadcasted_iota(jnp.int32, (16, SLOTS), 1)
    core, filled, base = numbers_ref[0], numbers_ref[1], numbers_ref[2]
    for group in range(NZ):
        own = own_ref[group * 16 : (group + 1) * 16, :]
        got = got_ref[group * 16 : (group + 1) * 16, :]
        for half in range(2):
            at = group * 32 + half * 16
            reach = jnp.minimum(filled, pos_ref[at : at + 16, :] - base + 1)
            rows = jnp.where(core == half, own, got)
            o_ref[at : at + 16, :] = jnp.where(local < reach, rows, 0.0)


def finish(numbers, own, got, own_positions):
    whole = pl.BlockSpec(memory_space=pltpu.VMEM)
    return pl.pallas_call(
        finish_kernel,
        in_specs=[pl.BlockSpec(memory_space=pltpu.SMEM), whole, whole, whole],
        out_specs=whole,
        out_shape=jax.ShapeDtypeStruct((2 * HALF, SLOTS), jnp.float32),
        compiler_params=kernel_params(),
    )(numbers, own, got, own_positions)


def down_weight_rows(latent_weight, index_proj, x, yl, c):
    piece = c * 8 + x * 2 + yl
    share = DZ // N_SEQ

    def own_rows(weight):
        return lax.dynamic_slice_in_dim(weight.reshape(NZ, DZ, weight.shape[1]), piece * share, share, 1)

    own = jnp.concatenate([own_rows(latent_weight), own_rows(index_proj)], axis=2)
    by_head = lax.all_to_all(jnp.repeat(own, 2, axis=0), HEAD, 0, 0).transpose(1, 0, 2)
    local = latent_weight.shape[1]
    wide = jnp.concatenate(
        [
            by_head[:, :, :local].reshape(share, QL),
            by_head[:, :, local:].reshape(share, IHEADS),
            jnp.zeros((share, 64), jnp.bfloat16),
        ],
        axis=1,
    )
    half = lax.all_to_all(jnp.broadcast_to(wide[None], (8,) + wide.shape), ("x", "yl"), 0, 0)
    half = half.reshape(8 * share, wide.shape[1])
    return half, swap(half, "c")


def turn(queries):
    moves = []
    for at in range(N_SEQ * N_HEAD):
        s, h = divmod(at, N_HEAD)
        pair, core = divmod(s, 2)
        level, high = divmod(h, 2)
        moves.append((at, ((pair ^ level) * 2 + high) * N_HEAD + pair * 2 + core))
    return lax.ppermute(queries, SEQ + HEAD, moves)


def shards(
    attn_out,
    out_weight,
    residual,
    norm_gain,
    latent_weight,
    index_proj,
    latent_gain,
    index_weight,
    index_keys,
    positions,
    cache_len,
):
    x, yl, c = (lax.axis_index(a) for a in SEQ)
    z, yh = (lax.axis_index(a) for a in HEAD)
    seq = (x * 2 + yl) * 2 + c
    head = z * 2 + yh
    rows = attn_out.shape[0]
    own = rows // N_HEAD
    local = latent_weight.shape[1]

    partial = project(attn_out, out_weight)
    summed = lax.psum_scatter(partial, "z", scatter_dimension=0, tiled=False)

    down_mine, down_other = down_weight_rows(latent_weight, index_proj, x, yl, c)
    residual_cols = lax.all_to_all(residual.reshape(own, NZ, DZ).transpose(1, 0, 2), "z", 0, 0)
    weight_other = swap(index_weight, "yh")
    keys_other = swap(index_keys, "c")
    keys_t = jnp.concatenate([index_keys, keys_other], axis=0).T

    kept = lax.dynamic_index_in_dim(summed, yh, 0, keepdims=False)
    got = swap(lax.dynamic_index_in_dim(summed, 1 - yh, 0, keepdims=False), "yh")
    gain = lax.dynamic_slice_in_dim(norm_gain, z * DZ, DZ).reshape(1, DZ)
    core = jnp.stack([c]).astype(jnp.int32)
    hidden, lifted = lift(
        core, kept, got, residual_cols.reshape(HALF, DZ), gain, down_mine, down_other
    )
    parts = lax.all_to_all(lifted.reshape(NZ, own, lifted.shape[1]), "z", 0, 0)
    total = jnp.sum(parts.astype(jnp.float32), axis=0)
    mean = (total[:, 1600:1601] + total[:, 1601:1602]) / D
    inverse = lax.rsqrt(mean + EPSILON)
    latent_raw = (total[:, :QL] * inverse).astype(jnp.bfloat16)
    head_weights = (total[:, QL:1600] * inverse * IHEADS ** (-0.5)).astype(jnp.bfloat16)
    latent = rms_round(latent_raw, latent_gain)
    packed = jnp.concatenate([latent, head_weights, jnp.zeros((own, 64), jnp.bfloat16)], axis=1)
    everyone = lax.all_to_all(jnp.broadcast_to(packed[None], (NZ,) + packed.shape), "z", 0, 0)
    everyone = everyone.reshape(HALF, packed.shape[1])

    lane = lax.broadcasted_iota(jnp.int32, (128, 128), 1)
    source = jnp.where(lane < 4, head * 4 + lane, (head ^ 1) * 4 + lane - 4)
    pick = (lax.broadcasted_iota(jnp.int32, (128, 128), 0) == source) & (lane < 8)
    queries = make_queries(everyone, index_weight, weight_other, pick.astype(jnp.bfloat16))
    queries, everyone, hidden = lax.optimization_barrier((queries, everyone, hidden))

    piece = turn(queries)
    hidden_rows = lax.all_to_all(hidden.reshape(NZ, own, DZ), "z", 0, 0).transpose(1, 0, 2).reshape(own, D)
    latent_mine = lax.dynamic_slice_in_dim(everyone, head * local, local, 1).reshape(NZ, own, local)
    latent_give = lax.dynamic_slice_in_dim(everyone, (head ^ 1) * local, local, 1)
    latent_got = swap(latent_give, "yh").reshape(NZ, own, local)
    latent_out = jnp.stack(
        [jnp.where(yh == 0, latent_mine, latent_got), jnp.where(yh == 0, latent_got, latent_mine)], axis=1
    ).reshape(rows, local)

    beside = swap(piece, "yl")
    right, left = shift(piece, "x", 4, 1), shift(piece, "x", 4, -1)
    scores = add_scores([piece], keys_t, None)
    beside_right, beside_left = shift(beside, "x", 4, 1), shift(beside, "x", 4, -1)
    across = shift(right, "x", 4, 1)
    scores = add_scores([beside, right, left], keys_t, scores)
    beside_across = shift(beside_left, "x", 4, -1)
    scores = add_scores([beside_right, beside_left], keys_t, scores)
    scores = add_scores([across, beside_across], keys_t, scores)
    got_scores = swap(scores[:, SLOTS:], "c")
    own_positions = lax.dynamic_slice_in_dim(positions, head * rows, rows).reshape(rows, 1)
    numbers = jnp.stack([c, cache_len[0], seq * SLOTS]).astype(jnp.int32)
    return (hidden_rows, latent_out, finish(numbers, scores[:, :SLOTS], got_scores, own_positions))


def solution(mesh):
    fine = Mesh(mesh.devices.reshape(4, 2, 2, 8, 2), SEQ + HEAD)
    in_specs = (
        P(SEQ, HEAD),
        P(HEAD, None),
        P(SEQ + HEAD, None),
        P(),
        P(None, HEAD),
        P(None, HEAD),
        P(),
        P(None, HEAD),
        P(SEQ, None),
        P(),
        P(SEQ),
    )
    out_specs = (P(SEQ + HEAD, None), P(SEQ, HEAD), P(HEAD, SEQ))
    return jax.shard_map(shards, mesh=fine, in_specs=in_specs, out_specs=out_specs, check_vma=False)
```

```python
import functools

import jax
import jax.numpy as jnp
from jax import lax
from jax.experimental import pallas as pl
from jax.experimental.pallas import tpu as pltpu
from jax.sharding import Mesh
from jax.sharding import PartitionSpec as P

D = 7168
QL = 1536
IHEADS = 64
IDIM = 128
N_SEQ = 16
N_HEAD = 16
NZ = 8
DZ = D // NZ
EPSILON = 1e-06
SEQ = ("x", "yl", "c")
HEAD = ("z", "yh")
HALF = 128
SLOTS = 1024
WIDE = 1024


def rms_round(values, gain):
    widened = values.astype(jnp.float32)
    inverse = lax.rsqrt(jnp.mean(widened * widened, axis=-1, keepdims=True) + EPSILON)
    return (widened * inverse * gain.astype(jnp.float32)).astype(jnp.bfloat16)


def swap(values, axis):
    return lax.ppermute(values, axis, [(0, 1), (1, 0)])


def shift(values, axis, size, by):
    return lax.ppermute(values, axis, [(i, (i + by) % size) for i in range(size)])


def kernel_params():
    return pltpu.CompilerParams(vmem_limit_bytes=48 * 1024 * 1024)


def project_kernel(a_ref, b_ref, o_ref):
    product = jnp.dot(a_ref[...], b_ref[...], preferred_element_type=jnp.float32).astype(o_ref.dtype)
    for group in range(NZ):
        for half in range(2):
            o_ref[0, half, group * 16 : (group + 1) * 16, :] = product[
                group * 32 + half * 16 : group * 32 + (half + 1) * 16, :
            ]


def project(attn_out, out_weight):
    rows, depth = attn_out.shape
    return pl.pallas_call(
        project_kernel,
        grid=(NZ,),
        in_specs=[
            pl.BlockSpec((rows, depth), lambda i: (0, 0)),
            pl.BlockSpec((depth, DZ), lambda i: (0, i)),
        ],
        out_specs=pl.BlockSpec((1, 2, HALF, DZ), lambda i: (i, 0, 0, 0)),
        out_shape=jax.ShapeDtypeStruct((NZ, 2, HALF, DZ), jnp.bfloat16),
        compiler_params=pltpu.CompilerParams(vmem_limit_bytes=60 * 1024 * 1024),
    )(attn_out, out_weight)


def lift_kernel(core_ref, kept_ref, got_ref, res_ref, gain_ref, mine_ref, other_ref, hidden_ref, o_ref):
    hidden = (
        kept_ref[...].astype(jnp.float32)
        + got_ref[...].astype(jnp.float32)
        + res_ref[...].astype(jnp.float32)
    ).astype(jnp.bfloat16)
    hidden_ref[...] = hidden
    wide = hidden.astype(jnp.float32)
    squares = jnp.sum(wide * wide, axis=1, keepdims=True)
    high = squares.astype(jnp.bfloat16).astype(jnp.float32)
    scaled = wide * gain_ref[...].astype(jnp.float32)
    first, second = scaled[:, : DZ // 2], scaled[:, DZ // 2 :]
    is_first = core_ref[0] == 0
    mine = jnp.where(is_first, first, second).astype(jnp.bfloat16)
    other = jnp.where(is_first, second, first).astype(jnp.bfloat16)
    lifted = jnp.dot(mine, mine_ref[...], preferred_element_type=jnp.float32) + jnp.dot(
        other, other_ref[...], preferred_element_type=jnp.float32
    )
    lane = lax.broadcasted_iota(jnp.int32, (HALF, 128), 1)
    tail = jnp.where(lane == IHEADS, high, jnp.where(lane == IHEADS + 1, squares - high, 0.0))
    o_ref[:, :QL] = lifted[:, :QL].astype(jnp.bfloat16)
    o_ref[:, QL:] = jnp.where(lane < IHEADS, lifted[:, QL:], tail).astype(jnp.bfloat16)


def lift(core, kept, got, residual, gain, mine, other):
    whole = pl.BlockSpec(memory_space=pltpu.VMEM)
    return pl.pallas_call(
        lift_kernel,
        in_specs=[pl.BlockSpec(memory_space=pltpu.SMEM)] + [whole] * 6,
        out_specs=[whole, whole],
        out_shape=[
            jax.ShapeDtypeStruct((HALF, DZ), jnp.bfloat16),
            jax.ShapeDtypeStruct((HALF, QL + 128), jnp.bfloat16),
        ],
        compiler_params=kernel_params(),
    )(core, kept, got, residual, gain, mine, other)


def query_kernel(latent_ref, own_ref, other_ref, first_ref, second_ref):
    latent = latent_ref[:, :QL]
    first_ref[...] = jnp.dot(latent, own_ref[...], preferred_element_type=jnp.float32).astype(jnp.bfloat16)
    second_ref[...] = jnp.dot(latent, other_ref[...], preferred_element_type=jnp.float32).astype(jnp.bfloat16)


def make_queries(latent, own, other):
    whole = pl.BlockSpec(memory_space=pltpu.VMEM)
    shape = jax.ShapeDtypeStruct((HALF, own.shape[1]), jnp.bfloat16)
    return pl.pallas_call(
        query_kernel,
        in_specs=[whole] * 3,
        out_specs=[whole, whole],
        out_shape=[shape, shape],
        compiler_params=kernel_params(),
    )(latent, own, other)


def score_kernel(count, first, groups_ref, w_ref, *refs):
    pieces, k_ref = refs[:count], refs[count]
    before, o_ref = (None if first else refs[count + 1]), refs[-1]
    scale = IDIM ** (-0.5)
    rows, slots = o_ref.shape
    tile_rows, tile_slots = 64, 256
    lane = lax.broadcasted_iota(jnp.int32, (128, 128), 1)
    row = lax.broadcasted_iota(jnp.int32, (128, 128), 0)
    picked = []
    for n in range(count):
        source = jnp.where(lane < 4, groups_ref[2 * n] * 4 + lane, groups_ref[2 * n + 1] * 4 + lane - 4)
        pick = jnp.where((row == source) & (lane < 8), 1.0, 0.0).astype(jnp.bfloat16)
        picked.append(jnp.dot(w_ref[...], pick, preferred_element_type=jnp.float32) * scale)
    for at in range(0, rows, tile_rows):
        for slot in range(0, slots, tile_slots):
            here = (slice(at, at + tile_rows), slice(slot, slot + tile_slots))
            total = jnp.zeros((tile_rows, tile_slots), jnp.float32) if first else before[here]
            for piece, weight in zip(pieces, picked):
                for j in range(8):
                    logits = jnp.dot(
                        piece[at : at + tile_rows, j * IDIM : (j + 1) * IDIM],
                        k_ref[:, slot : slot + tile_slots],
                        preferred_element_type=jnp.float32,
                    )
                    total = total + jnp.maximum(logits, 0.0) * weight[at : at + tile_rows, j : j + 1]
            o_ref[here] = total


def add_scores(pieces, groups, head_weights, keys_t, before):
    count, slots, block = len(pieces), keys_t.shape[1], 512
    tile = pl.BlockSpec((HALF, block), lambda i: (0, i))
    specs = [pl.BlockSpec(memory_space=pltpu.SMEM), pl.BlockSpec((HALF, 128), lambda i: (0, 0))]
    specs += [pl.BlockSpec((HALF, WIDE), lambda i: (0, 0))] * count
    specs += [pl.BlockSpec((IDIM, block), lambda i: (0, i))]
    args = [jnp.stack(groups).astype(jnp.int32), head_weights] + list(pieces) + [keys_t]
    if before is not None:
        specs.append(tile)
        args.append(before)
    return pl.pallas_call(
        functools.partial(score_kernel, count, before is None),
        grid=(slots // block,),
        in_specs=specs,
        out_specs=tile,
        out_shape=jax.ShapeDtypeStruct((HALF, slots), jnp.float32),
        compiler_params=kernel_params(),
        cost_estimate=pl.CostEstimate(
            flops=4 * count * 8 * HALF * slots * IDIM, bytes_accessed=2 * HALF * slots * 4, transcendentals=0
        ),
    )(*args)


def finish_kernel(numbers_ref, own_ref, got_ref, pos_ref, o_ref):
    local = lax.broadcasted_iota(jnp.int32, (16, SLOTS), 1)
    core, filled, base = numbers_ref[0], numbers_ref[1], numbers_ref[2]
    for group in range(NZ):
        own = own_ref[group * 16 : (group + 1) * 16, :]
        got = got_ref[group * 16 : (group + 1) * 16, :]
        for half in range(2):
            at = group * 32 + half * 16
            reach = jnp.minimum(filled, pos_ref[at : at + 16, :] - base + 1)
            rows = jnp.where(core == half, own, got)
            o_ref[at : at + 16, :] = jnp.where(local < reach, rows, 0.0)


def finish(numbers, own, got, own_positions):
    whole = pl.BlockSpec(memory_space=pltpu.VMEM)
    return pl.pallas_call(
        finish_kernel,
        in_specs=[pl.BlockSpec(memory_space=pltpu.SMEM), whole, whole, whole],
        out_specs=whole,
        out_shape=jax.ShapeDtypeStruct((2 * HALF, SLOTS), jnp.float32),
        compiler_params=kernel_params(),
    )(numbers, own, got, own_positions)


def down_weight_rows(latent_weight, index_proj, x, yl, c):
    piece = c * 8 + x * 2 + yl
    share = DZ // N_SEQ

    def own_rows(weight):
        return lax.dynamic_slice_in_dim(weight.reshape(NZ, DZ, weight.shape[1]), piece * share, share, 1)

    own = jnp.concatenate([own_rows(latent_weight), own_rows(index_proj)], axis=2)
    by_head = lax.all_to_all(jnp.repeat(own, 2, axis=0), HEAD, 0, 0).transpose(1, 0, 2)
    local = latent_weight.shape[1]
    wide = jnp.concatenate(
        [
            by_head[:, :, :local].reshape(share, QL),
            by_head[:, :, local:].reshape(share, IHEADS),
            jnp.zeros((share, 64), jnp.bfloat16),
        ],
        axis=1,
    )
    half = lax.all_to_all(jnp.broadcast_to(wide[None], (8,) + wide.shape), ("x", "yl"), 0, 0)
    half = half.reshape(8 * share, wide.shape[1])
    return half, swap(half, "c")


def spread(values, flip):
    moves = []
    for at in range(N_SEQ * N_HEAD):
        s, h = divmod(at, N_HEAD)
        moves.append((at, ((((s // 2) ^ (h // 2) ^ flip) * 2) + s % 2) * N_HEAD + h))
    return lax.ppermute(values, SEQ + HEAD, moves)


def cross(values, flip):
    moves = []
    for at in range(N_SEQ * N_HEAD):
        s, h = divmod(at, N_HEAD)
        (pair, core), (z, high) = divmod(s, 2), divmod(h, 2)
        moves.append((at, (pair * 2 + high) * N_HEAD + (pair ^ z ^ flip) * 2 + core))
    return lax.ppermute(values, SEQ + HEAD, moves)


def shards(
    attn_out,
    out_weight,
    residual,
    norm_gain,
    latent_weight,
    index_proj,
    latent_gain,
    index_weight,
    index_keys,
    positions,
    cache_len,
):
    x, yl, c = (lax.axis_index(a) for a in SEQ)
    z, yh = (lax.axis_index(a) for a in HEAD)
    seq = (x * 2 + yl) * 2 + c
    head = z * 2 + yh
    rows = attn_out.shape[0]
    own = rows // N_HEAD
    local = latent_weight.shape[1]

    partial = project(attn_out, out_weight)
    summed = lax.psum_scatter(partial, "z", scatter_dimension=0, tiled=False)

    down_mine, down_other = down_weight_rows(latent_weight, index_proj, x, yl, c)
    residual_cols = lax.all_to_all(residual.reshape(own, NZ, DZ).transpose(1, 0, 2), "z", 0, 0)
    weight_other = swap(index_weight, "yh")
    keys_other = swap(index_keys, "c")
    keys_t = jnp.concatenate([index_keys, keys_other], axis=0).T

    summed, residual_cols, down_mine, down_other, weight_other, keys_t = lax.optimization_barrier(
        (summed, residual_cols, down_mine, down_other, weight_other, keys_t)
    )
    kept = lax.dynamic_index_in_dim(summed, yh, 0, keepdims=False)
    got = swap(lax.dynamic_index_in_dim(summed, 1 - yh, 0, keepdims=False), "yh")
    gain = lax.dynamic_slice_in_dim(norm_gain, z * DZ, DZ).reshape(1, DZ)
    core = jnp.stack([c]).astype(jnp.int32)
    hidden, lifted = lift(
        core, kept, got, residual_cols.reshape(HALF, DZ), gain, down_mine, down_other
    )
    parts = lax.all_to_all(lifted.reshape(NZ, own, lifted.shape[1]), "z", 0, 0)
    total = jnp.sum(parts.astype(jnp.float32), axis=0)
    mean = (total[:, 1600:1601] + total[:, 1601:1602]) / D
    inverse = lax.rsqrt(mean + EPSILON)
    latent_raw = (total[:, :QL] * inverse).astype(jnp.bfloat16)
    head_weights = (total[:, QL:1600] * inverse * IHEADS ** (-0.5)).astype(jnp.bfloat16)
    latent = rms_round(latent_raw, latent_gain)
    packed = jnp.concatenate([latent, head_weights, jnp.zeros((own, 64), jnp.bfloat16)], axis=1)
    everyone = lax.all_to_all(jnp.broadcast_to(packed[None], (NZ,) + packed.shape), "z", 0, 0)
    everyone = everyone.reshape(HALF, packed.shape[1])

    first, second = make_queries(everyone, index_weight, weight_other)
    first, second, everyone, hidden = lax.optimization_barrier((first, second, everyone, hidden))
    all_weights = everyone[:, QL:]
    moved = (spread(first, 0), spread(second, 4), spread(all_weights, 0))
    hidden_rows = lax.all_to_all(hidden.reshape(NZ, own, DZ), "z", 0, 0).transpose(1, 0, 2).reshape(own, D)
    latent_mine = lax.dynamic_slice_in_dim(everyone, head * local, local, 1).reshape(NZ, own, local)
    latent_give = lax.dynamic_slice_in_dim(everyone, (head ^ 1) * local, local, 1)
    latent_got = swap(latent_give, "yh").reshape(NZ, own, local)
    first, second, all_weights = cross(moved[0], 0), cross(moved[1], 4), cross(moved[2], 0)
    first, second, all_weights, hidden_rows, latent_got = lax.optimization_barrier(
        (first, second, all_weights, hidden_rows, latent_got)
    )
    latent_out = jnp.stack(
        [jnp.where(yh == 0, latent_mine, latent_got), jnp.where(yh == 0, latent_got, latent_mine)], axis=1
    ).reshape(rows, local)

    def groups(*steps):
        out = []
        for dx, dy in steps:
            level = (((x + dx) % 4) * 2 + (yl ^ dy)) ^ z
            out += [level * 2 + c, (level ^ 4) * 2 + (c ^ 1)]
        return out

    def add(pieces, steps, before):
        return add_scores(pieces, groups(*steps), all_weights, keys_t, before)

    piece = jnp.concatenate([first, second], axis=1)
    beside = swap(piece, "yl")
    right, left = shift(piece, "x", 4, 1), shift(piece, "x", 4, -1)
    scores = add([piece], [(0, 0)], None)
    beside_right, beside_left = shift(beside, "x", 4, 1), shift(beside, "x", 4, -1)
    across = shift(right, "x", 4, 1)
    scores = add([beside, right, left], [(0, 1), (-1, 0), (1, 0)], scores)
    beside_across = shift(beside_left, "x", 4, -1)
    scores = add([beside_right, beside_left], [(-1, 1), (1, 1)], scores)
    scores = add([across, beside_across], [(2, 0), (2, 1)], scores)
    got_scores = swap(scores[:, SLOTS:], "c")
    own_positions = lax.dynamic_slice_in_dim(positions, head * rows, rows).reshape(rows, 1)
    numbers = jnp.stack([c, cache_len[0], seq * SLOTS]).astype(jnp.int32)
    return (hidden_rows, latent_out, finish(numbers, scores[:, :SLOTS], got_scores, own_positions))


def solution(mesh):
    fine = Mesh(mesh.devices.reshape(4, 2, 2, 8, 2), SEQ + HEAD)
    in_specs = (
        P(SEQ, HEAD),
        P(HEAD, None),
        P(SEQ + HEAD, None),
        P(),
        P(None, HEAD),
        P(None, HEAD),
        P(),
        P(None, HEAD),
        P(SEQ, None),
        P(),
        P(SEQ),
    )
    out_specs = (P(SEQ + HEAD, None), P(SEQ, HEAD), P(HEAD, SEQ))
    return jax.shard_map(shards, mesh=fine, in_specs=in_specs, out_specs=out_specs, check_vma=False)
```

```python
import functools

import jax
import jax.numpy as jnp
from jax import lax
from jax.experimental import pallas as pl
from jax.experimental.pallas import tpu as pltpu
from jax.sharding import Mesh
from jax.sharding import PartitionSpec as P

D = 7168
QL = 1536
IHEADS = 64
IDIM = 128
N_SEQ = 16
N_HEAD = 16
NZ = 8
DZ = D // NZ
EPSILON = 1e-06
SEQ = ("x", "yl", "c")
HEAD = ("z", "yh")
HALF = 128
SLOTS = 1024


def rms_round(values, gain):
    widened = values.astype(jnp.float32)
    inverse = lax.rsqrt(jnp.mean(widened * widened, axis=-1, keepdims=True) + EPSILON)
    return (widened * inverse * gain.astype(jnp.float32)).astype(jnp.bfloat16)


def swap(values, axis):
    return lax.ppermute(values, axis, [(0, 1), (1, 0)])


def shift(values, axis, size, by):
    return lax.ppermute(values, axis, [(i, (i + by) % size) for i in range(size)])


def kernel_params():
    return pltpu.CompilerParams(vmem_limit_bytes=48 * 1024 * 1024)


def project_kernel(a_ref, b_ref, o_ref):
    product = jnp.dot(a_ref[...], b_ref[...], preferred_element_type=jnp.float32).astype(o_ref.dtype)
    for group in range(NZ):
        for half in range(2):
            o_ref[0, half, group * 16 : (group + 1) * 16, :] = product[
                group * 32 + half * 16 : group * 32 + (half + 1) * 16, :
            ]


def project(attn_out, out_weight):
    rows, depth = attn_out.shape
    return pl.pallas_call(
        project_kernel,
        grid=(NZ,),
        in_specs=[
            pl.BlockSpec((rows, depth), lambda i: (0, 0)),
            pl.BlockSpec((depth, DZ), lambda i: (0, i)),
        ],
        out_specs=pl.BlockSpec((1, 2, HALF, DZ), lambda i: (i, 0, 0, 0)),
        out_shape=jax.ShapeDtypeStruct((NZ, 2, HALF, DZ), jnp.bfloat16),
        compiler_params=pltpu.CompilerParams(vmem_limit_bytes=60 * 1024 * 1024),
    )(attn_out, out_weight)


def lift_kernel(core_ref, kept_ref, got_ref, res_ref, gain_ref, mine_ref, other_ref, hidden_ref, o_ref):
    hidden = (
        kept_ref[...].astype(jnp.float32)
        + got_ref[...].astype(jnp.float32)
        + res_ref[...].astype(jnp.float32)
    ).astype(jnp.bfloat16)
    hidden_ref[...] = hidden
    wide = hidden.astype(jnp.float32)
    squares = jnp.sum(wide * wide, axis=1, keepdims=True)
    high = squares.astype(jnp.bfloat16).astype(jnp.float32)
    scaled = wide * gain_ref[...].astype(jnp.float32)
    first, second = scaled[:, : DZ // 2], scaled[:, DZ // 2 :]
    is_first = core_ref[0] == 0
    mine = jnp.where(is_first, first, second).astype(jnp.bfloat16)
    other = jnp.where(is_first, second, first).astype(jnp.bfloat16)
    lifted = jnp.dot(mine, mine_ref[...], preferred_element_type=jnp.float32) + jnp.dot(
        other, other_ref[...], preferred_element_type=jnp.float32
    )
    lane = lax.broadcasted_iota(jnp.int32, (HALF, 128), 1)
    tail = jnp.where(lane == IHEADS, high, jnp.where(lane == IHEADS + 1, squares - high, 0.0))
    o_ref[:, :QL] = lifted[:, :QL].astype(jnp.bfloat16)
    o_ref[:, QL:] = jnp.where(lane < IHEADS, lifted[:, QL:], tail).astype(jnp.bfloat16)


def lift(core, kept, got, residual, gain, mine, other):
    whole = pl.BlockSpec(memory_space=pltpu.VMEM)
    return pl.pallas_call(
        lift_kernel,
        in_specs=[pl.BlockSpec(memory_space=pltpu.SMEM)] + [whole] * 6,
        out_specs=[whole, whole],
        out_shape=[
            jax.ShapeDtypeStruct((HALF, DZ), jnp.bfloat16),
            jax.ShapeDtypeStruct((HALF, QL + 128), jnp.bfloat16),
        ],
        compiler_params=kernel_params(),
    )(core, kept, got, residual, gain, mine, other)


def query_kernel(place_ref, latent_ref, own_ref, mine_ref, theirs_ref, o_ref):
    core, high = place_ref[0], place_ref[1]
    is_first = core == 0
    left, right = latent_ref[:, : QL // 2], latent_ref[:, QL // 2 : QL]
    here = jnp.where(is_first, left, right)
    there = jnp.where(is_first, right, left)
    own = jnp.dot(latent_ref[:, :QL], own_ref[...], preferred_element_type=jnp.float32)
    other = jnp.dot(here, mine_ref[...], preferred_element_type=jnp.float32) + jnp.dot(
        there, theirs_ref[...], preferred_element_type=jnp.float32
    )
    for at, part in ((high * 4, own), ((1 - high) * 4, other)):
        part = part.astype(jnp.bfloat16)
        for j in range(4):
            for block in range(NZ):
                o_ref[block, at + j] = part[block * 16 : (block + 1) * 16, j * IDIM : (j + 1) * IDIM]


def make_queries(place, latent, own, mine, theirs):
    whole = pl.BlockSpec(memory_space=pltpu.VMEM)
    return pl.pallas_call(
        query_kernel,
        in_specs=[pl.BlockSpec(memory_space=pltpu.SMEM)] + [whole] * 4,
        out_specs=whole,
        out_shape=jax.ShapeDtypeStruct((NZ, 8, 16, IDIM), jnp.bfloat16),
        compiler_params=kernel_params(),
    )(place, latent, own, mine, theirs)


def score_kernel(q_ref, w_ref, k_ref, o_ref, wide_ref):
    scale = IDIM ** (-0.5)
    tile = 256

    @pl.when(pl.program_id(0) == 0)
    def _():
        weights = w_ref[...].astype(jnp.float32) * scale
        for j in range(IHEADS):
            wide_ref[j * 16 : (j + 1) * 16, :] = jnp.broadcast_to(weights[:, j : j + 1], (16, 128))

    blocks, _, slots = o_ref.shape
    for block in range(blocks):
        for slot in range(0, slots, tile):
            at = block * slots + slot
            logits = lax.dot_general(
                q_ref[...],
                k_ref[at : at + tile, :],
                (((1,), (1,)), ((), ())),
                preferred_element_type=jnp.float32,
            )
            halves = [jnp.zeros((16, 128), jnp.float32), jnp.zeros((16, 128), jnp.float32)]
            for j in range(IHEADS):
                weight = wide_ref[j * 16 : (j + 1) * 16, :]
                for n in range(2):
                    halves[n] += (
                        jnp.maximum(logits[j * 16 : (j + 1) * 16, n * 128 : (n + 1) * 128], 0.0) * weight
                    )
            for n in range(2):
                o_ref[block, :, slot + n * 128 : slot + (n + 1) * 128] = halves[n].astype(o_ref.dtype)


def make_scores(queries, head_weights, keys):
    per_step = 2
    return pl.pallas_call(
        score_kernel,
        grid=(N_SEQ // per_step,),
        in_specs=[
            pl.BlockSpec((IHEADS * 16, IDIM), lambda i: (0, 0)),
            pl.BlockSpec((16, 128), lambda i: (0, 0)),
            pl.BlockSpec((per_step * SLOTS, IDIM), lambda i: (i, 0)),
        ],
        out_specs=pl.BlockSpec((per_step, 16, SLOTS), lambda i: (i, 0, 0)),
        out_shape=jax.ShapeDtypeStruct((N_SEQ, 16, SLOTS), jnp.bfloat16),
        scratch_shapes=[pltpu.VMEM((IHEADS * 16, 128), jnp.float32)],
        compiler_params=kernel_params(),
    )(queries, head_weights, keys)


def finish_kernel(numbers_ref, s_ref, pos_ref, o_ref):
    local = lax.broadcasted_iota(jnp.int32, (16, SLOTS), 1)
    filled, base = numbers_ref[0], numbers_ref[1]
    for group in range(N_SEQ):
        here = slice(group * 16, (group + 1) * 16)
        reach = jnp.minimum(filled, pos_ref[here, :] - base + 1)
        o_ref[here, :] = jnp.where(local < reach, s_ref[group].astype(jnp.float32), 0.0)


def finish(numbers, scores, own_positions):
    whole = pl.BlockSpec(memory_space=pltpu.VMEM)
    return pl.pallas_call(
        finish_kernel,
        in_specs=[pl.BlockSpec(memory_space=pltpu.SMEM), whole, whole],
        out_specs=whole,
        out_shape=jax.ShapeDtypeStruct((N_SEQ * 16, SLOTS), jnp.float32),
        compiler_params=kernel_params(),
    )(numbers, scores, own_positions)


def down_weight_rows(latent_weight, index_proj, x, yl, c):
    piece = c * 8 + x * 2 + yl
    share = DZ // N_SEQ

    def own_rows(weight):
        return lax.dynamic_slice_in_dim(weight.reshape(NZ, DZ, weight.shape[1]), piece * share, share, 1)

    own = jnp.concatenate([own_rows(latent_weight), own_rows(index_proj)], axis=2)
    by_head = lax.all_to_all(jnp.repeat(own, 2, axis=0), HEAD, 0, 0).transpose(1, 0, 2)
    local = latent_weight.shape[1]
    wide = jnp.concatenate(
        [
            by_head[:, :, :local].reshape(share, QL),
            by_head[:, :, local:].reshape(share, IHEADS),
            jnp.zeros((share, 64), jnp.bfloat16),
        ],
        axis=1,
    )
    half = lax.all_to_all(jnp.broadcast_to(wide[None], (8,) + wide.shape), ("x", "yl"), 0, 0)
    half = half.reshape(8 * share, wide.shape[1])
    return half, swap(half, "c")


def turn(values):
    moves = [(s * N_HEAD + h, h * N_HEAD + s) for s in range(N_SEQ) for h in range(N_HEAD)]
    return lax.ppermute(values, SEQ + HEAD, moves)


def shards(
    attn_out,
    out_weight,
    residual,
    norm_gain,
    latent_weight,
    index_proj,
    latent_gain,
    index_weight,
    index_keys,
    positions,
    cache_len,
):
    x, yl, c = (lax.axis_index(a) for a in SEQ)
    z, yh = (lax.axis_index(a) for a in HEAD)
    seq = (x * 2 + yl) * 2 + c
    head = z * 2 + yh
    rows = attn_out.shape[0]
    own = rows // N_HEAD
    local = latent_weight.shape[1]

    partial = project(attn_out, out_weight)
    summed = lax.psum_scatter(partial, "z", scatter_dimension=0, tiled=False)

    down_mine, down_other = down_weight_rows(latent_weight, index_proj, x, yl, c)
    residual_cols = lax.all_to_all(residual.reshape(own, NZ, DZ).transpose(1, 0, 2), "z", 0, 0)
    depth = QL // 2
    weight_mine = swap(lax.dynamic_slice_in_dim(index_weight, c * depth, depth, 0), "yh")
    weight_theirs = swap(weight_mine, "c")
    (summed, residual_cols, down_mine, down_other, weight_mine, weight_theirs, index_keys) = (
        lax.optimization_barrier(
            (summed, residual_cols, down_mine, down_other, weight_mine, weight_theirs, index_keys)
        )
    )
    all_keys = lax.all_gather(index_keys, SEQ, axis=0, tiled=True)
    kept = lax.dynamic_index_in_dim(summed, yh, 0, keepdims=False)
    got = swap(lax.dynamic_index_in_dim(summed, 1 - yh, 0, keepdims=False), "yh")
    gain = lax.dynamic_slice_in_dim(norm_gain, z * DZ, DZ).reshape(1, DZ)
    core = jnp.stack([c]).astype(jnp.int32)
    hidden, lifted = lift(
        core, kept, got, residual_cols.reshape(HALF, DZ), gain, down_mine, down_other
    )
    parts = lax.all_to_all(lifted.reshape(NZ, own, lifted.shape[1]), "z", 0, 0)
    total = jnp.sum(parts.astype(jnp.float32), axis=0)
    mean = (total[:, 1600:1601] + total[:, 1601:1602]) / D
    inverse = lax.rsqrt(mean + EPSILON)
    latent_raw = (total[:, :QL] * inverse).astype(jnp.bfloat16)
    head_weights = (total[:, QL:1600] * inverse * IHEADS ** (-0.5)).astype(jnp.bfloat16)
    latent = rms_round(latent_raw, latent_gain)
    packed = jnp.concatenate([latent, head_weights, jnp.zeros((own, 64), jnp.bfloat16)], axis=1)
    turned = turn(packed)
    everyone = lax.all_to_all(jnp.broadcast_to(turned[None], (NZ,) + turned.shape), "z", 0, 0)
    place = jnp.stack([c, yh]).astype(jnp.int32)
    queries = make_queries(
        place, everyone.reshape(HALF, packed.shape[1]), index_weight, weight_mine, weight_theirs
    )
    queries = lax.all_to_all(queries, "z", 0, 0).reshape(IHEADS * own, IDIM)
    scores = make_scores(queries, turned[:, QL:], all_keys)
    latent, hidden, scores = lax.optimization_barrier((latent, hidden, scores))
    scores = lax.all_to_all(scores, SEQ, 0, 0)

    payload = jnp.concatenate(
        [hidden.reshape(NZ, own, DZ), latent.reshape(own, NZ, 2 * local).transpose(1, 0, 2)], axis=2
    )
    payload = lax.all_to_all(payload, "z", 0, 0)
    hidden_rows = payload[:, :, :DZ].transpose(1, 0, 2).reshape(own, D)
    latent_cols = payload[:, :, DZ:].reshape(NZ, own, 2, local)
    latent_mine = lax.dynamic_index_in_dim(latent_cols, yh, 2, keepdims=False)
    latent_got = swap(lax.dynamic_index_in_dim(latent_cols, 1 - yh, 2, keepdims=False), "yh")
    latent_out = jnp.stack(
        [jnp.where(yh == 0, latent_mine, latent_got), jnp.where(yh == 0, latent_got, latent_mine)], axis=1
    ).reshape(rows, local)

    own_positions = lax.dynamic_slice_in_dim(positions, head * rows, rows).reshape(rows, 1)
    numbers = jnp.stack([cache_len[0], seq * SLOTS]).astype(jnp.int32)
    return (hidden_rows, latent_out, finish(numbers, scores, own_positions))


def solution(mesh):
    fine = Mesh(mesh.devices.reshape(4, 2, 2, 8, 2), SEQ + HEAD)
    in_specs = (
        P(SEQ, HEAD),
        P(HEAD, None),
        P(SEQ + HEAD, None),
        P(),
        P(None, HEAD),
        P(None, HEAD),
        P(),
        P(None, HEAD),
        P(SEQ, None),
        P(),
        P(SEQ),
    )
    out_specs = (P(SEQ + HEAD, None), P(SEQ, HEAD), P(HEAD, SEQ))
    return jax.shard_map(shards, mesh=fine, in_specs=in_specs, out_specs=out_specs, check_vma=False)
```

```python
import functools

import jax
import jax.numpy as jnp
from jax import lax
from jax.experimental import pallas as pl
from jax.experimental.pallas import tpu as pltpu
from jax.sharding import Mesh
from jax.sharding import PartitionSpec as P

D = 7168
QL = 1536
IHEADS = 64
IDIM = 128
N_SEQ = 16
N_HEAD = 16
NZ = 8
DZ = D // NZ
EPSILON = 1e-06
SEQ = ("x", "yl", "c")
HEAD = ("z", "yh")
HALF = 128
SLOTS = 1024


def rms_round(values, gain):
    widened = values.astype(jnp.float32)
    inverse = lax.rsqrt(jnp.mean(widened * widened, axis=-1, keepdims=True) + EPSILON)
    return (widened * inverse * gain.astype(jnp.float32)).astype(jnp.bfloat16)


def swap(values, axis):
    return lax.ppermute(values, axis, [(0, 1), (1, 0)])


def shift(values, axis, size, by):
    return lax.ppermute(values, axis, [(i, (i + by) % size) for i in range(size)])


def kernel_params():
    return pltpu.CompilerParams(vmem_limit_bytes=48 * 1024 * 1024)


def big_params():
    return pltpu.CompilerParams(vmem_limit_bytes=60 * 1024 * 1024)


def project_kernel(head_ref, a_ref, b_ref, res_ref, o_ref, b_held, o_held, in_sems, out_sems):
    rows = a_ref.shape[0]

    def fetch(i):
        columns = pl.ds(pl.multiple_of(i * DZ, 128), DZ)
        return pltpu.make_async_copy(b_ref.at[:, columns], b_held.at[i], in_sems.at[i])

    def store(i):
        return pltpu.make_async_copy(o_held.at[i], o_ref.at[i], out_sems.at[i])

    for i in range(NZ):
        fetch(i).start()
    own = lax.broadcasted_iota(jnp.int32, (rows, 16), 1) + head_ref[0] * 16
    place = lax.broadcasted_iota(jnp.int32, (rows, 16), 0) == own
    place = jnp.where(place, 1.0, 0.0).astype(jnp.bfloat16)

    @pl.loop(0, NZ)
    def _(i):
        columns = pl.ds(pl.multiple_of(i * DZ, 128), DZ)
        fetch(i).wait()
        product = jnp.dot(a_ref[...], b_held[i], preferred_element_type=jnp.float32)
        product = product + jnp.dot(place, res_ref[:, columns], preferred_element_type=jnp.float32)
        product = product.astype(o_ref.dtype)
        for group in range(NZ):
            for half in range(2):
                o_held[i, half, group * 16 : (group + 1) * 16, :] = product[
                    group * 32 + half * 16 : group * 32 + (half + 1) * 16, :
                ]
        store(i).start()

    for i in range(NZ):
        store(i).wait()


def project(head, attn_out, out_weight, residual):
    rows, depth = attn_out.shape
    whole = pl.BlockSpec(memory_space=pltpu.VMEM)
    apart = pl.BlockSpec(memory_space=pl.ANY)
    shape = (NZ, 2, HALF, DZ)
    return pl.pallas_call(
        project_kernel,
        in_specs=[pl.BlockSpec(memory_space=pltpu.SMEM), whole, apart, whole],
        out_specs=apart,
        out_shape=jax.ShapeDtypeStruct(shape, jnp.bfloat16),
        scratch_shapes=[
            pltpu.VMEM((NZ, depth, DZ), jnp.bfloat16),
            pltpu.VMEM(shape, jnp.bfloat16),
            pltpu.SemaphoreType.DMA((NZ,)),
            pltpu.SemaphoreType.DMA((NZ,)),
        ],
        compiler_params=big_params(),
    )(head, attn_out, out_weight, residual)


def lift_kernel(core_ref, kept_ref, got_ref, gain_ref, mine_ref, other_ref, o_ref):
    hidden = (kept_ref[...].astype(jnp.float32) + got_ref[...].astype(jnp.float32)).astype(jnp.bfloat16)
    o_ref[:, QL + 128 :] = hidden
    wide = hidden.astype(jnp.float32)
    squares = jnp.sum(wide * wide, axis=1, keepdims=True)
    high = squares.astype(jnp.bfloat16).astype(jnp.float32)
    scaled = wide * gain_ref[...].astype(jnp.float32)
    first, second = scaled[:, : DZ // 2], scaled[:, DZ // 2 :]
    is_first = core_ref[0] == 0
    mine = jnp.where(is_first, first, second).astype(jnp.bfloat16)
    other = jnp.where(is_first, second, first).astype(jnp.bfloat16)
    lifted = jnp.dot(mine, mine_ref[...], preferred_element_type=jnp.float32) + jnp.dot(
        other, other_ref[...], preferred_element_type=jnp.float32
    )
    lane = lax.broadcasted_iota(jnp.int32, (HALF, 128), 1)
    tail = jnp.where(lane == IHEADS, high, jnp.where(lane == IHEADS + 1, squares - high, 0.0))
    o_ref[:, :QL] = lifted[:, :QL].astype(jnp.bfloat16)
    o_ref[:, QL : QL + 128] = jnp.where(lane < IHEADS, lifted[:, QL:], tail).astype(jnp.bfloat16)


def lift(core, kept, got, gain, mine, other):
    whole = pl.BlockSpec(memory_space=pltpu.VMEM)
    return pl.pallas_call(
        lift_kernel,
        in_specs=[pl.BlockSpec(memory_space=pltpu.SMEM)] + [whole] * 5,
        out_specs=whole,
        out_shape=jax.ShapeDtypeStruct((HALF, QL + 128 + DZ), jnp.bfloat16),
        compiler_params=kernel_params(),
    )(core, kept, got, gain, mine, other)


def query_kernel(place_ref, latent_ref, own_ref, mine_ref, theirs_ref, final_ref, o_ref):
    core, high = place_ref[0], place_ref[1]
    is_first = core == 0
    left, right = latent_ref[:, : QL // 2], latent_ref[:, QL // 2 : QL]
    here = jnp.where(is_first, left, right)
    there = jnp.where(is_first, right, left)
    own = jnp.dot(latent_ref[:, :QL], own_ref[...], preferred_element_type=jnp.float32)
    other = jnp.dot(here, mine_ref[...], preferred_element_type=jnp.float32) + jnp.dot(
        there, theirs_ref[...], preferred_element_type=jnp.float32
    )
    for at, part in ((high * 4, own), ((1 - high) * 4, other)):
        part = part.astype(jnp.bfloat16)
        for j in range(4):
            for block in range(NZ):
                o_ref[block, at + j] = part[block * 16 : (block + 1) * 16, j * IDIM : (j + 1) * IDIM]
    o_ref[:, 8:] = jnp.zeros((NZ, 2, 16, IDIM), jnp.bfloat16)
    for block in range(NZ):
        for half in range(2):
            at = (block * 2 + half) * 96
            o_ref[block, 8 + half, :, :96] = final_ref[:, at : at + 96]


def make_queries(place, latent, own, mine, theirs, final):
    whole = pl.BlockSpec(memory_space=pltpu.VMEM)
    return pl.pallas_call(
        query_kernel,
        in_specs=[pl.BlockSpec(memory_space=pltpu.SMEM)] + [whole] * 5,
        out_specs=whole,
        out_shape=jax.ShapeDtypeStruct((NZ, 10, 16, IDIM), jnp.bfloat16),
        compiler_params=kernel_params(),
    )(place, latent, own, mine, theirs, final)


def score_kernel(q_ref, w_ref, k_ref, o_ref, wide_ref, rows_ref):
    scale = IDIM ** (-0.5)
    tile = 256

    @pl.when(pl.program_id(0) == 0)
    def _():
        weights = w_ref[...].astype(jnp.float32) * scale
        for j in range(IHEADS):
            wide_ref[j * 16 : (j + 1) * 16, :] = jnp.broadcast_to(weights[:, j : j + 1], (16, 128))
            rows_ref[j * 16 : (j + 1) * 16, :] = q_ref[j // 8, j % 8]

    blocks, _, slots = o_ref.shape
    for block in range(blocks):
        for slot in range(0, slots, tile):
            at = block * slots + slot
            logits = lax.dot_general(
                rows_ref[...],
                k_ref[at : at + tile, :],
                (((1,), (1,)), ((), ())),
                preferred_element_type=jnp.float32,
            )
            halves = [jnp.zeros((16, 128), jnp.float32), jnp.zeros((16, 128), jnp.float32)]
            for j in range(IHEADS):
                weight = wide_ref[j * 16 : (j + 1) * 16, :]
                for n in range(2):
                    halves[n] += (
                        jnp.maximum(logits[j * 16 : (j + 1) * 16, n * 128 : (n + 1) * 128], 0.0) * weight
                    )
            for n in range(2):
                o_ref[block, :, slot + n * 128 : slot + (n + 1) * 128] = halves[n].astype(o_ref.dtype)


def make_scores(queries, head_weights, keys):
    per_step = 2
    return pl.pallas_call(
        score_kernel,
        grid=(N_SEQ // per_step,),
        in_specs=[
            pl.BlockSpec(queries.shape, lambda i: (0, 0, 0, 0)),
            pl.BlockSpec((16, 128), lambda i: (0, 0)),
            pl.BlockSpec((per_step * SLOTS, IDIM), lambda i: (i, 0)),
        ],
        out_specs=pl.BlockSpec((per_step, 16, SLOTS), lambda i: (i, 0, 0)),
        out_shape=jax.ShapeDtypeStruct((N_SEQ, 16, SLOTS), jnp.bfloat16),
        scratch_shapes=[
            pltpu.VMEM((IHEADS * 16, 128), jnp.float32),
            pltpu.VMEM((IHEADS * 16, IDIM), jnp.bfloat16),
        ],
        compiler_params=big_params(),
    )(queries, head_weights, keys)


def finish_kernel(numbers_ref, s_ref, pos_ref, o_ref):
    local = lax.broadcasted_iota(jnp.int32, (16, SLOTS), 1)
    filled, base = numbers_ref[0], numbers_ref[1]
    for group in range(N_SEQ):
        here = slice(group * 16, (group + 1) * 16)
        reach = jnp.minimum(filled, pos_ref[here, :] - base + 1)
        o_ref[here, :] = jnp.where(local < reach, s_ref[group].astype(jnp.float32), 0.0)


def finish(numbers, scores, own_positions):
    whole = pl.BlockSpec(memory_space=pltpu.VMEM)
    return pl.pallas_call(
        finish_kernel,
        in_specs=[pl.BlockSpec(memory_space=pltpu.SMEM), whole, whole],
        out_specs=whole,
        out_shape=jax.ShapeDtypeStruct((N_SEQ * 16, SLOTS), jnp.float32),
        compiler_params=kernel_params(),
    )(numbers, scores, own_positions)


def down_weight_rows(latent_weight, index_proj, piece, early):
    share = DZ // N_SEQ

    def own_rows(weight):
        return lax.dynamic_slice_in_dim(weight.reshape(NZ, DZ, weight.shape[1]), piece * share, share, 1)

    own = jnp.concatenate([own_rows(latent_weight), own_rows(index_proj)], axis=2)
    by_head = lax.all_to_all(jnp.repeat(own, 2, axis=0), HEAD, 0, 0).transpose(1, 0, 2)
    local = latent_weight.shape[1]
    wide = jnp.concatenate(
        [
            by_head[:, :, :local].reshape(share, QL),
            by_head[:, :, local:].reshape(share, IHEADS),
            jnp.zeros((share, 64), jnp.bfloat16),
        ],
        axis=1,
    )
    wide, early = lax.optimization_barrier((wide, early))
    half = lax.all_to_all(jnp.broadcast_to(wide[None], (8,) + wide.shape), ("x", "yl"), 0, 0)
    half = half.reshape(8 * share, wide.shape[1])
    return half, swap(half, "c"), early


def turn(values):
    moves = [(s * N_HEAD + h, h * N_HEAD + s) for s in range(N_SEQ) for h in range(N_HEAD)]
    return lax.ppermute(values, SEQ + HEAD, moves)


def shards(
    attn_out,
    out_weight,
    residual,
    norm_gain,
    latent_weight,
    index_proj,
    latent_gain,
    index_weight,
    index_keys,
    positions,
    cache_len,
):
    x, yl, c = (lax.axis_index(a) for a in SEQ)
    z, yh = (lax.axis_index(a) for a in HEAD)
    seq = (x * 2 + yl) * 2 + c
    head = z * 2 + yh
    rows = attn_out.shape[0]
    own = rows // N_HEAD
    local = latent_weight.shape[1]

    partial = project(jnp.stack([head]).astype(jnp.int32), attn_out, out_weight, residual)
    summed = lax.psum_scatter(partial, "z", scatter_dimension=0, tiled=False)

    depth = QL // 2
    weight_mine = swap(lax.dynamic_slice_in_dim(index_weight, c * depth, depth, 0), "yh")
    down_mine, down_other, weight_mine = down_weight_rows(
        latent_weight, index_proj, c * 8 + x * 2 + yl, weight_mine
    )
    weight_theirs = swap(weight_mine, "c")
    summed, down_mine, down_other, weight_mine, weight_theirs, index_keys = lax.optimization_barrier(
        (summed, down_mine, down_other, weight_mine, weight_theirs, index_keys)
    )
    all_keys = lax.all_gather(index_keys, SEQ, axis=0, tiled=True)
    kept = lax.dynamic_index_in_dim(summed, yh, 0, keepdims=False)
    got = swap(lax.dynamic_index_in_dim(summed, 1 - yh, 0, keepdims=False), "yh")
    gain = lax.dynamic_slice_in_dim(norm_gain, z * DZ, DZ).reshape(1, DZ)
    lifted = lift(jnp.stack([c]).astype(jnp.int32), kept, got, gain, down_mine, down_other)
    parts = lax.all_to_all(lifted.reshape(NZ, own, lifted.shape[1]), "z", 0, 0)
    hidden_rows = parts[:, :, QL + 128 :].transpose(1, 0, 2).reshape(own, D)
    total = jnp.sum(parts[:, :, : QL + 128].astype(jnp.float32), axis=0)
    mean = (total[:, 1600:1601] + total[:, 1601:1602]) / D
    inverse = lax.rsqrt(mean + EPSILON)
    latent_raw = (total[:, :QL] * inverse).astype(jnp.bfloat16)
    head_weights = (total[:, QL:1600] * inverse * IHEADS ** (-0.5)).astype(jnp.bfloat16)
    latent = rms_round(latent_raw, latent_gain)
    packed = jnp.concatenate([latent, head_weights, jnp.zeros((own, 64), jnp.bfloat16)], axis=1)
    turned = turn(packed)
    everyone = lax.all_to_all(jnp.broadcast_to(turned[None], (NZ,) + turned.shape), "z", 0, 0)
    place = jnp.stack([c, yh]).astype(jnp.int32)
    queries = make_queries(
        place, everyone.reshape(HALF, packed.shape[1]), index_weight, weight_mine, weight_theirs, latent
    )
    queries = lax.all_to_all(queries, "z", 0, 0)
    scores = make_scores(queries, turned[:, QL:], all_keys)
    scores = lax.all_to_all(scores, SEQ, 0, 0)

    latent_mine = lax.dynamic_index_in_dim(queries, 8 + yh, 1, keepdims=False)[:, :, :local]
    latent_give = lax.dynamic_index_in_dim(queries, 9 - yh, 1, keepdims=False)[:, :, :local]
    latent_got = swap(latent_give, "yh")
    latent_out = jnp.stack(
        [jnp.where(yh == 0, latent_mine, latent_got), jnp.where(yh == 0, latent_got, latent_mine)], axis=1
    ).reshape(rows, local)

    own_positions = lax.dynamic_slice_in_dim(positions, head * rows, rows).reshape(rows, 1)
    numbers = jnp.stack([cache_len[0], seq * SLOTS]).astype(jnp.int32)
    return (hidden_rows, latent_out, finish(numbers, scores, own_positions))


def solution(mesh):
    fine = Mesh(mesh.devices.reshape(4, 2, 2, 8, 2), SEQ + HEAD)
    in_specs = (
        P(SEQ, HEAD),
        P(HEAD, None),
        P(SEQ + HEAD, None),
        P(),
        P(None, HEAD),
        P(None, HEAD),
        P(),
        P(None, HEAD),
        P(SEQ, None),
        P(),
        P(SEQ),
    )
    out_specs = (P(SEQ + HEAD, None), P(SEQ, HEAD), P(HEAD, SEQ))
    return jax.shard_map(shards, mesh=fine, in_specs=in_specs, out_specs=out_specs, check_vma=False)
```

```python
import functools

import jax
import jax.numpy as jnp
from jax import lax
from jax.experimental import pallas as pl
from jax.experimental.pallas import tpu as pltpu
from jax.sharding import Mesh
from jax.sharding import PartitionSpec as P

D = 7168
QL = 1536
IHEADS = 64
IDIM = 128
N_SEQ = 16
N_HEAD = 16
NZ = 8
DZ = D // NZ
EPSILON = 1e-06
SEQ = ("x", "yl", "c")
HEAD = ("z", "yh")
HALF = 128
SLOTS = 1024


def rms_round(values, gain):
    widened = values.astype(jnp.float32)
    inverse = lax.rsqrt(jnp.mean(widened * widened, axis=-1, keepdims=True) + EPSILON)
    return (widened * inverse * gain.astype(jnp.float32)).astype(jnp.bfloat16)


def swap(values, axis):
    return lax.ppermute(values, axis, [(0, 1), (1, 0)])


def shift(values, axis, size, by):
    return lax.ppermute(values, axis, [(i, (i + by) % size) for i in range(size)])


def kernel_params():
    return pltpu.CompilerParams(vmem_limit_bytes=20 * 1024 * 1024)


def big_params():
    return pltpu.CompilerParams(vmem_limit_bytes=60 * 1024 * 1024)


def project_kernel(head_ref, a_ref, b_ref, res_ref, o_ref, b_held, o_held, in_sems, out_sems):
    rows = a_ref.shape[0]

    def fetch(i):
        columns = pl.ds(pl.multiple_of(i * DZ, 128), DZ)
        return pltpu.make_async_copy(b_ref.at[:, columns], b_held.at[i], in_sems.at[i])

    def store(i):
        return pltpu.make_async_copy(o_held.at[i], o_ref.at[i], out_sems.at[i])

    for i in range(NZ):
        fetch(i).start()
    own = lax.broadcasted_iota(jnp.int32, (rows, 16), 1) + head_ref[0] * 16
    place = lax.broadcasted_iota(jnp.int32, (rows, 16), 0) == own
    place = jnp.where(place, 1.0, 0.0).astype(jnp.bfloat16)

    @pl.loop(0, NZ)
    def _(i):
        columns = pl.ds(pl.multiple_of(i * DZ, 128), DZ)
        fetch(i).wait()
        product = jnp.dot(a_ref[...], b_held[i], preferred_element_type=jnp.float32)
        product = product + jnp.dot(place, res_ref[:, columns], preferred_element_type=jnp.float32)
        product = product.astype(o_ref.dtype)
        for group in range(NZ):
            for half in range(2):
                o_held[i, half, group * 16 : (group + 1) * 16, :] = product[
                    group * 32 + half * 16 : group * 32 + (half + 1) * 16, :
                ]
        store(i).start()

    for i in range(NZ):
        store(i).wait()


def project(head, attn_out, out_weight, residual):
    rows, depth = attn_out.shape
    whole = pl.BlockSpec(memory_space=pltpu.VMEM)
    apart = pl.BlockSpec(memory_space=pl.ANY)
    shape = (NZ, 2, HALF, DZ)
    return pl.pallas_call(
        project_kernel,
        in_specs=[pl.BlockSpec(memory_space=pltpu.SMEM), whole, apart, whole],
        out_specs=apart,
        out_shape=jax.ShapeDtypeStruct(shape, jnp.bfloat16),
        scratch_shapes=[
            pltpu.VMEM((NZ, depth, DZ), jnp.bfloat16),
            pltpu.VMEM(shape, jnp.bfloat16),
            pltpu.SemaphoreType.DMA((NZ,)),
            pltpu.SemaphoreType.DMA((NZ,)),
        ],
        compiler_params=big_params(),
    )(head, attn_out, out_weight, residual)


def lift_kernel(core_ref, kept_ref, got_ref, gain_ref, mine_ref, other_ref, o_ref):
    hidden = (kept_ref[...].astype(jnp.float32) + got_ref[...].astype(jnp.float32)).astype(jnp.bfloat16)
    o_ref[:, QL + 128 :] = hidden
    wide = hidden.astype(jnp.float32)
    squares = jnp.sum(wide * wide, axis=1, keepdims=True)
    high = squares.astype(jnp.bfloat16).astype(jnp.float32)
    scaled = wide * gain_ref[...].astype(jnp.float32)
    first, second = scaled[:, : DZ // 2], scaled[:, DZ // 2 :]
    is_first = core_ref[0] == 0
    mine = jnp.where(is_first, first, second).astype(jnp.bfloat16)
    other = jnp.where(is_first, second, first).astype(jnp.bfloat16)
    lifted = jnp.dot(mine, mine_ref[...], preferred_element_type=jnp.float32) + jnp.dot(
        other, other_ref[...], preferred_element_type=jnp.float32
    )
    lane = lax.broadcasted_iota(jnp.int32, (HALF, 128), 1)
    tail = jnp.where(lane == IHEADS, high, jnp.where(lane == IHEADS + 1, squares - high, 0.0))
    o_ref[:, :QL] = lifted[:, :QL].astype(jnp.bfloat16)
    o_ref[:, QL : QL + 128] = jnp.where(lane < IHEADS, lifted[:, QL:], tail).astype(jnp.bfloat16)


def lift(core, kept, got, gain, mine, other):
    whole = pl.BlockSpec(memory_space=pltpu.VMEM)
    return pl.pallas_call(
        lift_kernel,
        in_specs=[pl.BlockSpec(memory_space=pltpu.SMEM)] + [whole] * 5,
        out_specs=whole,
        out_shape=jax.ShapeDtypeStruct((HALF, QL + 128 + DZ), jnp.bfloat16),
        compiler_params=kernel_params(),
    )(core, kept, got, gain, mine, other)


def query_kernel(place_ref, own_ref, mine_ref, theirs_ref, final_ref, *refs):
    pieces, o_ref, latent_ref = refs[:NZ], refs[NZ], refs[NZ + 1]
    core, high, level = place_ref[0], place_ref[1], place_ref[2]
    for k in range(NZ):
        latent_ref[k * 16 : (k + 1) * 16, :] = pieces[k][:, :QL]
    is_first = core == 0
    left, right = latent_ref[:, : QL // 2], latent_ref[:, QL // 2 :]
    here = jnp.where(is_first, left, right)
    there = jnp.where(is_first, right, left)
    own = jnp.dot(latent_ref[...], own_ref[...], preferred_element_type=jnp.float32)
    other = jnp.dot(here, mine_ref[...], preferred_element_type=jnp.float32) + jnp.dot(
        there, theirs_ref[...], preferred_element_type=jnp.float32
    )
    for at, part in ((high * 4, own), ((1 - high) * 4, other)):
        part = part.astype(jnp.bfloat16)
        for j in range(4):
            for k in range(NZ):
                o_ref[level ^ k, at + j] = part[k * 16 : (k + 1) * 16, j * IDIM : (j + 1) * IDIM]
    o_ref[:, 8:] = jnp.zeros((NZ, 2, 16, IDIM), jnp.bfloat16)
    for block in range(NZ):
        for half in range(2):
            at = (block * 2 + half) * 96
            o_ref[block, 8 + half, :, :96] = final_ref[:, at : at + 96]


def make_queries(place, pieces, own, mine, theirs, final):
    whole = pl.BlockSpec(memory_space=pltpu.VMEM)
    return pl.pallas_call(
        query_kernel,
        in_specs=[pl.BlockSpec(memory_space=pltpu.SMEM)] + [whole] * (4 + NZ),
        out_specs=whole,
        out_shape=jax.ShapeDtypeStruct((NZ, 10, 16, IDIM), jnp.bfloat16),
        scratch_shapes=[pltpu.VMEM((HALF, QL), jnp.bfloat16)],
        compiler_params=kernel_params(),
    )(place, own, mine, theirs, final, *pieces)


def score_kernel(q_ref, w_ref, k_ref, o_ref, wide_ref, rows_ref):
    scale = IDIM ** (-0.5)
    tile = 256

    @pl.when(pl.program_id(0) == 0)
    def _():
        weights = w_ref[...].astype(jnp.float32) * scale
        for j in range(IHEADS):
            wide_ref[j * 16 : (j + 1) * 16, :] = jnp.broadcast_to(weights[:, j : j + 1], (16, 128))
            rows_ref[j * 16 : (j + 1) * 16, :] = q_ref[j // 8, j % 8]

    blocks, _, slots = o_ref.shape
    for block in range(blocks):
        for slot in range(0, slots, tile):
            at = block * slots + slot
            logits = lax.dot_general(
                rows_ref[...],
                k_ref[at : at + tile, :],
                (((1,), (1,)), ((), ())),
                preferred_element_type=jnp.float32,
            )
            halves = [jnp.zeros((16, 128), jnp.float32), jnp.zeros((16, 128), jnp.float32)]
            for j in range(IHEADS):
                weight = wide_ref[j * 16 : (j + 1) * 16, :]
                for n in range(2):
                    halves[n] += (
                        jnp.maximum(logits[j * 16 : (j + 1) * 16, n * 128 : (n + 1) * 128], 0.0) * weight
                    )
            for n in range(2):
                o_ref[block, :, slot + n * 128 : slot + (n + 1) * 128] = halves[n].astype(o_ref.dtype)


def make_scores(queries, head_weights, keys):
    per_step = 2
    return pl.pallas_call(
        score_kernel,
        grid=(N_SEQ // per_step,),
        in_specs=[
            pl.BlockSpec(queries.shape, lambda i: (0, 0, 0, 0)),
            pl.BlockSpec((16, 128), lambda i: (0, 0)),
            pl.BlockSpec((per_step * SLOTS, IDIM), lambda i: (i, 0)),
        ],
        out_specs=pl.BlockSpec((per_step, 16, SLOTS), lambda i: (i, 0, 0)),
        out_shape=jax.ShapeDtypeStruct((N_SEQ, 16, SLOTS), jnp.bfloat16),
        scratch_shapes=[
            pltpu.VMEM((IHEADS * 16, 128), jnp.float32),
            pltpu.VMEM((IHEADS * 16, IDIM), jnp.bfloat16),
        ],
        compiler_params=big_params(),
    )(queries, head_weights, keys)


def finish_kernel(numbers_ref, s_ref, pos_ref, o_ref):
    local = lax.broadcasted_iota(jnp.int32, (16, SLOTS), 1)
    filled, base = numbers_ref[0], numbers_ref[1]
    for group in range(N_SEQ):
        here = slice(group * 16, (group + 1) * 16)
        reach = jnp.minimum(filled, pos_ref[here, :] - base + 1)
        o_ref[here, :] = jnp.where(local < reach, s_ref[group].astype(jnp.float32), 0.0)


def finish(numbers, scores, own_positions):
    whole = pl.BlockSpec(memory_space=pltpu.VMEM)
    return pl.pallas_call(
        finish_kernel,
        in_specs=[pl.BlockSpec(memory_space=pltpu.SMEM), whole, whole],
        out_specs=whole,
        out_shape=jax.ShapeDtypeStruct((N_SEQ * 16, SLOTS), jnp.float32),
        compiler_params=kernel_params(),
    )(numbers, scores, own_positions)


def down_weight_rows(latent_weight, index_proj, piece, early):
    share = DZ // N_SEQ

    def own_rows(weight):
        return lax.dynamic_slice_in_dim(weight.reshape(NZ, DZ, weight.shape[1]), piece * share, share, 1)

    own = jnp.concatenate([own_rows(latent_weight), own_rows(index_proj)], axis=2)
    by_head = lax.all_to_all(jnp.repeat(own, 2, axis=0), HEAD, 0, 0).transpose(1, 0, 2)
    local = latent_weight.shape[1]
    wide = jnp.concatenate(
        [
            by_head[:, :, :local].reshape(share, QL),
            by_head[:, :, local:].reshape(share, IHEADS),
            jnp.zeros((share, 64), jnp.bfloat16),
        ],
        axis=1,
    )
    wide, early = lax.optimization_barrier((wide, early))
    half = lax.all_to_all(jnp.broadcast_to(wide[None], (8,) + wide.shape), ("x", "yl"), 0, 0)
    half = half.reshape(8 * share, wide.shape[1])
    return half, swap(half, "c"), early


def turn(values, flip):
    moves = []
    for s in range(N_SEQ):
        for h in range(N_HEAD):
            moves.append((s * N_HEAD + h, h * N_HEAD + (s ^ (flip * 2))))
    return lax.ppermute(values, SEQ + HEAD, moves)


def shards(
    attn_out,
    out_weight,
    residual,
    norm_gain,
    latent_weight,
    index_proj,
    latent_gain,
    index_weight,
    index_keys,
    positions,
    cache_len,
):
    x, yl, c = (lax.axis_index(a) for a in SEQ)
    z, yh = (lax.axis_index(a) for a in HEAD)
    seq = (x * 2 + yl) * 2 + c
    head = z * 2 + yh
    rows = attn_out.shape[0]
    own = rows // N_HEAD
    local = latent_weight.shape[1]

    partial = project(jnp.stack([head]).astype(jnp.int32), attn_out, out_weight, residual)
    summed = lax.psum_scatter(partial, "z", scatter_dimension=0, tiled=False)

    depth = QL // 2
    weight_mine = swap(lax.dynamic_slice_in_dim(index_weight, c * depth, depth, 0), "yh")
    down_mine, down_other, weight_mine = down_weight_rows(
        latent_weight, index_proj, c * 8 + x * 2 + yl, weight_mine
    )
    weight_theirs = swap(weight_mine, "c")
    summed, down_mine, down_other, index_keys = lax.optimization_barrier(
        (summed, down_mine, down_other, index_keys)
    )
    all_keys = lax.all_gather(index_keys, SEQ, axis=0, tiled=True)
    kept = lax.dynamic_index_in_dim(summed, yh, 0, keepdims=False)
    got = swap(lax.dynamic_index_in_dim(summed, 1 - yh, 0, keepdims=False), "yh")
    gain = lax.dynamic_slice_in_dim(norm_gain, z * DZ, DZ).reshape(1, DZ)
    lifted = lift(jnp.stack([c]).astype(jnp.int32), kept, got, gain, down_mine, down_other)
    parts = lax.all_to_all(lifted.reshape(NZ, own, lifted.shape[1]), "z", 0, 0)
    hidden_rows = parts[:, :, QL + 128 :].transpose(1, 0, 2).reshape(own, D)
    total = jnp.sum(parts[:, :, : QL + 128].astype(jnp.float32), axis=0)
    mean = (total[:, 1600:1601] + total[:, 1601:1602]) / D
    inverse = lax.rsqrt(mean + EPSILON)
    latent_raw = (total[:, :QL] * inverse).astype(jnp.bfloat16)
    head_weights = (total[:, QL:1600] * inverse * IHEADS ** (-0.5)).astype(jnp.bfloat16)
    latent = rms_round(latent_raw, latent_gain)
    packed = jnp.concatenate([latent, head_weights, jnp.zeros((own, 64), jnp.bfloat16)], axis=1)
    pieces = [turn(packed, k) for k in range(NZ)]
    place = jnp.stack([c, yh, z]).astype(jnp.int32)
    queries = make_queries(place, pieces, index_weight, weight_mine, weight_theirs, latent)
    queries = lax.all_to_all(queries, "z", 0, 0)
    scores = make_scores(queries, pieces[0][:, QL:], all_keys)
    scores, queries = lax.optimization_barrier((scores, queries))
    scores = lax.all_to_all(scores, SEQ, 0, 0)

    latent_mine = lax.dynamic_index_in_dim(queries, 8 + yh, 1, keepdims=False)[:, :, :local]
    latent_give = lax.dynamic_index_in_dim(queries, 9 - yh, 1, keepdims=False)[:, :, :local]
    latent_got = swap(latent_give, "yh")
    latent_out = jnp.stack(
        [jnp.where(yh == 0, latent_mine, latent_got), jnp.where(yh == 0, latent_got, latent_mine)], axis=1
    ).reshape(rows, local)

    own_positions = lax.dynamic_slice_in_dim(positions, head * rows, rows).reshape(rows, 1)
    numbers = jnp.stack([cache_len[0], seq * SLOTS]).astype(jnp.int32)
    return (hidden_rows, latent_out, finish(numbers, scores, own_positions))


def solution(mesh):
    fine = Mesh(mesh.devices.reshape(4, 2, 2, 8, 2), SEQ + HEAD)
    in_specs = (
        P(SEQ, HEAD),
        P(HEAD, None),
        P(SEQ + HEAD, None),
        P(),
        P(None, HEAD),
        P(None, HEAD),
        P(),
        P(None, HEAD),
        P(SEQ, None),
        P(),
        P(SEQ),
    )
    out_specs = (P(SEQ + HEAD, None), P(SEQ, HEAD), P(HEAD, SEQ))
    return jax.shard_map(shards, mesh=fine, in_specs=in_specs, out_specs=out_specs, check_vma=False)
```

```python
import functools

import jax
import jax.numpy as jnp
from jax import lax
from jax.experimental import pallas as pl
from jax.experimental.pallas import tpu as pltpu
from jax.sharding import Mesh
from jax.sharding import PartitionSpec as P

D = 7168
QL = 1536
IHEADS = 64
IDIM = 128
N_SEQ = 16
N_HEAD = 16
NZ = 8
DZ = D // NZ
EPSILON = 1e-06
SEQ = ("x", "yl", "c")
HEAD = ("z", "yh")
HALF = 128
SLOTS = 1024


def rms_round(values, gain):
    widened = values.astype(jnp.float32)
    inverse = lax.rsqrt(jnp.mean(widened * widened, axis=-1, keepdims=True) + EPSILON)
    return (widened * inverse * gain.astype(jnp.float32)).astype(jnp.bfloat16)


def swap(values, axis):
    return lax.ppermute(values, axis, [(0, 1), (1, 0)])


def shift(values, axis, size, by):
    return lax.ppermute(values, axis, [(i, (i + by) % size) for i in range(size)])


def kernel_params():
    return pltpu.CompilerParams(vmem_limit_bytes=20 * 1024 * 1024)


def big_params():
    return pltpu.CompilerParams(vmem_limit_bytes=60 * 1024 * 1024)


def project_kernel(head_ref, a_ref, b_ref, res_ref, o_ref, b_held, o_held, in_sems, out_sems):
    rows = a_ref.shape[0]

    def fetch(i):
        columns = pl.ds(pl.multiple_of(i * DZ, 128), DZ)
        return pltpu.make_async_copy(b_ref.at[:, columns], b_held.at[i], in_sems.at[i])

    def store(i):
        return pltpu.make_async_copy(o_held.at[i], o_ref.at[i], out_sems.at[i])

    for i in range(NZ):
        fetch(i).start()
    own = lax.broadcasted_iota(jnp.int32, (rows, 16), 1) + head_ref[0] * 16
    place = lax.broadcasted_iota(jnp.int32, (rows, 16), 0) == own
    place = jnp.where(place, 1.0, 0.0).astype(jnp.bfloat16)

    @pl.loop(0, NZ)
    def _(i):
        columns = pl.ds(pl.multiple_of(i * DZ, 128), DZ)
        fetch(i).wait()
        product = jnp.dot(a_ref[...], b_held[i], preferred_element_type=jnp.float32)
        product = product + jnp.dot(place, res_ref[:, columns], preferred_element_type=jnp.float32)
        product = product.astype(o_ref.dtype)
        for group in range(NZ):
            for half in range(2):
                o_held[i, half ^ head_ref[1], group * 16 : (group + 1) * 16, :] = product[
                    group * 32 + half * 16 : group * 32 + (half + 1) * 16, :
                ]
        store(i).start()

    for i in range(NZ):
        store(i).wait()


def project(head, attn_out, out_weight, residual):
    rows, depth = attn_out.shape
    whole = pl.BlockSpec(memory_space=pltpu.VMEM)
    apart = pl.BlockSpec(memory_space=pl.ANY)
    shape = (NZ, 2, HALF, DZ)
    return pl.pallas_call(
        project_kernel,
        in_specs=[pl.BlockSpec(memory_space=pltpu.SMEM), whole, apart, whole],
        out_specs=apart,
        out_shape=jax.ShapeDtypeStruct(shape, jnp.bfloat16),
        scratch_shapes=[
            pltpu.VMEM((NZ, depth, DZ), jnp.bfloat16),
            pltpu.VMEM(shape, jnp.bfloat16),
            pltpu.SemaphoreType.DMA((NZ,)),
            pltpu.SemaphoreType.DMA((NZ,)),
        ],
        compiler_params=big_params(),
    )(head, attn_out, out_weight, residual)


def lift_kernel(core_ref, kept_ref, got_ref, gain_ref, mine_ref, other_ref, o_ref):
    hidden = (kept_ref[...].astype(jnp.float32) + got_ref[...].astype(jnp.float32)).astype(jnp.bfloat16)
    o_ref[:, QL + 128 :] = hidden
    wide = hidden.astype(jnp.float32)
    squares = jnp.sum(wide * wide, axis=1, keepdims=True)
    high = squares.astype(jnp.bfloat16).astype(jnp.float32)
    scaled = wide * gain_ref[...].astype(jnp.float32)
    first, second = scaled[:, : DZ // 2], scaled[:, DZ // 2 :]
    is_first = core_ref[0] == 0
    mine = jnp.where(is_first, first, second).astype(jnp.bfloat16)
    other = jnp.where(is_first, second, first).astype(jnp.bfloat16)
    lifted = jnp.dot(mine, mine_ref[...], preferred_element_type=jnp.float32) + jnp.dot(
        other, other_ref[...], preferred_element_type=jnp.float32
    )
    lane = lax.broadcasted_iota(jnp.int32, (HALF, 128), 1)
    tail = jnp.where(lane == IHEADS, high, jnp.where(lane == IHEADS + 1, squares - high, 0.0))
    o_ref[:, :QL] = lifted[:, :QL].astype(jnp.bfloat16)
    o_ref[:, QL : QL + 128] = jnp.where(lane < IHEADS, lifted[:, QL:], tail).astype(jnp.bfloat16)


def lift(core, kept, got, gain, mine, other):
    whole = pl.BlockSpec(memory_space=pltpu.VMEM)
    return pl.pallas_call(
        lift_kernel,
        in_specs=[pl.BlockSpec(memory_space=pltpu.SMEM)] + [whole] * 5,
        out_specs=whole,
        out_shape=jax.ShapeDtypeStruct((HALF, QL + 128 + DZ), jnp.bfloat16),
        compiler_params=kernel_params(),
    )(core, kept, got, gain, mine, other)


def query_kernel(place_ref, latent_ref, own_ref, mine_ref, theirs_ref, final_ref, beside_ref, o_ref):
    core, high = place_ref[0], place_ref[1]
    is_first = core == 0
    left, right = latent_ref[:, : QL // 2], latent_ref[:, QL // 2 : QL]
    here = jnp.where(is_first, left, right)
    there = jnp.where(is_first, right, left)
    own = jnp.dot(latent_ref[:, :QL], own_ref[...], preferred_element_type=jnp.float32)
    other = jnp.dot(here, mine_ref[...], preferred_element_type=jnp.float32) + jnp.dot(
        there, theirs_ref[...], preferred_element_type=jnp.float32
    )
    for at, part in ((high * 4, own), ((1 - high) * 4, other)):
        part = part.astype(jnp.bfloat16)
        for j in range(4):
            for block in range(NZ):
                o_ref[block, at + j] = part[block * 16 : (block + 1) * 16, j * IDIM : (j + 1) * IDIM]
    o_ref[:, 8:] = jnp.zeros((NZ, 2, 16, IDIM), jnp.bfloat16)
    for block in range(NZ):
        low = final_ref[:, block * 192 : block * 192 + 96]
        top = final_ref[:, block * 192 + 96 : block * 192 + 192]
        o_ref[block, 8 + high, :, :96] = jnp.where(high == 0, low, top)
        o_ref[block, 9 - high, :, :96] = beside_ref[:, block * 96 : (block + 1) * 96]


def make_queries(place, latent, own, mine, theirs, final, beside):
    whole = pl.BlockSpec(memory_space=pltpu.VMEM)
    return pl.pallas_call(
        query_kernel,
        in_specs=[pl.BlockSpec(memory_space=pltpu.SMEM)] + [whole] * 6,
        out_specs=whole,
        out_shape=jax.ShapeDtypeStruct((NZ, 10, 16, IDIM), jnp.bfloat16),
        compiler_params=kernel_params(),
    )(place, latent, own, mine, theirs, final, beside)


def score_kernel(q_ref, w_ref, k_ref, o_ref, wide_ref, rows_ref):
    scale = IDIM ** (-0.5)
    tile = 256

    @pl.when(pl.program_id(0) == 0)
    def _():
        weights = w_ref[...].astype(jnp.float32) * scale
        for j in range(IHEADS):
            wide_ref[j * 16 : (j + 1) * 16, :] = jnp.broadcast_to(weights[:, j : j + 1], (16, 128))
            rows_ref[j * 16 : (j + 1) * 16, :] = q_ref[j // 8, j % 8]

    blocks, _, slots = o_ref.shape
    for block in range(blocks):
        for slot in range(0, slots, tile):
            at = block * slots + slot
            logits = lax.dot_general(
                rows_ref[...],
                k_ref[at : at + tile, :],
                (((1,), (1,)), ((), ())),
                preferred_element_type=jnp.float32,
            )
            halves = [jnp.zeros((16, 128), jnp.float32), jnp.zeros((16, 128), jnp.float32)]
            for j in range(IHEADS):
                weight = wide_ref[j * 16 : (j + 1) * 16, :]
                for n in range(2):
                    halves[n] += (
                        jnp.maximum(logits[j * 16 : (j + 1) * 16, n * 128 : (n + 1) * 128], 0.0) * weight
                    )
            for n in range(2):
                o_ref[block, :, slot + n * 128 : slot + (n + 1) * 128] = halves[n].astype(o_ref.dtype)


def make_scores(queries, head_weights, keys):
    per_step = 2
    return pl.pallas_call(
        score_kernel,
        grid=(N_SEQ // per_step,),
        in_specs=[
            pl.BlockSpec(queries.shape, lambda i: (0, 0, 0, 0)),
            pl.BlockSpec((16, 128), lambda i: (0, 0)),
            pl.BlockSpec((per_step * SLOTS, IDIM), lambda i: (i, 0)),
        ],
        out_specs=pl.BlockSpec((per_step, 16, SLOTS), lambda i: (i, 0, 0)),
        out_shape=jax.ShapeDtypeStruct((N_SEQ, 16, SLOTS), jnp.bfloat16),
        scratch_shapes=[
            pltpu.VMEM((IHEADS * 16, 128), jnp.float32),
            pltpu.VMEM((IHEADS * 16, IDIM), jnp.bfloat16),
        ],
        compiler_params=big_params(),
    )(queries, head_weights, keys)


def finish_kernel(numbers_ref, s_ref, pos_ref, o_ref):
    local = lax.broadcasted_iota(jnp.int32, (16, SLOTS), 1)
    filled, base = numbers_ref[0], numbers_ref[1]
    for group in range(N_SEQ):
        here = slice(group * 16, (group + 1) * 16)
        reach = jnp.minimum(filled, pos_ref[here, :] - base + 1)
        o_ref[here, :] = jnp.where(local < reach, s_ref[group].astype(jnp.float32), 0.0)


def finish(numbers, scores, own_positions):
    whole = pl.BlockSpec(memory_space=pltpu.VMEM)
    return pl.pallas_call(
        finish_kernel,
        in_specs=[pl.BlockSpec(memory_space=pltpu.SMEM), whole, whole],
        out_specs=whole,
        out_shape=jax.ShapeDtypeStruct((N_SEQ * 16, SLOTS), jnp.float32),
        compiler_params=kernel_params(),
    )(numbers, scores, own_positions)


def down_weight_rows(latent_weight, index_proj, piece):
    share = DZ // N_SEQ

    def own_rows(weight):
        return lax.dynamic_slice_in_dim(weight.reshape(NZ, DZ, weight.shape[1]), piece * share, share, 1)

    own = jnp.concatenate([own_rows(latent_weight), own_rows(index_proj)], axis=2)
    by_head = lax.all_to_all(jnp.repeat(own, 2, axis=0), HEAD, 0, 0).transpose(1, 0, 2)
    local = latent_weight.shape[1]
    wide = jnp.concatenate(
        [
            by_head[:, :, :local].reshape(share, QL),
            by_head[:, :, local:].reshape(share, IHEADS),
            jnp.zeros((share, 64), jnp.bfloat16),
        ],
        axis=1,
    )
    half = lax.all_to_all(jnp.broadcast_to(wide[None], (8,) + wide.shape), ("x", "yl"), 0, 0)
    half = half.reshape(8 * share, wide.shape[1])
    return half, swap(half, "c")


def turn(values):
    moves = [(s * N_HEAD + h, h * N_HEAD + s) for s in range(N_SEQ) for h in range(N_HEAD)]
    return lax.ppermute(values, SEQ + HEAD, moves)


def shards(
    attn_out,
    out_weight,
    residual,
    norm_gain,
    latent_weight,
    index_proj,
    latent_gain,
    index_weight,
    index_keys,
    positions,
    cache_len,
):
    x, yl, c = (lax.axis_index(a) for a in SEQ)
    z, yh = (lax.axis_index(a) for a in HEAD)
    seq = (x * 2 + yl) * 2 + c
    head = z * 2 + yh
    rows = attn_out.shape[0]
    own = rows // N_HEAD
    local = latent_weight.shape[1]

    partial = project(jnp.stack([head, yh]).astype(jnp.int32), attn_out, out_weight, residual)
    summed = lax.psum_scatter(partial, "z", scatter_dimension=0, tiled=False)

    depth = QL // 2
    weight_mine = swap(lax.dynamic_slice_in_dim(index_weight, c * depth, depth, 0), "yh")
    weight_theirs = swap(weight_mine, "c")
    down_mine, down_other = down_weight_rows(latent_weight, index_proj, c * 8 + x * 2 + yl)
    summed, index_keys = lax.optimization_barrier((summed, index_keys))
    all_keys = lax.all_gather(index_keys, SEQ, axis=0, tiled=True)
    kept, got = summed[0], swap(summed[1], "yh")
    gain = lax.dynamic_slice_in_dim(norm_gain, z * DZ, DZ).reshape(1, DZ)
    lifted = lift(jnp.stack([c]).astype(jnp.int32), kept, got, gain, down_mine, down_other)
    parts = lax.all_to_all(lifted.reshape(NZ, own, lifted.shape[1]), "z", 0, 0)
    hidden_rows = parts[:, :, QL + 128 :].transpose(1, 0, 2).reshape(own, D)
    total = jnp.sum(parts[:, :, : QL + 128].astype(jnp.float32), axis=0)
    mean = (total[:, 1600:1601] + total[:, 1601:1602]) / D
    inverse = lax.rsqrt(mean + EPSILON)
    latent_raw = (total[:, :QL] * inverse).astype(jnp.bfloat16)
    head_weights = (total[:, QL:1600] * inverse * IHEADS ** (-0.5)).astype(jnp.bfloat16)
    latent = rms_round(latent_raw, latent_gain)
    packed = jnp.concatenate([latent, head_weights, jnp.zeros((own, 64), jnp.bfloat16)], axis=1)
    turned = turn(packed)
    give = lax.dynamic_index_in_dim(latent.reshape(own, NZ, 2, local), 1 - yh, 2, keepdims=False)
    beside = swap(give.reshape(own, NZ * local), "yh")
    everyone = lax.all_to_all(jnp.broadcast_to(turned[None], (NZ,) + turned.shape), "z", 0, 0)
    everyone = everyone.reshape(HALF, packed.shape[1])
    place = jnp.stack([c, yh]).astype(jnp.int32)
    queries = make_queries(place, everyone, index_weight, weight_mine, weight_theirs, latent, beside)
    queries = lax.all_to_all(queries, "z", 0, 0)
    latent_out = queries[:, 8:, :, :local].reshape(rows, local)
    scores = make_scores(queries, turned[:, QL:], all_keys)
    scores = lax.all_to_all(scores, SEQ, 0, 0)

    own_positions = lax.dynamic_slice_in_dim(positions, head * rows, rows).reshape(rows, 1)
    numbers = jnp.stack([cache_len[0], seq * SLOTS]).astype(jnp.int32)
    return (hidden_rows, latent_out, finish(numbers, scores, own_positions))


def solution(mesh):
    fine = Mesh(mesh.devices.reshape(4, 2, 2, 8, 2), SEQ + HEAD)
    in_specs = (
        P(SEQ, HEAD),
        P(HEAD, None),
        P(SEQ + HEAD, None),
        P(),
        P(None, HEAD),
        P(None, HEAD),
        P(),
        P(None, HEAD),
        P(SEQ, None),
        P(),
        P(SEQ),
    )
    out_specs = (P(SEQ + HEAD, None), P(SEQ, HEAD), P(HEAD, SEQ))
    return jax.shard_map(shards, mesh=fine, in_specs=in_specs, out_specs=out_specs, check_vma=False)
```

```python
import functools

import jax
import jax.numpy as jnp
from jax import lax
from jax.experimental import pallas as pl
from jax.experimental.pallas import tpu as pltpu
from jax.sharding import Mesh
from jax.sharding import PartitionSpec as P

D = 7168
QL = 1536
IHEADS = 64
IDIM = 128
N_SEQ = 16
N_HEAD = 16
NZ = 8
DZ = D // NZ
EPSILON = 1e-06
SEQ = ("x", "yl", "c")
HEAD = ("z", "yh")
HALF = 128
SLOTS = 1024


def rms_round(values, gain):
    widened = values.astype(jnp.float32)
    inverse = lax.rsqrt(jnp.mean(widened * widened, axis=-1, keepdims=True) + EPSILON)
    return (widened * inverse * gain.astype(jnp.float32)).astype(jnp.bfloat16)


def swap(values, axis):
    return lax.ppermute(values, axis, [(0, 1), (1, 0)])


def shift(values, axis, size, by):
    return lax.ppermute(values, axis, [(i, (i + by) % size) for i in range(size)])


def kernel_params():
    return pltpu.CompilerParams(vmem_limit_bytes=20 * 1024 * 1024)


def big_params():
    return pltpu.CompilerParams(vmem_limit_bytes=60 * 1024 * 1024)


def project_kernel(head_ref, a_ref, b_ref, res_ref, o_ref, b_held, o_held, in_sems, out_sems):
    rows = a_ref.shape[0]

    def fetch(i):
        columns = pl.ds(pl.multiple_of(i * DZ, 128), DZ)
        return pltpu.make_async_copy(b_ref.at[:, columns], b_held.at[i], in_sems.at[i])

    def store(i):
        return pltpu.make_async_copy(o_held.at[i], o_ref.at[i], out_sems.at[i])

    for i in range(NZ):
        fetch(i).start()
    own = lax.broadcasted_iota(jnp.int32, (rows, 16), 1) + head_ref[0] * 16
    place = lax.broadcasted_iota(jnp.int32, (rows, 16), 0) == own
    place = jnp.where(place, 1.0, 0.0).astype(jnp.bfloat16)

    @pl.loop(0, NZ)
    def _(i):
        columns = pl.ds(pl.multiple_of(i * DZ, 128), DZ)
        fetch(i).wait()
        product = jnp.dot(a_ref[...], b_held[i], preferred_element_type=jnp.float32)
        product = product + jnp.dot(place, res_ref[:, columns], preferred_element_type=jnp.float32)
        product = product.astype(o_ref.dtype)
        for group in range(NZ):
            for half in range(2):
                o_held[i, half ^ (head_ref[0] % 2), group * 16 : (group + 1) * 16, :] = product[
                    group * 32 + half * 16 : group * 32 + (half + 1) * 16, :
                ]
        store(i).start()

    for i in range(NZ):
        store(i).wait()


def project(head, attn_out, out_weight, residual):
    rows, depth = attn_out.shape
    whole = pl.BlockSpec(memory_space=pltpu.VMEM)
    apart = pl.BlockSpec(memory_space=pl.ANY)
    shape = (NZ, 2, HALF, DZ)
    return pl.pallas_call(
        project_kernel,
        in_specs=[pl.BlockSpec(memory_space=pltpu.SMEM), whole, apart, whole],
        out_specs=apart,
        out_shape=jax.ShapeDtypeStruct(shape, jnp.bfloat16),
        scratch_shapes=[
            pltpu.VMEM((NZ, depth, DZ), jnp.bfloat16),
            pltpu.VMEM(shape, jnp.bfloat16),
            pltpu.SemaphoreType.DMA((NZ,)),
            pltpu.SemaphoreType.DMA((NZ,)),
        ],
        compiler_params=big_params(),
    )(head, attn_out, out_weight, residual)


def lift_kernel(core_ref, kept_ref, got_ref, gain_ref, mine_ref, other_ref, hidden_ref, o_ref):
    hidden = (kept_ref[...].astype(jnp.float32) + got_ref[...].astype(jnp.float32)).astype(jnp.bfloat16)
    hidden_ref[...] = hidden
    wide = hidden.astype(jnp.float32)
    squares = jnp.sum(wide * wide, axis=1, keepdims=True)
    high = squares.astype(jnp.bfloat16).astype(jnp.float32)
    scaled = wide * gain_ref[...].astype(jnp.float32)
    first, second = scaled[:, : DZ // 2], scaled[:, DZ // 2 :]
    is_first = core_ref[0] == 0
    mine = jnp.where(is_first, first, second).astype(jnp.bfloat16)
    other = jnp.where(is_first, second, first).astype(jnp.bfloat16)
    lifted = jnp.dot(mine, mine_ref[...], preferred_element_type=jnp.float32) + jnp.dot(
        other, other_ref[...], preferred_element_type=jnp.float32
    )
    lane = lax.broadcasted_iota(jnp.int32, (HALF, 128), 1)
    tail = jnp.where(lane == IHEADS, high, jnp.where(lane == IHEADS + 1, squares - high, 0.0))
    o_ref[:, :QL] = lifted[:, :QL].astype(jnp.bfloat16)
    o_ref[:, QL:] = jnp.where(lane < IHEADS, lifted[:, QL:], tail).astype(jnp.bfloat16)


def lift(core, kept, got, gain, mine, other):
    whole = pl.BlockSpec(memory_space=pltpu.VMEM)
    return pl.pallas_call(
        lift_kernel,
        in_specs=[pl.BlockSpec(memory_space=pltpu.SMEM)] + [whole] * 5,
        out_specs=[whole, whole],
        out_shape=[
            jax.ShapeDtypeStruct((HALF, DZ), jnp.bfloat16),
            jax.ShapeDtypeStruct((HALF, QL + 128), jnp.bfloat16),
        ],
        compiler_params=kernel_params(),
    )(core, kept, got, gain, mine, other)


def query_kernel(place_ref, latent_ref, own_ref, mine_ref, theirs_ref, final_ref, beside_ref, o_ref):
    core, high = place_ref[0], place_ref[1]
    is_first = core == 0
    left, right = latent_ref[:, : QL // 2], latent_ref[:, QL // 2 : QL]
    here = jnp.where(is_first, left, right)
    there = jnp.where(is_first, right, left)
    own = jnp.dot(latent_ref[:, :QL], own_ref[...], preferred_element_type=jnp.float32)
    other = jnp.dot(here, mine_ref[...], preferred_element_type=jnp.float32) + jnp.dot(
        there, theirs_ref[...], preferred_element_type=jnp.float32
    )
    for at, part in ((high * 4, own), ((1 - high) * 4, other)):
        part = part.astype(jnp.bfloat16)
        for j in range(4):
            for block in range(NZ):
                o_ref[block, at + j] = part[block * 16 : (block + 1) * 16, j * IDIM : (j + 1) * IDIM]
    o_ref[:, 8:] = jnp.zeros((NZ, 2, 16, IDIM), jnp.bfloat16)
    for block in range(NZ):
        low = final_ref[:, block * 192 : block * 192 + 96]
        top = final_ref[:, block * 192 + 96 : block * 192 + 192]
        o_ref[block, 8 + high, :, :96] = jnp.where(high == 0, low, top)
        o_ref[block, 9 - high, :, :96] = beside_ref[:, block * 96 : (block + 1) * 96]


def make_queries(place, latent, own, mine, theirs, final, beside):
    whole = pl.BlockSpec(memory_space=pltpu.VMEM)
    return pl.pallas_call(
        query_kernel,
        in_specs=[pl.BlockSpec(memory_space=pltpu.SMEM)] + [whole] * 6,
        out_specs=whole,
        out_shape=jax.ShapeDtypeStruct((NZ, 10, 16, IDIM), jnp.bfloat16),
        compiler_params=kernel_params(),
    )(place, latent, own, mine, theirs, final, beside)


def score_kernel(q_ref, w_ref, k_ref, o_ref, wide_ref, rows_ref):
    scale = IDIM ** (-0.5)
    tile = 256

    @pl.when(pl.program_id(0) == 0)
    def _():
        weights = w_ref[...].astype(jnp.float32) * scale
        for j in range(IHEADS):
            wide_ref[j * 16 : (j + 1) * 16, :] = jnp.broadcast_to(weights[:, j : j + 1], (16, 128))
            rows_ref[j * 16 : (j + 1) * 16, :] = q_ref[j // 8, j % 8]

    blocks, _, slots = o_ref.shape
    for block in range(blocks):
        for slot in range(0, slots, tile):
            at = block * slots + slot
            logits = lax.dot_general(
                rows_ref[...],
                k_ref[at : at + tile, :],
                (((1,), (1,)), ((), ())),
                preferred_element_type=jnp.float32,
            )
            halves = [jnp.zeros((16, 128), jnp.float32), jnp.zeros((16, 128), jnp.float32)]
            for j in range(IHEADS):
                weight = wide_ref[j * 16 : (j + 1) * 16, :]
                for n in range(2):
                    halves[n] += (
                        jnp.maximum(logits[j * 16 : (j + 1) * 16, n * 128 : (n + 1) * 128], 0.0) * weight
                    )
            for n in range(2):
                o_ref[block, :, slot + n * 128 : slot + (n + 1) * 128] = halves[n].astype(o_ref.dtype)


def make_scores(queries, head_weights, keys):
    per_step = 2
    return pl.pallas_call(
        score_kernel,
        grid=(N_SEQ // per_step,),
        in_specs=[
            pl.BlockSpec(queries.shape, lambda i: (0, 0, 0, 0)),
            pl.BlockSpec((16, 128), lambda i: (0, 0)),
            pl.BlockSpec((per_step * SLOTS, IDIM), lambda i: (i, 0)),
        ],
        out_specs=pl.BlockSpec((per_step, 16, SLOTS), lambda i: (i, 0, 0)),
        out_shape=jax.ShapeDtypeStruct((N_SEQ, 16, SLOTS), jnp.bfloat16),
        scratch_shapes=[
            pltpu.VMEM((IHEADS * 16, 128), jnp.float32),
            pltpu.VMEM((IHEADS * 16, IDIM), jnp.bfloat16),
        ],
        compiler_params=big_params(),
    )(queries, head_weights, keys)


def finish_kernel(numbers_ref, s_ref, pos_ref, o_ref):
    local = lax.broadcasted_iota(jnp.int32, (16, SLOTS), 1)
    filled, base = numbers_ref[0], numbers_ref[1]
    for group in range(N_SEQ):
        here = slice(group * 16, (group + 1) * 16)
        reach = jnp.minimum(filled, pos_ref[here, :] - base + 1)
        o_ref[here, :] = jnp.where(local < reach, s_ref[group].astype(jnp.float32), 0.0)


def finish(numbers, scores, own_positions):
    whole = pl.BlockSpec(memory_space=pltpu.VMEM)
    return pl.pallas_call(
        finish_kernel,
        in_specs=[pl.BlockSpec(memory_space=pltpu.SMEM), whole, whole],
        out_specs=whole,
        out_shape=jax.ShapeDtypeStruct((N_SEQ * 16, SLOTS), jnp.float32),
        compiler_params=kernel_params(),
    )(numbers, scores, own_positions)


def down_weight_rows(latent_weight, index_proj, piece):
    share = DZ // N_SEQ

    def own_rows(weight):
        return lax.dynamic_slice_in_dim(weight.reshape(NZ, DZ, weight.shape[1]), piece * share, share, 1)

    own = jnp.concatenate([own_rows(latent_weight), own_rows(index_proj)], axis=2)
    by_head = lax.all_to_all(jnp.repeat(own, 2, axis=0), HEAD, 0, 0).transpose(1, 0, 2)
    local = latent_weight.shape[1]
    wide = jnp.concatenate(
        [
            by_head[:, :, :local].reshape(share, QL),
            by_head[:, :, local:].reshape(share, IHEADS),
            jnp.zeros((share, 64), jnp.bfloat16),
        ],
        axis=1,
    )
    half = lax.all_to_all(jnp.broadcast_to(wide[None], (8,) + wide.shape), ("x", "yl"), 0, 0)
    half = half.reshape(8 * share, wide.shape[1])
    return half, swap(half, "c")


def turn(values):
    moves = [(s * N_HEAD + h, h * N_HEAD + s) for s in range(N_SEQ) for h in range(N_HEAD)]
    return lax.ppermute(values, SEQ + HEAD, moves)


def shards(
    attn_out,
    out_weight,
    residual,
    norm_gain,
    latent_weight,
    index_proj,
    latent_gain,
    index_weight,
    index_keys,
    positions,
    cache_len,
):
    x, yl, c = (lax.axis_index(a) for a in SEQ)
    z, yh = (lax.axis_index(a) for a in HEAD)
    seq = (x * 2 + yl) * 2 + c
    head = z * 2 + yh
    rows = attn_out.shape[0]
    own = rows // N_HEAD
    local = latent_weight.shape[1]

    partial = project(jnp.stack([head]).astype(jnp.int32), attn_out, out_weight, residual)
    summed = lax.psum_scatter(partial, "z", scatter_dimension=0, tiled=False)

    depth = QL // 2
    weight_mine = swap(lax.dynamic_slice_in_dim(index_weight, c * depth, depth, 0), "yh")
    weight_theirs = swap(weight_mine, "c")
    down_mine, down_other = down_weight_rows(latent_weight, index_proj, c * 8 + x * 2 + yl)
    summed, index_keys, down_mine, down_other = lax.optimization_barrier(
        (summed, index_keys, down_mine, down_other)
    )
    all_keys = lax.all_gather(index_keys, SEQ, axis=0, tiled=True)
    kept, got = summed[0], swap(summed[1], "yh")
    gain = lax.dynamic_slice_in_dim(norm_gain, z * DZ, DZ).reshape(1, DZ)
    hidden, lifted = lift(jnp.stack([c]).astype(jnp.int32), kept, got, gain, down_mine, down_other)
    parts = lax.all_to_all(lifted.reshape(NZ, own, lifted.shape[1]), "z", 0, 0)
    total = jnp.sum(parts.astype(jnp.float32), axis=0)
    mean = (total[:, 1600:1601] + total[:, 1601:1602]) / D
    inverse = lax.rsqrt(mean + EPSILON)
    latent_raw = (total[:, :QL] * inverse).astype(jnp.bfloat16)
    head_weights = (total[:, QL:1600] * inverse * IHEADS ** (-0.5)).astype(jnp.bfloat16)
    latent = rms_round(latent_raw, latent_gain)
    packed = jnp.concatenate([latent, head_weights, jnp.zeros((own, 64), jnp.bfloat16)], axis=1)
    turned = turn(packed)
    give = lax.dynamic_index_in_dim(latent.reshape(own, NZ, 2, local), 1 - yh, 2, keepdims=False)
    beside = swap(give.reshape(own, NZ * local), "yh")
    everyone = lax.all_to_all(jnp.broadcast_to(turned[None], (NZ,) + turned.shape), "z", 0, 0)
    everyone = everyone.reshape(HALF, packed.shape[1])
    everyone, hidden = lax.optimization_barrier((everyone, hidden))
    all_hidden = lax.all_gather(hidden, "z", axis=0, tiled=False)
    hidden_rows = lax.dynamic_slice_in_dim(all_hidden, z * own, own, 1)
    hidden_rows = hidden_rows.transpose(1, 0, 2).reshape(own, D)
    place = jnp.stack([c, yh]).astype(jnp.int32)
    queries = make_queries(place, everyone, index_weight, weight_mine, weight_theirs, latent, beside)
    queries = lax.all_to_all(queries, "z", 0, 0)
    latent_out = queries[:, 8:, :, :local].reshape(rows, local)
    scores = make_scores(queries, turned[:, QL:], all_keys)
    scores = lax.all_to_all(scores, SEQ, 0, 0)

    own_positions = lax.dynamic_slice_in_dim(positions, head * rows, rows).reshape(rows, 1)
    numbers = jnp.stack([cache_len[0], seq * SLOTS]).astype(jnp.int32)
    return (hidden_rows, latent_out, finish(numbers, scores, own_positions))


def solution(mesh):
    fine = Mesh(mesh.devices.reshape(4, 2, 2, 8, 2), SEQ + HEAD)
    in_specs = (
        P(SEQ, HEAD),
        P(HEAD, None),
        P(SEQ + HEAD, None),
        P(),
        P(None, HEAD),
        P(None, HEAD),
        P(),
        P(None, HEAD),
        P(SEQ, None),
        P(),
        P(SEQ),
    )
    out_specs = (P(SEQ + HEAD, None), P(SEQ, HEAD), P(HEAD, SEQ))
    return jax.shard_map(shards, mesh=fine, in_specs=in_specs, out_specs=out_specs, check_vma=False)
```

```python
import functools

import jax
import jax.numpy as jnp
from jax import lax
from jax.experimental import pallas as pl
from jax.experimental.pallas import tpu as pltpu
from jax.sharding import Mesh
from jax.sharding import PartitionSpec as P

D = 7168
QL = 1536
IHEADS = 64
IDIM = 128
N_SEQ = 16
N_HEAD = 16
NZ = 8
DZ = D // NZ
EPSILON = 1e-06
SEQ = ("x", "yl", "c")
HEAD = ("z", "yh")
HALF = 128
SLOTS = 1024


def swap(values, axis):
    return lax.ppermute(values, axis, [(0, 1), (1, 0)])


def shift(values, axis, size, by):
    return lax.ppermute(values, axis, [(i, (i + by) % size) for i in range(size)])


def kernel_params():
    return pltpu.CompilerParams(vmem_limit_bytes=20 * 1024 * 1024)


def big_params():
    return pltpu.CompilerParams(vmem_limit_bytes=60 * 1024 * 1024)


def project_kernel(head_ref, a_ref, b_ref, res_ref, o_ref, b_held, o_held, in_sems, out_sems):
    rows = a_ref.shape[0]

    def fetch(i):
        columns = pl.ds(pl.multiple_of(i * DZ, 128), DZ)
        return pltpu.make_async_copy(b_ref.at[:, columns], b_held.at[i], in_sems.at[i])

    def store(i):
        return pltpu.make_async_copy(o_held.at[i], o_ref.at[i], out_sems.at[i])

    for i in range(NZ):
        fetch(i).start()
    own = lax.broadcasted_iota(jnp.int32, (rows, 16), 1) + head_ref[0] * 16
    place = lax.broadcasted_iota(jnp.int32, (rows, 16), 0) == own
    place = jnp.where(place, 1.0, 0.0).astype(jnp.bfloat16)

    @pl.loop(0, NZ)
    def _(i):
        columns = pl.ds(pl.multiple_of(i * DZ, 128), DZ)
        fetch(i).wait()
        product = jnp.dot(a_ref[...], b_held[i], preferred_element_type=jnp.float32)
        product = product + jnp.dot(place, res_ref[:, columns], preferred_element_type=jnp.float32)
        product = product.astype(o_ref.dtype)
        for group in range(NZ):
            for half in range(2):
                o_held[i, half ^ (head_ref[0] % 2), group * 16 : (group + 1) * 16, :] = product[
                    group * 32 + half * 16 : group * 32 + (half + 1) * 16, :
                ]
        store(i).start()

    for i in range(NZ):
        store(i).wait()


def project(head, attn_out, out_weight, residual):
    rows, depth = attn_out.shape
    whole = pl.BlockSpec(memory_space=pltpu.VMEM)
    apart = pl.BlockSpec(memory_space=pl.ANY)
    shape = (NZ, 2, HALF, DZ)
    return pl.pallas_call(
        project_kernel,
        in_specs=[pl.BlockSpec(memory_space=pltpu.SMEM), whole, apart, whole],
        out_specs=apart,
        out_shape=jax.ShapeDtypeStruct(shape, jnp.bfloat16),
        scratch_shapes=[
            pltpu.VMEM((NZ, depth, DZ), jnp.bfloat16),
            pltpu.VMEM(shape, jnp.bfloat16),
            pltpu.SemaphoreType.DMA((NZ,)),
            pltpu.SemaphoreType.DMA((NZ,)),
        ],
        compiler_params=big_params(),
    )(head, attn_out, out_weight, residual)


def lift_kernel(core_ref, kept_ref, got_ref, gain_ref, mine_ref, other_ref, hidden_ref, o_ref):
    hidden = (kept_ref[0].astype(jnp.float32) + got_ref[...].astype(jnp.float32)).astype(jnp.bfloat16)
    hidden_ref[...] = hidden
    wide = hidden.astype(jnp.float32)
    squares = jnp.sum(wide * wide, axis=1, keepdims=True)
    high = squares.astype(jnp.bfloat16).astype(jnp.float32)
    scaled = wide * gain_ref[...].astype(jnp.float32)
    first, second = scaled[:, : DZ // 2], scaled[:, DZ // 2 :]
    is_first = core_ref[0] == 0
    mine = jnp.where(is_first, first, second).astype(jnp.bfloat16)
    other = jnp.where(is_first, second, first).astype(jnp.bfloat16)
    lifted = jnp.dot(mine, mine_ref[...], preferred_element_type=jnp.float32) + jnp.dot(
        other, other_ref[...], preferred_element_type=jnp.float32
    )
    lane = lax.broadcasted_iota(jnp.int32, (HALF, 128), 1)
    tail = jnp.where(lane == IHEADS, high, jnp.where(lane == IHEADS + 1, squares - high, 0.0))
    o_ref[:, :QL] = lifted[:, :QL].astype(jnp.bfloat16)
    o_ref[:, QL:] = jnp.where(lane < IHEADS, lifted[:, QL:], tail).astype(jnp.bfloat16)


def lift(core, kept, got, gain, mine, other):
    whole = pl.BlockSpec(memory_space=pltpu.VMEM)
    return pl.pallas_call(
        lift_kernel,
        in_specs=[pl.BlockSpec(memory_space=pltpu.SMEM)] + [whole] * 5,
        out_specs=[whole, whole],
        out_shape=[
            jax.ShapeDtypeStruct((HALF, DZ), jnp.bfloat16),
            jax.ShapeDtypeStruct((HALF, QL + 128), jnp.bfloat16),
        ],
        compiler_params=kernel_params(),
    )(core, kept, got, gain, mine, other)


def norm_kernel(high_ref, parts_ref, gain_ref, o_ref, give_ref):
    total = parts_ref[0].astype(jnp.float32)
    for n in range(1, NZ):
        total = total + parts_ref[n].astype(jnp.float32)
    mean = (total[:, 1600:1601] + total[:, 1601:1602]) / D
    inverse = lax.rsqrt(mean + EPSILON)
    raw = (total[:, :QL] * inverse).astype(jnp.bfloat16).astype(jnp.float32)
    level = lax.rsqrt(jnp.mean(raw * raw, axis=-1, keepdims=True) + EPSILON)
    latent = (raw * level * gain_ref[...].astype(jnp.float32)).astype(jnp.bfloat16)
    lane = lax.broadcasted_iota(jnp.int32, (16, 128), 1)
    weights = jnp.where(lane < IHEADS, total[:, QL:] * inverse * IHEADS ** (-0.5), 0.0)
    o_ref[:, :QL] = latent
    o_ref[:, QL:] = weights.astype(jnp.bfloat16)
    for block in range(NZ):
        low = latent[:, block * 192 : block * 192 + 96]
        top = latent[:, block * 192 + 96 : block * 192 + 192]
        give_ref[:, block * 96 : (block + 1) * 96] = jnp.where(high_ref[0] == 0, top, low)


def normalize(high, parts, gain):
    whole = pl.BlockSpec(memory_space=pltpu.VMEM)
    return pl.pallas_call(
        norm_kernel,
        in_specs=[pl.BlockSpec(memory_space=pltpu.SMEM), whole, whole],
        out_specs=[whole, whole],
        out_shape=[
            jax.ShapeDtypeStruct((16, QL + 128), jnp.bfloat16),
            jax.ShapeDtypeStruct((16, QL // 2), jnp.bfloat16),
        ],
        compiler_params=kernel_params(),
    )(high, parts, gain)


def query_kernel(place_ref, latent_ref, own_ref, mine_ref, theirs_ref, final_ref, beside_ref, o_ref):
    core, high = place_ref[0], place_ref[1]
    is_first = core == 0
    left, right = latent_ref[:, : QL // 2], latent_ref[:, QL // 2 : QL]
    here = jnp.where(is_first, left, right)
    there = jnp.where(is_first, right, left)
    own = jnp.dot(latent_ref[:, :QL], own_ref[...], preferred_element_type=jnp.float32)
    other = jnp.dot(here, mine_ref[...], preferred_element_type=jnp.float32) + jnp.dot(
        there, theirs_ref[...], preferred_element_type=jnp.float32
    )
    for at, part in ((high * 4, own), ((1 - high) * 4, other)):
        part = part.astype(jnp.bfloat16)
        for j in range(4):
            for block in range(NZ):
                o_ref[block, at + j] = part[block * 16 : (block + 1) * 16, j * IDIM : (j + 1) * IDIM]
    o_ref[:, 8:] = jnp.zeros((NZ, 2, 16, IDIM), jnp.bfloat16)
    for block in range(NZ):
        low = final_ref[:, block * 192 : block * 192 + 96]
        top = final_ref[:, block * 192 + 96 : block * 192 + 192]
        o_ref[block, 8 + high, :, :96] = jnp.where(high == 0, low, top)
        o_ref[block, 9 - high, :, :96] = beside_ref[:, block * 96 : (block + 1) * 96]


def make_queries(place, latent, own, mine, theirs, final, beside):
    whole = pl.BlockSpec(memory_space=pltpu.VMEM)
    return pl.pallas_call(
        query_kernel,
        in_specs=[pl.BlockSpec(memory_space=pltpu.SMEM)] + [whole] * 6,
        out_specs=whole,
        out_shape=jax.ShapeDtypeStruct((NZ, 10, 16, IDIM), jnp.bfloat16),
        compiler_params=kernel_params(),
    )(place, latent, own, mine, theirs, final, beside)


def score_kernel(q_ref, w_ref, k_ref, o_ref, wide_ref, rows_ref):
    scale = IDIM ** (-0.5)
    tile = 256

    @pl.when(pl.program_id(0) == 0)
    def _():
        weights = w_ref[...].astype(jnp.float32) * scale
        for j in range(IHEADS):
            wide_ref[j * 16 : (j + 1) * 16, :] = jnp.broadcast_to(weights[:, j : j + 1], (16, 128))
            rows_ref[j * 16 : (j + 1) * 16, :] = q_ref[j // 8, j % 8]

    blocks, _, slots = o_ref.shape
    for block in range(blocks):
        for slot in range(0, slots, tile):
            at = block * slots + slot
            logits = lax.dot_general(
                rows_ref[...],
                k_ref[at : at + tile, :],
                (((1,), (1,)), ((), ())),
                preferred_element_type=jnp.float32,
            )
            halves = [jnp.zeros((16, 128), jnp.float32), jnp.zeros((16, 128), jnp.float32)]
            for j in range(IHEADS):
                weight = wide_ref[j * 16 : (j + 1) * 16, :]
                for n in range(2):
                    halves[n] += (
                        jnp.maximum(logits[j * 16 : (j + 1) * 16, n * 128 : (n + 1) * 128], 0.0) * weight
                    )
            for n in range(2):
                o_ref[block, :, slot + n * 128 : slot + (n + 1) * 128] = halves[n].astype(o_ref.dtype)


def make_scores(queries, head_weights, keys):
    per_step = 2
    return pl.pallas_call(
        score_kernel,
        grid=(N_SEQ // per_step,),
        in_specs=[
            pl.BlockSpec(queries.shape, lambda i: (0, 0, 0, 0)),
            pl.BlockSpec((16, 128), lambda i: (0, 0)),
            pl.BlockSpec((per_step * SLOTS, IDIM), lambda i: (i, 0)),
        ],
        out_specs=pl.BlockSpec((per_step, 16, SLOTS), lambda i: (i, 0, 0)),
        out_shape=jax.ShapeDtypeStruct((N_SEQ, 16, SLOTS), jnp.bfloat16),
        scratch_shapes=[
            pltpu.VMEM((IHEADS * 16, 128), jnp.float32),
            pltpu.VMEM((IHEADS * 16, IDIM), jnp.bfloat16),
        ],
        compiler_params=big_params(),
    )(queries, head_weights, keys)


def finish_kernel(numbers_ref, s_ref, pos_ref, o_ref):
    local = lax.broadcasted_iota(jnp.int32, (16, SLOTS), 1)
    filled, base = numbers_ref[0], numbers_ref[1]
    for group in range(N_SEQ):
        here = slice(group * 16, (group + 1) * 16)
        reach = jnp.minimum(filled, pos_ref[here, :] - base + 1)
        o_ref[here, :] = jnp.where(local < reach, s_ref[group].astype(jnp.float32), 0.0)


def finish(numbers, scores, own_positions):
    whole = pl.BlockSpec(memory_space=pltpu.VMEM)
    return pl.pallas_call(
        finish_kernel,
        in_specs=[pl.BlockSpec(memory_space=pltpu.SMEM), whole, whole],
        out_specs=whole,
        out_shape=jax.ShapeDtypeStruct((N_SEQ * 16, SLOTS), jnp.float32),
        compiler_params=kernel_params(),
    )(numbers, scores, own_positions)


def down_weight_rows(latent_weight, index_proj, piece, early):
    share = DZ // N_SEQ

    def own_rows(weight):
        return lax.dynamic_slice_in_dim(weight.reshape(NZ, DZ, weight.shape[1]), piece * share, share, 1)

    own = jnp.concatenate([own_rows(latent_weight), own_rows(index_proj)], axis=2)
    by_head = lax.all_to_all(jnp.repeat(own, 2, axis=0), HEAD, 0, 0).transpose(1, 0, 2)
    local = latent_weight.shape[1]
    wide = jnp.concatenate(
        [
            by_head[:, :, :local].reshape(share, QL),
            by_head[:, :, local:].reshape(share, IHEADS),
            jnp.zeros((share, 64), jnp.bfloat16),
        ],
        axis=1,
    )
    wide, early = lax.optimization_barrier((wide, early))
    half = lax.all_to_all(jnp.broadcast_to(wide[None], (8,) + wide.shape), ("x", "yl"), 0, 0)
    half = half.reshape(8 * share, wide.shape[1])
    return half, swap(half, "c"), early


def turn(values):
    moves = [(s * N_HEAD + h, h * N_HEAD + s) for s in range(N_SEQ) for h in range(N_HEAD)]
    return lax.ppermute(values, SEQ + HEAD, moves)


def shards(
    attn_out,
    out_weight,
    residual,
    norm_gain,
    latent_weight,
    index_proj,
    latent_gain,
    index_weight,
    index_keys,
    positions,
    cache_len,
):
    x, yl, c = (lax.axis_index(a) for a in SEQ)
    z, yh = (lax.axis_index(a) for a in HEAD)
    seq = (x * 2 + yl) * 2 + c
    head = z * 2 + yh
    rows = attn_out.shape[0]
    own = rows // N_HEAD
    local = latent_weight.shape[1]

    partial = project(jnp.stack([head]).astype(jnp.int32), attn_out, out_weight, residual)
    summed = lax.psum_scatter(partial, "z", scatter_dimension=0, tiled=False)

    depth = QL // 2
    weight_mine = swap(lax.dynamic_slice_in_dim(index_weight, c * depth, depth, 0), "yh")
    down_mine, down_other, weight_mine = down_weight_rows(
        latent_weight, index_proj, c * 8 + x * 2 + yl, weight_mine
    )
    weight_theirs = swap(weight_mine, "c")
    summed, index_keys, down_mine, down_other = lax.optimization_barrier(
        (summed, index_keys, down_mine, down_other)
    )
    all_keys = lax.all_gather(index_keys, SEQ, axis=0, tiled=True)
    got = swap(summed[1], "yh")
    gain = lax.dynamic_slice_in_dim(norm_gain, z * DZ, DZ).reshape(1, DZ)
    hidden, lifted = lift(jnp.stack([c]).astype(jnp.int32), summed, got, gain, down_mine, down_other)
    parts = lax.all_to_all(lifted.reshape(NZ, own, lifted.shape[1]), "z", 0, 0)
    packed, give = normalize(jnp.stack([yh]).astype(jnp.int32), parts, latent_gain.reshape(1, QL))
    turned, beside = lax.optimization_barrier((turn(packed), swap(give, "yh")))
    everyone = lax.all_to_all(jnp.broadcast_to(turned[None], (NZ,) + turned.shape), "z", 0, 0)
    everyone = everyone.reshape(HALF, packed.shape[1])
    everyone, hidden = lax.optimization_barrier((everyone, hidden))
    all_hidden = lax.all_gather(hidden, "z", axis=0, tiled=False)
    hidden_rows = lax.dynamic_slice_in_dim(all_hidden, z * own, own, 1)
    hidden_rows = hidden_rows.transpose(1, 0, 2).reshape(own, D)
    place = jnp.stack([c, yh]).astype(jnp.int32)
    queries = make_queries(place, everyone, index_weight, weight_mine, weight_theirs, packed, beside)
    queries = lax.all_to_all(queries, "z", 0, 0)
    latent_out = queries[:, 8:, :, :local].reshape(rows, local)
    scores = make_scores(queries, turned[:, QL:], all_keys)
    scores = lax.all_to_all(scores, SEQ, 0, 0)

    own_positions = lax.dynamic_slice_in_dim(positions, head * rows, rows).reshape(rows, 1)
    numbers = jnp.stack([cache_len[0], seq * SLOTS]).astype(jnp.int32)
    return (hidden_rows, latent_out, finish(numbers, scores, own_positions))


def solution(mesh):
    fine = Mesh(mesh.devices.reshape(4, 2, 2, 8, 2), SEQ + HEAD)
    in_specs = (
        P(SEQ, HEAD),
        P(HEAD, None),
        P(SEQ + HEAD, None),
        P(),
        P(None, HEAD),
        P(None, HEAD),
        P(),
        P(None, HEAD),
        P(SEQ, None),
        P(),
        P(SEQ),
    )
    out_specs = (P(SEQ + HEAD, None), P(SEQ, HEAD), P(HEAD, SEQ))
    return jax.shard_map(shards, mesh=fine, in_specs=in_specs, out_specs=out_specs, check_vma=False)
```

```python
import functools

import jax
import jax.numpy as jnp
from jax import lax
from jax.experimental import pallas as pl
from jax.experimental.pallas import tpu as pltpu
from jax.sharding import Mesh
from jax.sharding import PartitionSpec as P

D = 7168
QL = 1536
IHEADS = 64
IDIM = 128
N_SEQ = 16
N_HEAD = 16
NZ = 8
DZ = D // NZ
EPSILON = 1e-06
SEQ = ("x", "yl", "c")
HEAD = ("z", "yh")
HALF = 128
SLOTS = 1024


def swap(values, axis):
    return lax.ppermute(values, axis, [(0, 1), (1, 0)])


def shift(values, axis, size, by):
    return lax.ppermute(values, axis, [(i, (i + by) % size) for i in range(size)])


def kernel_params():
    return pltpu.CompilerParams(vmem_limit_bytes=20 * 1024 * 1024)


def big_params():
    return pltpu.CompilerParams(vmem_limit_bytes=60 * 1024 * 1024)


def project_kernel(head_ref, a_ref, b_ref, res_ref, o_ref, b_held, o_held, in_sems, out_sems):
    head = head_ref[0]
    own = pl.ds(pl.multiple_of(head // 2 * 16, 16), 16)

    def fetch(i):
        columns = pl.ds(pl.multiple_of(i * DZ, 128), DZ)
        return pltpu.make_async_copy(b_ref.at[:, columns], b_held.at[i], in_sems.at[i])

    def store(i):
        return pltpu.make_async_copy(o_held.at[i], o_ref.at[i], out_sems.at[i])

    for i in range(NZ):
        fetch(i).start()
    @pl.loop(0, NZ)
    def _(i):
        columns = pl.ds(pl.multiple_of(i * DZ, 128), DZ)
        fetch(i).wait()
        product = jnp.dot(a_ref[...], b_held[i], preferred_element_type=jnp.float32)
        product = product.astype(o_ref.dtype)
        for group in range(NZ):
            for half in range(2):
                o_held[i, half ^ (head % 2), group * 16 : (group + 1) * 16, :] = product[
                    group * 32 + half * 16 : group * 32 + (half + 1) * 16, :
                ]
        added = o_held[i, 0, own, :].astype(jnp.float32) + res_ref[:, columns].astype(jnp.float32)
        o_held[i, 0, own, :] = added.astype(o_ref.dtype)
        store(i).start()

    for i in range(NZ):
        store(i).wait()


def project(head, attn_out, out_weight, residual):
    rows, depth = attn_out.shape
    whole = pl.BlockSpec(memory_space=pltpu.VMEM)
    apart = pl.BlockSpec(memory_space=pl.ANY)
    shape = (NZ, 2, HALF, DZ)
    return pl.pallas_call(
        project_kernel,
        in_specs=[pl.BlockSpec(memory_space=pltpu.SMEM), whole, apart, whole],
        out_specs=apart,
        out_shape=jax.ShapeDtypeStruct(shape, jnp.bfloat16),
        scratch_shapes=[
            pltpu.VMEM((NZ, depth, DZ), jnp.bfloat16),
            pltpu.VMEM(shape, jnp.bfloat16),
            pltpu.SemaphoreType.DMA((NZ,)),
            pltpu.SemaphoreType.DMA((NZ,)),
        ],
        compiler_params=big_params(),
    )(head, attn_out, out_weight, residual)


def lift_kernel(core_ref, kept_ref, got_ref, gain_ref, mine_ref, other_ref, hidden_ref, o_ref):
    hidden = (kept_ref[...].astype(jnp.float32) + got_ref[...].astype(jnp.float32)).astype(jnp.bfloat16)
    hidden_ref[...] = hidden
    wide = hidden.astype(jnp.float32)
    squares = jnp.sum(wide * wide, axis=1, keepdims=True)
    high = squares.astype(jnp.bfloat16).astype(jnp.float32)
    scaled = wide * gain_ref[...].astype(jnp.float32)
    first, second = scaled[:, : DZ // 2], scaled[:, DZ // 2 :]
    is_first = core_ref[0] == 0
    mine = jnp.where(is_first, first, second).astype(jnp.bfloat16)
    other = jnp.where(is_first, second, first).astype(jnp.bfloat16)
    lifted = jnp.dot(mine, mine_ref[...], preferred_element_type=jnp.float32) + jnp.dot(
        other, other_ref[...], preferred_element_type=jnp.float32
    )
    lane = lax.broadcasted_iota(jnp.int32, (HALF, 128), 1)
    tail = jnp.where(lane == IHEADS, high, jnp.where(lane == IHEADS + 1, squares - high, 0.0))
    o_ref[:, :QL] = lifted[:, :QL].astype(jnp.bfloat16)
    o_ref[:, QL:] = jnp.where(lane < IHEADS, lifted[:, QL:], tail).astype(jnp.bfloat16)


def lift(core, kept, got, gain, mine, other):
    whole = pl.BlockSpec(memory_space=pltpu.VMEM)
    return pl.pallas_call(
        lift_kernel,
        in_specs=[pl.BlockSpec(memory_space=pltpu.SMEM)] + [whole] * 5,
        out_specs=[whole, whole],
        out_shape=[
            jax.ShapeDtypeStruct((HALF, DZ), jnp.bfloat16),
            jax.ShapeDtypeStruct((HALF, QL + 128), jnp.bfloat16),
        ],
        compiler_params=kernel_params(),
    )(core, kept, got, gain, mine, other)


def norm_kernel(high_ref, parts_ref, gain_ref, o_ref, give_ref):
    total = parts_ref[0].astype(jnp.float32)
    for n in range(1, NZ):
        total = total + parts_ref[n].astype(jnp.float32)
    mean = (total[:, 1600:1601] + total[:, 1601:1602]) / D
    inverse = lax.rsqrt(mean + EPSILON)
    raw = (total[:, :QL] * inverse).astype(jnp.bfloat16).astype(jnp.float32)
    level = lax.rsqrt(jnp.mean(raw * raw, axis=-1, keepdims=True) + EPSILON)
    latent = (raw * level * gain_ref[...].astype(jnp.float32)).astype(jnp.bfloat16)
    lane = lax.broadcasted_iota(jnp.int32, (16, 128), 1)
    weights = jnp.where(lane < IHEADS, total[:, QL:] * inverse * IHEADS ** (-0.5), 0.0)
    o_ref[:, :QL] = latent
    o_ref[:, QL:] = weights.astype(jnp.bfloat16)
    for block in range(NZ):
        low = latent[:, block * 192 : block * 192 + 96]
        top = latent[:, block * 192 + 96 : block * 192 + 192]
        give_ref[:, block * 96 : (block + 1) * 96] = jnp.where(high_ref[0] == 0, top, low)


def normalize(high, parts, gain):
    whole = pl.BlockSpec(memory_space=pltpu.VMEM)
    return pl.pallas_call(
        norm_kernel,
        in_specs=[pl.BlockSpec(memory_space=pltpu.SMEM), whole, whole],
        out_specs=[whole, whole],
        out_shape=[
            jax.ShapeDtypeStruct((16, QL + 128), jnp.bfloat16),
            jax.ShapeDtypeStruct((16, QL // 2), jnp.bfloat16),
        ],
        compiler_params=kernel_params(),
    )(high, parts, gain)


def query_kernel(place_ref, latent_ref, own_ref, mine_ref, theirs_ref, final_ref, beside_ref, o_ref):
    core, high = place_ref[0], place_ref[1]
    is_first = core == 0
    left, right = latent_ref[:, : QL // 2], latent_ref[:, QL // 2 : QL]
    here = jnp.where(is_first, left, right)
    there = jnp.where(is_first, right, left)
    own = jnp.dot(latent_ref[:, :QL], own_ref[...], preferred_element_type=jnp.float32)
    other = jnp.dot(here, mine_ref[...], preferred_element_type=jnp.float32) + jnp.dot(
        there, theirs_ref[...], preferred_element_type=jnp.float32
    )
    for at, part in ((high * 4, own), ((1 - high) * 4, other)):
        part = part.astype(jnp.bfloat16)
        for j in range(4):
            for block in range(NZ):
                o_ref[block, at + j] = part[block * 16 : (block + 1) * 16, j * IDIM : (j + 1) * IDIM]
    o_ref[:, 8:] = jnp.zeros((NZ, 2, 16, IDIM), jnp.bfloat16)
    for block in range(NZ):
        low = final_ref[:, block * 192 : block * 192 + 96]
        top = final_ref[:, block * 192 + 96 : block * 192 + 192]
        o_ref[block, 8 + high, :, :96] = jnp.where(high == 0, low, top)
        o_ref[block, 9 - high, :, :96] = beside_ref[:, block * 96 : (block + 1) * 96]


def make_queries(place, latent, own, mine, theirs, final, beside):
    whole = pl.BlockSpec(memory_space=pltpu.VMEM)
    return pl.pallas_call(
        query_kernel,
        in_specs=[pl.BlockSpec(memory_space=pltpu.SMEM)] + [whole] * 6,
        out_specs=whole,
        out_shape=jax.ShapeDtypeStruct((NZ, 10, 16, IDIM), jnp.bfloat16),
        compiler_params=kernel_params(),
    )(place, latent, own, mine, theirs, final, beside)


def score_kernel(q_ref, w_ref, k_ref, o_ref, wide_ref, rows_ref):
    scale = IDIM ** (-0.5)
    tile = 256

    @pl.when(pl.program_id(0) == 0)
    def _():
        weights = w_ref[...].astype(jnp.float32) * scale
        for j in range(IHEADS):
            wide_ref[j * 16 : (j + 1) * 16, :] = jnp.broadcast_to(weights[:, j : j + 1], (16, 128))
            rows_ref[j * 16 : (j + 1) * 16, :] = q_ref[j // 8, j % 8]

    blocks, _, slots = o_ref.shape
    for block in range(blocks):
        for slot in range(0, slots, tile):
            at = block * slots + slot
            logits = lax.dot_general(
                rows_ref[...],
                k_ref[at : at + tile, :],
                (((1,), (1,)), ((), ())),
                preferred_element_type=jnp.float32,
            )
            halves = [jnp.zeros((16, 128), jnp.float32), jnp.zeros((16, 128), jnp.float32)]
            for j in range(IHEADS):
                weight = wide_ref[j * 16 : (j + 1) * 16, :]
                for n in range(2):
                    halves[n] += (
                        jnp.maximum(logits[j * 16 : (j + 1) * 16, n * 128 : (n + 1) * 128], 0.0) * weight
                    )
            for n in range(2):
                o_ref[block, :, slot + n * 128 : slot + (n + 1) * 128] = halves[n].astype(o_ref.dtype)


def make_scores(queries, head_weights, keys):
    per_step = 2
    return pl.pallas_call(
        score_kernel,
        grid=(N_SEQ // per_step,),
        in_specs=[
            pl.BlockSpec(queries.shape, lambda i: (0, 0, 0, 0)),
            pl.BlockSpec((16, 128), lambda i: (0, 0)),
            pl.BlockSpec((per_step * SLOTS, IDIM), lambda i: (i, 0)),
        ],
        out_specs=pl.BlockSpec((per_step, 16, SLOTS), lambda i: (i, 0, 0)),
        out_shape=jax.ShapeDtypeStruct((N_SEQ, 16, SLOTS), jnp.bfloat16),
        scratch_shapes=[
            pltpu.VMEM((IHEADS * 16, 128), jnp.float32),
            pltpu.VMEM((IHEADS * 16, IDIM), jnp.bfloat16),
        ],
        compiler_params=big_params(),
        cost_estimate=pl.CostEstimate(
            flops=4 * IHEADS * 16 * keys.shape[0] * IDIM, bytes_accessed=2 * keys.size * 2, transcendentals=0
        ),
    )(queries, head_weights, keys)


def finish_kernel(numbers_ref, s_ref, pos_ref, o_ref):
    local = lax.broadcasted_iota(jnp.int32, (16, SLOTS), 1)
    filled, base = numbers_ref[0], numbers_ref[1]
    for group in range(N_SEQ):
        here = slice(group * 16, (group + 1) * 16)
        reach = jnp.minimum(filled, pos_ref[here, :] - base + 1)
        o_ref[here, :] = jnp.where(local < reach, s_ref[group].astype(jnp.float32), 0.0)


def finish(numbers, scores, own_positions):
    whole = pl.BlockSpec(memory_space=pltpu.VMEM)
    return pl.pallas_call(
        finish_kernel,
        in_specs=[pl.BlockSpec(memory_space=pltpu.SMEM), whole, whole],
        out_specs=whole,
        out_shape=jax.ShapeDtypeStruct((N_SEQ * 16, SLOTS), jnp.float32),
        compiler_params=kernel_params(),
    )(numbers, scores, own_positions)


def down_weight_rows(latent_weight, index_proj, piece):
    share = DZ // N_SEQ

    def own_rows(weight):
        return lax.dynamic_slice_in_dim(weight.reshape(NZ, DZ, weight.shape[1]), piece * share, share, 1)

    own = jnp.concatenate([own_rows(latent_weight), own_rows(index_proj)], axis=2)
    by_head = lax.all_to_all(jnp.repeat(own, 2, axis=0), HEAD, 0, 0).transpose(1, 0, 2)
    local = latent_weight.shape[1]
    wide = jnp.concatenate(
        [
            by_head[:, :, :local].reshape(share, QL),
            by_head[:, :, local:].reshape(share, IHEADS),
            jnp.zeros((share, 64), jnp.bfloat16),
        ],
        axis=1,
    )
    half = lax.all_to_all(jnp.broadcast_to(wide[None], (8,) + wide.shape), ("x", "yl"), 0, 0)
    half = half.reshape(8 * share, wide.shape[1])
    return half, swap(half, "c")


def turn(values):
    moves = [(s * N_HEAD + h, h * N_HEAD + s) for s in range(N_SEQ) for h in range(N_HEAD)]
    return lax.ppermute(values, SEQ + HEAD, moves)


def shards(
    attn_out,
    out_weight,
    residual,
    norm_gain,
    latent_weight,
    index_proj,
    latent_gain,
    index_weight,
    index_keys,
    positions,
    cache_len,
):
    x, yl, c = (lax.axis_index(a) for a in SEQ)
    z, yh = (lax.axis_index(a) for a in HEAD)
    seq = (x * 2 + yl) * 2 + c
    head = z * 2 + yh
    rows = attn_out.shape[0]
    own = rows // N_HEAD
    local = latent_weight.shape[1]

    partial = project(jnp.stack([head]).astype(jnp.int32), attn_out, out_weight, residual)
    summed = lax.psum_scatter(partial, "z", scatter_dimension=0, tiled=False)

    down_mine, down_other = down_weight_rows(latent_weight, index_proj, c * 8 + x * 2 + yl)
    summed, index_keys, down_mine, down_other = lax.optimization_barrier(
        (summed, index_keys, down_mine, down_other)
    )
    all_keys = lax.all_gather(index_keys, SEQ, axis=0, tiled=True)
    kept, got = summed[0], swap(summed[1], "yh")
    gain = lax.dynamic_slice_in_dim(norm_gain, z * DZ, DZ).reshape(1, DZ)
    hidden, lifted = lift(jnp.stack([c]).astype(jnp.int32), kept, got, gain, down_mine, down_other)
    lifted, index_weight = lax.optimization_barrier((lifted, index_weight))
    parts = lax.all_to_all(lifted.reshape(NZ, own, lifted.shape[1]), "z", 0, 0)
    depth = QL // 2
    weight_mine = swap(lax.dynamic_slice_in_dim(index_weight, c * depth, depth, 0), "yh")
    weight_theirs = swap(weight_mine, "c")
    packed, give = normalize(jnp.stack([yh]).astype(jnp.int32), parts, latent_gain.reshape(1, QL))
    turned, beside, weight_mine, weight_theirs = lax.optimization_barrier(
        (turn(packed), swap(give, "yh"), weight_mine, weight_theirs)
    )
    everyone = lax.all_to_all(jnp.broadcast_to(turned[None], (NZ,) + turned.shape), "z", 0, 0)
    everyone = everyone.reshape(HALF, packed.shape[1])
    place = jnp.stack([c, yh]).astype(jnp.int32)
    queries = make_queries(place, everyone, index_weight, weight_mine, weight_theirs, packed, beside)
    queries = lax.all_to_all(queries, "z", 0, 0)
    latent_out = queries[:, 8:, :, :local].reshape(rows, local)
    queries, hidden = lax.optimization_barrier((queries, hidden))
    hidden_rows = lax.all_to_all(hidden.reshape(NZ, own, DZ), "z", 0, 0)
    scores = make_scores(queries, turned[:, QL:], all_keys)
    scores, hidden_rows = lax.optimization_barrier((scores, hidden_rows))
    hidden_rows = hidden_rows.transpose(1, 0, 2).reshape(own, D)
    scores = lax.all_to_all(scores, SEQ, 0, 0)

    own_positions = lax.dynamic_slice_in_dim(positions, head * rows, rows).reshape(rows, 1)
    numbers = jnp.stack([cache_len[0], seq * SLOTS]).astype(jnp.int32)
    return (hidden_rows, latent_out, finish(numbers, scores, own_positions))


def solution(mesh):
    fine = Mesh(mesh.devices.reshape(4, 2, 2, 8, 2), SEQ + HEAD)
    in_specs = (
        P(SEQ, HEAD),
        P(HEAD, None),
        P(SEQ + HEAD, None),
        P(),
        P(None, HEAD),
        P(None, HEAD),
        P(),
        P(None, HEAD),
        P(SEQ, None),
        P(),
        P(SEQ),
    )
    out_specs = (P(SEQ + HEAD, None), P(SEQ, HEAD), P(HEAD, SEQ))
    return jax.shard_map(shards, mesh=fine, in_specs=in_specs, out_specs=out_specs, check_vma=False)
```

```python
import functools

import jax
import jax.numpy as jnp
from jax import lax
from jax.experimental import pallas as pl
from jax.experimental.pallas import tpu as pltpu
from jax.sharding import Mesh
from jax.sharding import PartitionSpec as P

D = 7168
QL = 1536
IHEADS = 64
IDIM = 128
N_SEQ = 16
N_HEAD = 16
NZ = 8
DZ = D // NZ
EPSILON = 1e-06
SEQ = ("x", "yl", "c")
HEAD = ("z", "yh")
HALF = 128
SLOTS = 1024


def swap(values, axis):
    return lax.ppermute(values, axis, [(0, 1), (1, 0)])


def shift(values, axis, size, by):
    return lax.ppermute(values, axis, [(i, (i + by) % size) for i in range(size)])


def kernel_params():
    return pltpu.CompilerParams(vmem_limit_bytes=20 * 1024 * 1024)


def big_params():
    return pltpu.CompilerParams(vmem_limit_bytes=60 * 1024 * 1024)


def project_kernel(place_ref, a_ref, b_ref, res_ref, w_ref, o_ref, half_ref, b_held, o_held, in_sems, out_sems, half_sem):
    head, core = place_ref[0] // 2, place_ref[0] % 2
    own = pl.ds(pl.multiple_of(head // 2 * 16, 16), 16)
    depth = half_ref.shape[0]
    half_copy = pltpu.make_async_copy(
        w_ref.at[pl.ds(pl.multiple_of(core * depth, 16), depth), :], half_ref, half_sem
    )

    def fetch(i):
        columns = pl.ds(pl.multiple_of(i * DZ, 128), DZ)
        return pltpu.make_async_copy(b_ref.at[:, columns], b_held.at[i], in_sems.at[i])

    def store(i):
        return pltpu.make_async_copy(o_held.at[i], o_ref.at[i], out_sems.at[i])

    for i in range(NZ):
        fetch(i).start()
    half_copy.start()

    @pl.loop(0, NZ)
    def _(i):
        columns = pl.ds(pl.multiple_of(i * DZ, 128), DZ)
        fetch(i).wait()
        product = jnp.dot(a_ref[...], b_held[i], preferred_element_type=jnp.float32)
        product = product.astype(o_ref.dtype)
        for group in range(NZ):
            for half in range(2):
                o_held[i, half ^ (head % 2), group * 16 : (group + 1) * 16, :] = product[
                    group * 32 + half * 16 : group * 32 + (half + 1) * 16, :
                ]
        added = o_held[i, 0, own, :].astype(jnp.float32) + res_ref[:, columns].astype(jnp.float32)
        o_held[i, 0, own, :] = added.astype(o_ref.dtype)
        store(i).start()

    for i in range(NZ):
        store(i).wait()
    half_copy.wait()


def project(place, attn_out, out_weight, residual, index_weight):
    rows, depth = attn_out.shape
    whole = pl.BlockSpec(memory_space=pltpu.VMEM)
    apart = pl.BlockSpec(memory_space=pl.ANY)
    shape = (NZ, 2, HALF, DZ)
    return pl.pallas_call(
        project_kernel,
        in_specs=[pl.BlockSpec(memory_space=pltpu.SMEM), whole, apart, whole, apart],
        out_specs=[apart, apart],
        out_shape=[
            jax.ShapeDtypeStruct(shape, jnp.bfloat16),
            jax.ShapeDtypeStruct((QL // 2, index_weight.shape[1]), jnp.bfloat16),
        ],
        scratch_shapes=[
            pltpu.VMEM((NZ, depth, DZ), jnp.bfloat16),
            pltpu.VMEM(shape, jnp.bfloat16),
            pltpu.SemaphoreType.DMA((NZ,)),
            pltpu.SemaphoreType.DMA((NZ,)),
            pltpu.SemaphoreType.DMA,
        ],
        compiler_params=big_params(),
    )(place, attn_out, out_weight, residual, index_weight)


def lift_kernel(core_ref, kept_ref, got_ref, gain_ref, mine_ref, other_ref, o_ref):
    hidden = (kept_ref[...].astype(jnp.float32) + got_ref[...].astype(jnp.float32)).astype(jnp.bfloat16)
    o_ref[:, QL + 128 :] = hidden
    wide = hidden.astype(jnp.float32)
    squares = jnp.sum(wide * wide, axis=1, keepdims=True)
    high = squares.astype(jnp.bfloat16).astype(jnp.float32)
    scaled = wide * gain_ref[...].astype(jnp.float32)
    first, second = scaled[:, : DZ // 2], scaled[:, DZ // 2 :]
    is_first = core_ref[0] == 0
    mine = jnp.where(is_first, first, second).astype(jnp.bfloat16)
    other = jnp.where(is_first, second, first).astype(jnp.bfloat16)
    lifted = jnp.dot(mine, mine_ref[...], preferred_element_type=jnp.float32) + jnp.dot(
        other, other_ref[...], preferred_element_type=jnp.float32
    )
    lane = lax.broadcasted_iota(jnp.int32, (HALF, 128), 1)
    tail = jnp.where(lane == IHEADS, high, jnp.where(lane == IHEADS + 1, squares - high, 0.0))
    o_ref[:, :QL] = lifted[:, :QL].astype(jnp.bfloat16)
    o_ref[:, QL : QL + 128] = jnp.where(lane < IHEADS, lifted[:, QL:], tail).astype(jnp.bfloat16)


def lift(core, kept, got, gain, mine, other):
    whole = pl.BlockSpec(memory_space=pltpu.VMEM)
    return pl.pallas_call(
        lift_kernel,
        in_specs=[pl.BlockSpec(memory_space=pltpu.SMEM)] + [whole] * 5,
        out_specs=whole,
        out_shape=jax.ShapeDtypeStruct((HALF, QL + 128 + DZ), jnp.bfloat16),
        compiler_params=kernel_params(),
    )(core, kept, got, gain, mine, other)


def norm_kernel(high_ref, parts_ref, gain_ref, o_ref, give_ref, hidden_ref):
    total = parts_ref[0, :, : QL + 128].astype(jnp.float32)
    for n in range(1, NZ):
        total = total + parts_ref[n, :, : QL + 128].astype(jnp.float32)
    for n in range(NZ):
        hidden_ref[:, n * DZ : (n + 1) * DZ] = parts_ref[n, :, QL + 128 :]
    mean = (total[:, 1600:1601] + total[:, 1601:1602]) / D
    inverse = lax.rsqrt(mean + EPSILON)
    raw = (total[:, :QL] * inverse).astype(jnp.bfloat16).astype(jnp.float32)
    level = lax.rsqrt(jnp.mean(raw * raw, axis=-1, keepdims=True) + EPSILON)
    latent = (raw * level * gain_ref[...].astype(jnp.float32)).astype(jnp.bfloat16)
    lane = lax.broadcasted_iota(jnp.int32, (16, 128), 1)
    weights = jnp.where(lane < IHEADS, total[:, QL:] * inverse * IHEADS ** (-0.5), 0.0)
    o_ref[:, :QL] = latent
    o_ref[:, QL:] = weights.astype(jnp.bfloat16)
    for block in range(NZ):
        low = latent[:, block * 192 : block * 192 + 96]
        top = latent[:, block * 192 + 96 : block * 192 + 192]
        give_ref[:, block * 96 : (block + 1) * 96] = jnp.where(high_ref[0] == 0, top, low)


def normalize(high, parts, gain):
    whole = pl.BlockSpec(memory_space=pltpu.VMEM)
    return pl.pallas_call(
        norm_kernel,
        in_specs=[pl.BlockSpec(memory_space=pltpu.SMEM), whole, whole],
        out_specs=[whole] * 3,
        out_shape=[
            jax.ShapeDtypeStruct((16, QL + 128), jnp.bfloat16),
            jax.ShapeDtypeStruct((16, QL // 2), jnp.bfloat16),
            jax.ShapeDtypeStruct((16, D), jnp.bfloat16),
        ],
        compiler_params=kernel_params(),
    )(high, parts, gain)


def query_kernel(place_ref, latent_ref, own_ref, mine_ref, theirs_ref, final_ref, beside_ref, o_ref):
    core, high = place_ref[0], place_ref[1]
    is_first = core == 0
    left, right = latent_ref[:, : QL // 2], latent_ref[:, QL // 2 : QL]
    here = jnp.where(is_first, left, right)
    there = jnp.where(is_first, right, left)
    own = jnp.dot(latent_ref[:, :QL], own_ref[...], preferred_element_type=jnp.float32)
    other = jnp.dot(here, mine_ref[...], preferred_element_type=jnp.float32) + jnp.dot(
        there, theirs_ref[...], preferred_element_type=jnp.float32
    )
    for at, part in ((high * 4, own), ((1 - high) * 4, other)):
        part = part.astype(jnp.bfloat16)
        for j in range(4):
            for block in range(NZ):
                o_ref[block, at + j] = part[block * 16 : (block + 1) * 16, j * IDIM : (j + 1) * IDIM]
    o_ref[:, 8:] = jnp.zeros((NZ, 2, 16, IDIM), jnp.bfloat16)
    for block in range(NZ):
        low = final_ref[:, block * 192 : block * 192 + 96]
        top = final_ref[:, block * 192 + 96 : block * 192 + 192]
        o_ref[block, 8 + high, :, :96] = jnp.where(high == 0, low, top)
        o_ref[block, 9 - high, :, :96] = beside_ref[:, block * 96 : (block + 1) * 96]


def make_queries(place, latent, own, mine, theirs, final, beside):
    whole = pl.BlockSpec(memory_space=pltpu.VMEM)
    return pl.pallas_call(
        query_kernel,
        in_specs=[pl.BlockSpec(memory_space=pltpu.SMEM)] + [whole] * 6,
        out_specs=whole,
        out_shape=jax.ShapeDtypeStruct((NZ, 10, 16, IDIM), jnp.bfloat16),
        compiler_params=kernel_params(),
    )(place, latent, own, mine, theirs, final, beside)


def score_kernel(q_ref, w_ref, k_ref, o_ref, wide_ref, rows_ref):
    scale = IDIM ** (-0.5)
    tile = 256

    @pl.when(pl.program_id(0) == 0)
    def _():
        weights = w_ref[...].astype(jnp.float32) * scale
        for j in range(IHEADS):
            wide_ref[j * 16 : (j + 1) * 16, :] = jnp.broadcast_to(weights[:, j : j + 1], (16, 128))
            rows_ref[j * 16 : (j + 1) * 16, :] = q_ref[j // 8, j % 8]

    blocks, _, slots = o_ref.shape
    for block in range(blocks):
        for slot in range(0, slots, tile):
            at = block * slots + slot
            logits = lax.dot_general(
                rows_ref[...],
                k_ref[at : at + tile, :],
                (((1,), (1,)), ((), ())),
                preferred_element_type=jnp.float32,
            )
            halves = [jnp.zeros((16, 128), jnp.float32), jnp.zeros((16, 128), jnp.float32)]
            for j in range(IHEADS):
                weight = wide_ref[j * 16 : (j + 1) * 16, :]
                for n in range(2):
                    halves[n] += (
                        jnp.maximum(logits[j * 16 : (j + 1) * 16, n * 128 : (n + 1) * 128], 0.0) * weight
                    )
            for n in range(2):
                o_ref[block, :, slot + n * 128 : slot + (n + 1) * 128] = halves[n].astype(o_ref.dtype)


def make_scores(queries, head_weights, keys):
    per_step = 2
    return pl.pallas_call(
        score_kernel,
        grid=(N_SEQ // per_step,),
        in_specs=[
            pl.BlockSpec(queries.shape, lambda i: (0, 0, 0, 0)),
            pl.BlockSpec((16, 128), lambda i: (0, 0)),
            pl.BlockSpec((per_step * SLOTS, IDIM), lambda i: (i, 0)),
        ],
        out_specs=pl.BlockSpec((per_step, 16, SLOTS), lambda i: (i, 0, 0)),
        out_shape=jax.ShapeDtypeStruct((N_SEQ, 16, SLOTS), jnp.bfloat16),
        scratch_shapes=[
            pltpu.VMEM((IHEADS * 16, 128), jnp.float32),
            pltpu.VMEM((IHEADS * 16, IDIM), jnp.bfloat16),
        ],
        compiler_params=big_params(),
        cost_estimate=pl.CostEstimate(
            flops=4 * IHEADS * 16 * keys.shape[0] * IDIM, bytes_accessed=2 * keys.size * 2, transcendentals=0
        ),
    )(queries, head_weights, keys)


def finish_kernel(numbers_ref, s_ref, pos_ref, o_ref):
    local = lax.broadcasted_iota(jnp.int32, (16, SLOTS), 1)
    filled, base = numbers_ref[0], numbers_ref[1]
    for group in range(N_SEQ):
        here = slice(group * 16, (group + 1) * 16)
        reach = jnp.minimum(filled, pos_ref[here, :] - base + 1)
        o_ref[here, :] = jnp.where(local < reach, s_ref[group].astype(jnp.float32), 0.0)


def finish(numbers, scores, own_positions):
    whole = pl.BlockSpec(memory_space=pltpu.VMEM)
    return pl.pallas_call(
        finish_kernel,
        in_specs=[pl.BlockSpec(memory_space=pltpu.SMEM), whole, whole],
        out_specs=whole,
        out_shape=jax.ShapeDtypeStruct((N_SEQ * 16, SLOTS), jnp.float32),
        compiler_params=kernel_params(),
    )(numbers, scores, own_positions)


def down_weight_rows(latent_weight, index_proj, piece, early):
    share = DZ // N_SEQ

    def own_rows(weight):
        return lax.dynamic_slice_in_dim(weight.reshape(NZ, DZ, weight.shape[1]), piece * share, share, 1)

    own = jnp.concatenate([own_rows(latent_weight), own_rows(index_proj)], axis=2)
    by_head = lax.all_to_all(jnp.repeat(own, 2, axis=0), HEAD, 0, 0).transpose(1, 0, 2)
    local = latent_weight.shape[1]
    wide = jnp.concatenate(
        [
            by_head[:, :, :local].reshape(share, QL),
            by_head[:, :, local:].reshape(share, IHEADS),
            jnp.zeros((share, 64), jnp.bfloat16),
        ],
        axis=1,
    )
    wide, early = lax.optimization_barrier((wide, early))
    half = lax.all_to_all(jnp.broadcast_to(wide[None], (8,) + wide.shape), ("x", "yl"), 0, 0)
    half = half.reshape(8 * share, wide.shape[1])
    return half, swap(half, "c"), early


def turn(values):
    moves = [(s * N_HEAD + h, h * N_HEAD + s) for s in range(N_SEQ) for h in range(N_HEAD)]
    return lax.ppermute(values, SEQ + HEAD, moves)


def shards(
    attn_out,
    out_weight,
    residual,
    norm_gain,
    latent_weight,
    index_proj,
    latent_gain,
    index_weight,
    index_keys,
    positions,
    cache_len,
):
    x, yl, c = (lax.axis_index(a) for a in SEQ)
    z, yh = (lax.axis_index(a) for a in HEAD)
    seq = (x * 2 + yl) * 2 + c
    head = z * 2 + yh
    rows = attn_out.shape[0]
    own = rows // N_HEAD
    local = latent_weight.shape[1]

    partial, half_weight = project(
        jnp.stack([head * 2 + c]).astype(jnp.int32), attn_out, out_weight, residual, index_weight
    )
    summed = lax.psum_scatter(partial, "z", scatter_dimension=0, tiled=False)

    weight_mine = swap(half_weight, "yh")
    down_mine, down_other, weight_mine = down_weight_rows(
        latent_weight, index_proj, c * 8 + x * 2 + yl, weight_mine
    )
    weight_theirs = swap(weight_mine, "c")
    summed, index_keys, down_mine, down_other = lax.optimization_barrier(
        (summed, index_keys, down_mine, down_other)
    )
    all_keys = lax.all_gather(index_keys, SEQ, axis=0, tiled=True)
    kept, got = summed[0], swap(summed[1], "yh")
    gain = lax.dynamic_slice_in_dim(norm_gain, z * DZ, DZ).reshape(1, DZ)
    lifted = lift(jnp.stack([c]).astype(jnp.int32), kept, got, gain, down_mine, down_other)
    lifted, weight_theirs = lax.optimization_barrier((lifted, weight_theirs))
    parts = lax.all_to_all(lifted.reshape(NZ, own, lifted.shape[1]), "z", 0, 0)
    packed, give, hidden_rows = normalize(
        jnp.stack([yh]).astype(jnp.int32), parts, latent_gain.reshape(1, QL)
    )
    turned, beside = lax.optimization_barrier((turn(packed), swap(give, "yh")))
    everyone = lax.all_to_all(jnp.broadcast_to(turned[None], (NZ,) + turned.shape), "z", 0, 0)
    everyone = everyone.reshape(HALF, packed.shape[1])
    place = jnp.stack([c, yh]).astype(jnp.int32)
    queries = make_queries(place, everyone, index_weight, weight_mine, weight_theirs, packed, beside)
    queries = lax.all_to_all(queries, "z", 0, 0)
    latent_out = queries[:, 8:, :, :local].reshape(rows, local)
    scores = make_scores(queries, turned[:, QL:], all_keys)
    scores = lax.all_to_all(scores, SEQ, 0, 0)

    own_positions = lax.dynamic_slice_in_dim(positions, head * rows, rows).reshape(rows, 1)
    numbers = jnp.stack([cache_len[0], seq * SLOTS]).astype(jnp.int32)
    return (hidden_rows, latent_out, finish(numbers, scores, own_positions))


def solution(mesh):
    fine = Mesh(mesh.devices.reshape(4, 2, 2, 8, 2), SEQ + HEAD)
    in_specs = (
        P(SEQ, HEAD),
        P(HEAD, None),
        P(SEQ + HEAD, None),
        P(),
        P(None, HEAD),
        P(None, HEAD),
        P(),
        P(None, HEAD),
        P(SEQ, None),
        P(),
        P(SEQ),
    )
    out_specs = (P(SEQ + HEAD, None), P(SEQ, HEAD), P(HEAD, SEQ))
    return jax.shard_map(shards, mesh=fine, in_specs=in_specs, out_specs=out_specs, check_vma=False)
```

```python
import functools

import jax
import jax.numpy as jnp
from jax import lax
from jax.experimental import pallas as pl
from jax.experimental.pallas import tpu as pltpu
from jax.sharding import Mesh
from jax.sharding import PartitionSpec as P

D = 7168
QL = 1536
IHEADS = 64
IDIM = 128
N_SEQ = 16
N_HEAD = 16
NZ = 8
DZ = D // NZ
EPSILON = 1e-06
SEQ = ("x", "yl", "c")
HEAD = ("z", "yh")
HALF = 128
SLOTS = 1024


def swap(values, axis):
    return lax.ppermute(values, axis, [(0, 1), (1, 0)])


def shift(values, axis, size, by):
    return lax.ppermute(values, axis, [(i, (i + by) % size) for i in range(size)])


def kernel_params():
    return pltpu.CompilerParams(vmem_limit_bytes=20 * 1024 * 1024)


def big_params():
    return pltpu.CompilerParams(vmem_limit_bytes=60 * 1024 * 1024)


def project_kernel(place_ref, a_ref, b_ref, res_ref, w_ref, o_ref, half_ref, b_held, o_held, in_sems, out_sems, half_sem):
    head, core = place_ref[0] // 2, place_ref[0] % 2
    own = pl.ds(pl.multiple_of(head // 2 * 16, 16), 16)
    depth = half_ref.shape[0]
    half_copy = pltpu.make_async_copy(
        w_ref.at[pl.ds(pl.multiple_of(core * depth, 16), depth), :], half_ref, half_sem
    )

    def fetch(i):
        columns = pl.ds(pl.multiple_of(i * DZ, 128), DZ)
        return pltpu.make_async_copy(b_ref.at[:, columns], b_held.at[i], in_sems.at[i])

    def store(i):
        return pltpu.make_async_copy(o_held.at[i], o_ref.at[i], out_sems.at[i])

    for i in range(NZ):
        fetch(i).start()
    half_copy.start()

    @pl.loop(0, NZ)
    def _(i):
        columns = pl.ds(pl.multiple_of(i * DZ, 128), DZ)
        fetch(i).wait()
        product = jnp.dot(a_ref[...], b_held[i], preferred_element_type=jnp.float32)
        product = product.astype(o_ref.dtype)
        for group in range(NZ):
            for half in range(2):
                o_held[i, half ^ (head % 2), group * 16 : (group + 1) * 16, :] = product[
                    group * 32 + half * 16 : group * 32 + (half + 1) * 16, :
                ]
        added = o_held[i, 0, own, :].astype(jnp.float32) + res_ref[:, columns].astype(jnp.float32)
        o_held[i, 0, own, :] = added.astype(o_ref.dtype)
        store(i).start()

    for i in range(NZ):
        store(i).wait()
    half_copy.wait()


def project(place, attn_out, out_weight, residual, index_weight):
    rows, depth = attn_out.shape
    whole = pl.BlockSpec(memory_space=pltpu.VMEM)
    apart = pl.BlockSpec(memory_space=pl.ANY)
    shape = (NZ, 2, HALF, DZ)
    return pl.pallas_call(
        project_kernel,
        in_specs=[pl.BlockSpec(memory_space=pltpu.SMEM), whole, apart, whole, apart],
        out_specs=[apart, whole],
        out_shape=[
            jax.ShapeDtypeStruct(shape, jnp.bfloat16),
            jax.ShapeDtypeStruct((QL // 2, index_weight.shape[1]), jnp.bfloat16),
        ],
        scratch_shapes=[
            pltpu.VMEM((NZ, depth, DZ), jnp.bfloat16),
            pltpu.VMEM(shape, jnp.bfloat16),
            pltpu.SemaphoreType.DMA((NZ,)),
            pltpu.SemaphoreType.DMA((NZ,)),
            pltpu.SemaphoreType.DMA,
        ],
        compiler_params=big_params(),
    )(place, attn_out, out_weight, residual, index_weight)


def lift_kernel(core_ref, kept_ref, got_ref, gain_ref, mine_ref, other_ref, o_ref):
    hidden = (kept_ref[...].astype(jnp.float32) + got_ref[...].astype(jnp.float32)).astype(jnp.bfloat16)
    o_ref[:, QL + 128 :] = hidden
    wide = hidden.astype(jnp.float32)
    squares = jnp.sum(wide * wide, axis=1, keepdims=True)
    high = squares.astype(jnp.bfloat16).astype(jnp.float32)
    scaled = wide * gain_ref[...].astype(jnp.float32)
    first, second = scaled[:, : DZ // 2], scaled[:, DZ // 2 :]
    is_first = core_ref[0] == 0
    mine = jnp.where(is_first, first, second).astype(jnp.bfloat16)
    other = jnp.where(is_first, second, first).astype(jnp.bfloat16)
    lifted = jnp.dot(mine, mine_ref[...], preferred_element_type=jnp.float32) + jnp.dot(
        other, other_ref[...], preferred_element_type=jnp.float32
    )
    lane = lax.broadcasted_iota(jnp.int32, (HALF, 128), 1)
    tail = jnp.where(lane == IHEADS, high, jnp.where(lane == IHEADS + 1, squares - high, 0.0))
    o_ref[:, :QL] = lifted[:, :QL].astype(jnp.bfloat16)
    o_ref[:, QL : QL + 128] = jnp.where(lane < IHEADS, lifted[:, QL:], tail).astype(jnp.bfloat16)


def lift(core, kept, got, gain, mine, other):
    whole = pl.BlockSpec(memory_space=pltpu.VMEM)
    return pl.pallas_call(
        lift_kernel,
        in_specs=[pl.BlockSpec(memory_space=pltpu.SMEM)] + [whole] * 5,
        out_specs=whole,
        out_shape=jax.ShapeDtypeStruct((HALF, QL + 128 + DZ), jnp.bfloat16),
        compiler_params=kernel_params(),
    )(core, kept, got, gain, mine, other)


def norm_kernel(high_ref, parts_ref, gain_ref, o_ref, give_ref, hidden_ref):
    total = parts_ref[0, :, : QL + 128].astype(jnp.float32)
    for n in range(1, NZ):
        total = total + parts_ref[n, :, : QL + 128].astype(jnp.float32)
    for n in range(NZ):
        hidden_ref[:, n * DZ : (n + 1) * DZ] = parts_ref[n, :, QL + 128 :]
    mean = (total[:, 1600:1601] + total[:, 1601:1602]) / D
    inverse = lax.rsqrt(mean + EPSILON)
    raw = (total[:, :QL] * inverse).astype(jnp.bfloat16).astype(jnp.float32)
    level = lax.rsqrt(jnp.mean(raw * raw, axis=-1, keepdims=True) + EPSILON)
    latent = (raw * level * gain_ref[...].astype(jnp.float32)).astype(jnp.bfloat16)
    lane = lax.broadcasted_iota(jnp.int32, (16, 128), 1)
    weights = jnp.where(lane < IHEADS, total[:, QL:] * inverse * IHEADS ** (-0.5), 0.0)
    o_ref[:, :QL] = latent
    o_ref[:, QL:] = weights.astype(jnp.bfloat16)
    for block in range(NZ):
        low = latent[:, block * 192 : block * 192 + 96]
        top = latent[:, block * 192 + 96 : block * 192 + 192]
        give_ref[:, block * 96 : (block + 1) * 96] = jnp.where(high_ref[0] == 0, top, low)


def normalize(high, parts, gain):
    whole = pl.BlockSpec(memory_space=pltpu.VMEM)
    return pl.pallas_call(
        norm_kernel,
        in_specs=[pl.BlockSpec(memory_space=pltpu.SMEM), whole, whole],
        out_specs=[whole] * 3,
        out_shape=[
            jax.ShapeDtypeStruct((16, QL + 128), jnp.bfloat16),
            jax.ShapeDtypeStruct((16, QL // 2), jnp.bfloat16),
            jax.ShapeDtypeStruct((16, D), jnp.bfloat16),
        ],
        compiler_params=kernel_params(),
    )(high, parts, gain)


def query_kernel(place_ref, latent_ref, own_ref, mine_ref, theirs_ref, final_ref, beside_ref, o_ref):
    core, high = place_ref[0], place_ref[1]
    is_first = core == 0
    left, right = latent_ref[:, : QL // 2], latent_ref[:, QL // 2 : QL]
    here = jnp.where(is_first, left, right)
    there = jnp.where(is_first, right, left)
    own = jnp.dot(latent_ref[:, :QL], own_ref[...], preferred_element_type=jnp.float32)
    other = jnp.dot(here, mine_ref[...], preferred_element_type=jnp.float32) + jnp.dot(
        there, theirs_ref[...], preferred_element_type=jnp.float32
    )
    for at, part in ((high * 4, own), ((1 - high) * 4, other)):
        part = part.astype(jnp.bfloat16)
        for j in range(4):
            for block in range(NZ):
                o_ref[NZ - 1 - block, at + j] = part[block * 16 : (block + 1) * 16, j * IDIM : (j + 1) * IDIM]
    o_ref[:, 8:] = jnp.zeros((NZ, 2, 16, IDIM), jnp.bfloat16)
    for block in range(NZ):
        low = final_ref[:, block * 192 : block * 192 + 96]
        top = final_ref[:, block * 192 + 96 : block * 192 + 192]
        o_ref[NZ - 1 - block, 8 + high, :, :96] = jnp.where(high == 0, low, top)
        o_ref[NZ - 1 - block, 9 - high, :, :96] = beside_ref[:, block * 96 : (block + 1) * 96]


def make_queries(place, latent, own, mine, theirs, final, beside):
    whole = pl.BlockSpec(memory_space=pltpu.VMEM)
    return pl.pallas_call(
        query_kernel,
        in_specs=[pl.BlockSpec(memory_space=pltpu.SMEM)] + [whole] * 6,
        out_specs=whole,
        out_shape=jax.ShapeDtypeStruct((NZ, 10, 16, IDIM), jnp.bfloat16),
        compiler_params=kernel_params(),
    )(place, latent, own, mine, theirs, final, beside)


def score_kernel(q_ref, w_ref, k_ref, o_ref, wide_ref, rows_ref):
    scale = IDIM ** (-0.5)
    tile = 256

    @pl.when(pl.program_id(0) == 0)
    def _():
        weights = w_ref[...].astype(jnp.float32) * scale
        for j in range(IHEADS):
            wide_ref[j * 16 : (j + 1) * 16, :] = jnp.broadcast_to(weights[:, j : j + 1], (16, 128))
            rows_ref[j * 16 : (j + 1) * 16, :] = q_ref[NZ - 1 - j // 8, j % 8]

    blocks, _, slots = o_ref.shape
    for block in range(blocks):
        for slot in range(0, slots, tile):
            at = block * slots + slot
            logits = lax.dot_general(
                rows_ref[...],
                k_ref[at : at + tile, :],
                (((1,), (1,)), ((), ())),
                preferred_element_type=jnp.float32,
            )
            halves = [jnp.zeros((16, 128), jnp.float32), jnp.zeros((16, 128), jnp.float32)]
            for j in range(IHEADS):
                weight = wide_ref[j * 16 : (j + 1) * 16, :]
                for n in range(2):
                    halves[n] += (
                        jnp.maximum(logits[j * 16 : (j + 1) * 16, n * 128 : (n + 1) * 128], 0.0) * weight
                    )
            for n in range(2):
                o_ref[block, :, slot + n * 128 : slot + (n + 1) * 128] = halves[n].astype(o_ref.dtype)


def make_scores(queries, head_weights, keys):
    per_step = 2
    return pl.pallas_call(
        score_kernel,
        grid=(N_SEQ // per_step,),
        in_specs=[
            pl.BlockSpec(queries.shape, lambda i: (0, 0, 0, 0)),
            pl.BlockSpec((16, 128), lambda i: (0, 0)),
            pl.BlockSpec((per_step * SLOTS, IDIM), lambda i: (i, 0)),
        ],
        out_specs=pl.BlockSpec((per_step, 16, SLOTS), lambda i: (i, 0, 0)),
        out_shape=jax.ShapeDtypeStruct((N_SEQ, 16, SLOTS), jnp.bfloat16),
        scratch_shapes=[
            pltpu.VMEM((IHEADS * 16, 128), jnp.float32),
            pltpu.VMEM((IHEADS * 16, IDIM), jnp.bfloat16),
        ],
        compiler_params=big_params(),
        cost_estimate=pl.CostEstimate(
            flops=4 * IHEADS * 16 * keys.shape[0] * IDIM, bytes_accessed=2 * keys.size * 2, transcendentals=0
        ),
    )(queries, head_weights, keys)


def finish_kernel(numbers_ref, s_ref, pos_ref, o_ref):
    local = lax.broadcasted_iota(jnp.int32, (16, SLOTS), 1)
    filled, base = numbers_ref[0], numbers_ref[1]
    for group in range(N_SEQ):
        here = slice(group * 16, (group + 1) * 16)
        reach = jnp.minimum(filled, pos_ref[here, :] - base + 1)
        o_ref[here, :] = jnp.where(local < reach, s_ref[group].astype(jnp.float32), 0.0)


def finish(numbers, scores, own_positions):
    whole = pl.BlockSpec(memory_space=pltpu.VMEM)
    return pl.pallas_call(
        finish_kernel,
        in_specs=[pl.BlockSpec(memory_space=pltpu.SMEM), whole, whole],
        out_specs=whole,
        out_shape=jax.ShapeDtypeStruct((N_SEQ * 16, SLOTS), jnp.float32),
        compiler_params=kernel_params(),
    )(numbers, scores, own_positions)


def down_weight_rows(latent_weight, index_proj, piece, early):
    share = DZ // N_SEQ

    def own_rows(weight):
        return lax.dynamic_slice_in_dim(weight.reshape(NZ, DZ, weight.shape[1]), piece * share, share, 1)

    own = jnp.concatenate([own_rows(latent_weight), own_rows(index_proj)], axis=2)
    by_head = lax.all_to_all(jnp.repeat(own, 2, axis=0), HEAD, 0, 0).transpose(1, 0, 2)
    local = latent_weight.shape[1]
    wide = jnp.concatenate(
        [
            by_head[:, :, :local].reshape(share, QL),
            by_head[:, :, local:].reshape(share, IHEADS),
            jnp.zeros((share, 64), jnp.bfloat16),
        ],
        axis=1,
    )
    wide, early = lax.optimization_barrier((wide, early))
    half = lax.all_to_all(jnp.broadcast_to(wide[None], (8,) + wide.shape), ("x", "yl"), 0, 0)
    half = half.reshape(8 * share, wide.shape[1])
    return half, swap(half, "c"), early


def turn(values):
    moves = [(s * N_HEAD + h, h * N_HEAD + s) for s in range(N_SEQ) for h in range(N_HEAD)]
    return lax.ppermute(values, SEQ + HEAD, moves)


def shards(
    attn_out,
    out_weight,
    residual,
    norm_gain,
    latent_weight,
    index_proj,
    latent_gain,
    index_weight,
    index_keys,
    positions,
    cache_len,
):
    x, yl, c = (lax.axis_index(a) for a in SEQ)
    z, yh = (lax.axis_index(a) for a in HEAD)
    seq = (x * 2 + yl) * 2 + c
    head = z * 2 + yh
    rows = attn_out.shape[0]
    own = rows // N_HEAD
    local = latent_weight.shape[1]

    partial, half_weight = project(
        jnp.stack([head * 2 + c]).astype(jnp.int32), attn_out, out_weight, residual, index_weight
    )
    summed = lax.psum_scatter(partial, "z", scatter_dimension=0, tiled=False)

    weight_mine = swap(half_weight, "yh")
    down_mine, down_other, weight_mine = down_weight_rows(
        latent_weight, index_proj, c * 8 + x * 2 + yl, weight_mine
    )
    weight_theirs = swap(weight_mine, "c")
    summed, index_keys, down_mine, down_other = lax.optimization_barrier(
        (summed, index_keys, down_mine, down_other)
    )
    all_keys = lax.all_gather(index_keys, SEQ, axis=0, tiled=True)
    kept, got = summed[0], swap(summed[1], "yh")
    gain = lax.dynamic_slice_in_dim(norm_gain, z * DZ, DZ).reshape(1, DZ)
    lifted = lift(jnp.stack([c]).astype(jnp.int32), kept, got, gain, down_mine, down_other)
    lifted, weight_theirs = lax.optimization_barrier((lifted, weight_theirs))
    parts = lax.all_to_all(lifted.reshape(NZ, own, lifted.shape[1]), "z", 0, 0)
    packed, give, hidden_rows = normalize(
        jnp.stack([yh]).astype(jnp.int32), parts, latent_gain.reshape(1, QL)
    )
    turned, beside = lax.optimization_barrier((turn(packed), swap(give, "yh")))
    everyone = lax.all_to_all(jnp.broadcast_to(turned[None, :, :QL], (NZ, own, QL)), "z", 0, 0)
    everyone = everyone.reshape(HALF, QL)
    place = jnp.stack([c, yh]).astype(jnp.int32)
    queries = make_queries(place, everyone, index_weight, weight_mine, weight_theirs, packed, beside)
    queries = lax.all_to_all(queries, "z", 0, 0, axis_index_groups=[list(range(NZ))[::-1]])
    latent_out = queries[::-1, 8:, :, :local].reshape(rows, local)
    scores = make_scores(queries, turned[:, QL:], all_keys)
    scores = lax.all_to_all(scores, SEQ, 0, 0)

    own_positions = lax.dynamic_slice_in_dim(positions, head * rows, rows).reshape(rows, 1)
    numbers = jnp.stack([cache_len[0], seq * SLOTS]).astype(jnp.int32)
    return (hidden_rows, latent_out, finish(numbers, scores, own_positions))


def solution(mesh):
    fine = Mesh(mesh.devices.reshape(4, 2, 2, 8, 2), SEQ + HEAD)
    in_specs = (
        P(SEQ, HEAD),
        P(HEAD, None),
        P(SEQ + HEAD, None),
        P(),
        P(None, HEAD),
        P(None, HEAD),
        P(),
        P(None, HEAD),
        P(SEQ, None),
        P(),
        P(SEQ),
    )
    out_specs = (P(SEQ + HEAD, None), P(SEQ, HEAD), P(HEAD, SEQ))
    return jax.shard_map(shards, mesh=fine, in_specs=in_specs, out_specs=out_specs, check_vma=False)
```

```python
import functools

import jax
import jax.numpy as jnp
from jax import lax
from jax.experimental import pallas as pl
from jax.experimental.pallas import tpu as pltpu
from jax.sharding import Mesh
from jax.sharding import PartitionSpec as P

D = 7168
QL = 1536
IHEADS = 64
IDIM = 128
N_SEQ = 16
N_HEAD = 16
NZ = 8
DZ = D // NZ
EPSILON = 1e-06
SEQ = ("x", "yl", "c")
HEAD = ("z", "yh")
HALF = 128
SLOTS = 1024


def swap(values, axis):
    return lax.ppermute(values, axis, [(0, 1), (1, 0)])


def from_last(values):
    return lax.all_to_all(values, "z", 0, 0, axis_index_groups=[list(range(NZ))[::-1]])


def kernel_params():
    return pltpu.CompilerParams(vmem_limit_bytes=20 * 1024 * 1024)


def big_params():
    return pltpu.CompilerParams(vmem_limit_bytes=60 * 1024 * 1024)


def project_kernel(place_ref, a_ref, b_ref, res_ref, w_ref, o_ref, half_ref, b_held, o_held, in_sems, out_sems, half_sem):
    head, core = place_ref[0] // 2, place_ref[0] % 2
    own = pl.ds(pl.multiple_of((NZ - 1 - head // 2) * 16, 16), 16)
    depth = half_ref.shape[0]
    half_copy = pltpu.make_async_copy(
        w_ref.at[pl.ds(pl.multiple_of(core * depth, 16), depth), :], half_ref, half_sem
    )

    def fetch(i):
        columns = pl.ds(pl.multiple_of(i * DZ, 128), DZ)
        return pltpu.make_async_copy(b_ref.at[:, columns], b_held.at[i], in_sems.at[i])

    def store(i):
        return pltpu.make_async_copy(o_held.at[i], o_ref.at[i], out_sems.at[i])

    for i in range(NZ):
        fetch(i).start()
    half_copy.start()

    @pl.loop(0, NZ)
    def _(i):
        columns = pl.ds(pl.multiple_of(i * DZ, 128), DZ)
        fetch(i).wait()
        product = jnp.dot(a_ref[...], b_held[i], preferred_element_type=jnp.float32)
        product = product.astype(o_ref.dtype)
        for group in range(NZ):
            for half in range(2):
                at = (NZ - 1 - group) * 16
                o_held[i, half ^ (head % 2), at : at + 16, :] = product[
                    group * 32 + half * 16 : group * 32 + (half + 1) * 16, :
                ]
        added = o_held[i, 0, own, :].astype(jnp.float32) + res_ref[:, columns].astype(jnp.float32)
        o_held[i, 0, own, :] = added.astype(o_ref.dtype)
        store(i).start()

    for i in range(NZ):
        store(i).wait()
    half_copy.wait()


def project(place, attn_out, out_weight, residual, index_weight):
    rows, depth = attn_out.shape
    whole = pl.BlockSpec(memory_space=pltpu.VMEM)
    apart = pl.BlockSpec(memory_space=pl.ANY)
    shape = (NZ, 2, HALF, DZ)
    return pl.pallas_call(
        project_kernel,
        in_specs=[pl.BlockSpec(memory_space=pltpu.SMEM), whole, apart, whole, apart],
        out_specs=[apart, whole],
        out_shape=[
            jax.ShapeDtypeStruct(shape, jnp.bfloat16),
            jax.ShapeDtypeStruct((QL // 2, index_weight.shape[1]), jnp.bfloat16),
        ],
        scratch_shapes=[
            pltpu.VMEM((NZ, depth, DZ), jnp.bfloat16),
            pltpu.VMEM(shape, jnp.bfloat16),
            pltpu.SemaphoreType.DMA((NZ,)),
            pltpu.SemaphoreType.DMA((NZ,)),
            pltpu.SemaphoreType.DMA,
        ],
        compiler_params=big_params(),
    )(place, attn_out, out_weight, residual, index_weight)


def lift_kernel(core_ref, kept_ref, got_ref, gain_ref, mine_ref, other_ref, o_ref):
    hidden = (kept_ref[...].astype(jnp.float32) + got_ref[...].astype(jnp.float32)).astype(jnp.bfloat16)
    o_ref[:, QL + 128 :] = hidden
    wide = hidden.astype(jnp.float32)
    squares = jnp.sum(wide * wide, axis=1, keepdims=True)
    high = squares.astype(jnp.bfloat16).astype(jnp.float32)
    scaled = wide * gain_ref[...].astype(jnp.float32)
    first, second = scaled[:, : DZ // 2], scaled[:, DZ // 2 :]
    is_first = core_ref[0] == 0
    mine = jnp.where(is_first, first, second).astype(jnp.bfloat16)
    other = jnp.where(is_first, second, first).astype(jnp.bfloat16)
    lifted = jnp.dot(mine, mine_ref[...], preferred_element_type=jnp.float32) + jnp.dot(
        other, other_ref[...], preferred_element_type=jnp.float32
    )
    lane = lax.broadcasted_iota(jnp.int32, (HALF, 128), 1)
    tail = jnp.where(lane == IHEADS, high, jnp.where(lane == IHEADS + 1, squares - high, 0.0))
    o_ref[:, :QL] = lifted[:, :QL].astype(jnp.bfloat16)
    o_ref[:, QL : QL + 128] = jnp.where(lane < IHEADS, lifted[:, QL:], tail).astype(jnp.bfloat16)


def lift(core, kept, got, gain, mine, other):
    whole = pl.BlockSpec(memory_space=pltpu.VMEM)
    return pl.pallas_call(
        lift_kernel,
        in_specs=[pl.BlockSpec(memory_space=pltpu.SMEM)] + [whole] * 5,
        out_specs=whole,
        out_shape=jax.ShapeDtypeStruct((HALF, QL + 128 + DZ), jnp.bfloat16),
        compiler_params=kernel_params(),
    )(core, kept, got, gain, mine, other)


def norm_kernel(high_ref, parts_ref, gain_ref, o_ref, give_ref, hidden_ref):
    total = parts_ref[0, :, : QL + 128].astype(jnp.float32)
    for n in range(1, NZ):
        total = total + parts_ref[n, :, : QL + 128].astype(jnp.float32)
    for n in range(NZ):
        hidden_ref[:, n * DZ : (n + 1) * DZ] = parts_ref[NZ - 1 - n, :, QL + 128 :]
    mean = (total[:, 1600:1601] + total[:, 1601:1602]) / D
    inverse = lax.rsqrt(mean + EPSILON)
    raw = (total[:, :QL] * inverse).astype(jnp.bfloat16).astype(jnp.float32)
    level = lax.rsqrt(jnp.mean(raw * raw, axis=-1, keepdims=True) + EPSILON)
    latent = (raw * level * gain_ref[...].astype(jnp.float32)).astype(jnp.bfloat16)
    lane = lax.broadcasted_iota(jnp.int32, (16, 128), 1)
    weights = jnp.where(lane < IHEADS, total[:, QL:] * inverse * IHEADS ** (-0.5), 0.0)
    o_ref[:, :QL] = latent
    o_ref[:, QL:] = weights.astype(jnp.bfloat16)
    for block in range(NZ):
        low = latent[:, block * 192 : block * 192 + 96]
        top = latent[:, block * 192 + 96 : block * 192 + 192]
        give_ref[:, block * 96 : (block + 1) * 96] = jnp.where(high_ref[0] == 0, top, low)


def normalize(high, parts, gain):
    whole = pl.BlockSpec(memory_space=pltpu.VMEM)
    return pl.pallas_call(
        norm_kernel,
        in_specs=[pl.BlockSpec(memory_space=pltpu.SMEM), whole, whole],
        out_specs=[whole] * 3,
        out_shape=[
            jax.ShapeDtypeStruct((16, QL + 128), jnp.bfloat16),
            jax.ShapeDtypeStruct((16, QL // 2), jnp.bfloat16),
            jax.ShapeDtypeStruct((16, D), jnp.bfloat16),
        ],
        compiler_params=kernel_params(),
    )(high, parts, gain)


def query_kernel(place_ref, latent_ref, own_ref, mine_ref, theirs_ref, final_ref, beside_ref, o_ref):
    core, high = place_ref[0], place_ref[1]
    is_first = core == 0
    left, right = latent_ref[:, : QL // 2], latent_ref[:, QL // 2 : QL]
    here = jnp.where(is_first, left, right)
    there = jnp.where(is_first, right, left)
    own = jnp.dot(latent_ref[:, :QL], own_ref[...], preferred_element_type=jnp.float32)
    other = jnp.dot(here, mine_ref[...], preferred_element_type=jnp.float32) + jnp.dot(
        there, theirs_ref[...], preferred_element_type=jnp.float32
    )
    for at, part in ((high * 4, own), ((1 - high) * 4, other)):
        part = part.astype(jnp.bfloat16)
        for j in range(4):
            for block in range(NZ):
                o_ref[NZ - 1 - block, at + j] = part[block * 16 : (block + 1) * 16, j * IDIM : (j + 1) * IDIM]
    o_ref[:, 8:] = jnp.zeros((NZ, 2, 16, IDIM), jnp.bfloat16)
    for block in range(NZ):
        low = final_ref[:, block * 192 : block * 192 + 96]
        top = final_ref[:, block * 192 + 96 : block * 192 + 192]
        o_ref[NZ - 1 - block, 8 + high, :, :96] = jnp.where(high == 0, low, top)
        o_ref[NZ - 1 - block, 9 - high, :, :96] = beside_ref[:, block * 96 : (block + 1) * 96]


def make_queries(place, latent, own, mine, theirs, final, beside):
    whole = pl.BlockSpec(memory_space=pltpu.VMEM)
    return pl.pallas_call(
        query_kernel,
        in_specs=[pl.BlockSpec(memory_space=pltpu.SMEM)] + [whole] * 6,
        out_specs=whole,
        out_shape=jax.ShapeDtypeStruct((NZ, 10, 16, IDIM), jnp.bfloat16),
        compiler_params=kernel_params(),
    )(place, latent, own, mine, theirs, final, beside)


def score_kernel(q_ref, w_ref, k_ref, o_ref, wide_ref, rows_ref):
    scale = IDIM ** (-0.5)
    tile = 256

    @pl.when(pl.program_id(0) == 0)
    def _():
        weights = w_ref[...].astype(jnp.float32) * scale
        for j in range(IHEADS):
            wide_ref[j * 16 : (j + 1) * 16, :] = jnp.broadcast_to(weights[:, j : j + 1], (16, 128))
            rows_ref[j * 16 : (j + 1) * 16, :] = q_ref[NZ - 1 - j // 8, j % 8]

    blocks, _, slots = o_ref.shape
    for block in range(blocks):
        for slot in range(0, slots, tile):
            at = block * slots + slot
            logits = lax.dot_general(
                rows_ref[...],
                k_ref[at : at + tile, :],
                (((1,), (1,)), ((), ())),
                preferred_element_type=jnp.float32,
            )
            halves = [jnp.zeros((16, 128), jnp.float32), jnp.zeros((16, 128), jnp.float32)]
            for j in range(IHEADS):
                weight = wide_ref[j * 16 : (j + 1) * 16, :]
                for n in range(2):
                    halves[n] += (
                        jnp.maximum(logits[j * 16 : (j + 1) * 16, n * 128 : (n + 1) * 128], 0.0) * weight
                    )
            for n in range(2):
                o_ref[block, :, slot + n * 128 : slot + (n + 1) * 128] = halves[n].astype(o_ref.dtype)


def make_scores(queries, head_weights, keys):
    per_step = 2
    return pl.pallas_call(
        score_kernel,
        grid=(N_SEQ // per_step,),
        in_specs=[
            pl.BlockSpec(queries.shape, lambda i: (0, 0, 0, 0)),
            pl.BlockSpec((16, 128), lambda i: (0, 0)),
            pl.BlockSpec((per_step * SLOTS, IDIM), lambda i: (i, 0)),
        ],
        out_specs=pl.BlockSpec((per_step, 16, SLOTS), lambda i: (i, 0, 0)),
        out_shape=jax.ShapeDtypeStruct((N_SEQ, 16, SLOTS), jnp.bfloat16),
        scratch_shapes=[
            pltpu.VMEM((IHEADS * 16, 128), jnp.float32),
            pltpu.VMEM((IHEADS * 16, IDIM), jnp.bfloat16),
        ],
        compiler_params=big_params(),
        cost_estimate=pl.CostEstimate(
            flops=4 * IHEADS * 16 * keys.shape[0] * IDIM, bytes_accessed=2 * keys.size * 2, transcendentals=0
        ),
    )(queries, head_weights, keys)


def finish_kernel(numbers_ref, s_ref, pos_ref, o_ref):
    local = lax.broadcasted_iota(jnp.int32, (16, SLOTS), 1)
    filled, base = numbers_ref[0], numbers_ref[1]
    for group in range(N_SEQ):
        here = slice(group * 16, (group + 1) * 16)
        reach = jnp.minimum(filled, pos_ref[here, :] - base + 1)
        o_ref[here, :] = jnp.where(local < reach, s_ref[group].astype(jnp.float32), 0.0)


def finish(numbers, scores, own_positions):
    whole = pl.BlockSpec(memory_space=pltpu.VMEM)
    return pl.pallas_call(
        finish_kernel,
        in_specs=[pl.BlockSpec(memory_space=pltpu.SMEM), whole, whole],
        out_specs=whole,
        out_shape=jax.ShapeDtypeStruct((N_SEQ * 16, SLOTS), jnp.float32),
        compiler_params=kernel_params(),
    )(numbers, scores, own_positions)


def down_weight_rows(latent_weight, index_proj, piece, high, early):
    share = DZ // N_SEQ

    def own_rows(weight):
        return lax.dynamic_slice_in_dim(weight.reshape(NZ, DZ, weight.shape[1]), piece * share, share, 1)

    own = jnp.concatenate([own_rows(latent_weight), own_rows(index_proj)], axis=2)
    mine = lax.all_to_all(own, "z", 0, 0)
    theirs = swap(mine, "yh")
    pair = [jnp.where(high == 0, mine, theirs), jnp.where(high == 0, theirs, mine)]
    by_head = jnp.stack(pair, axis=1).reshape(N_HEAD, share, own.shape[2]).transpose(1, 0, 2)
    local = latent_weight.shape[1]
    wide = jnp.concatenate(
        [
            by_head[:, :, :local].reshape(share, QL),
            by_head[:, :, local:].reshape(share, IHEADS),
            jnp.zeros((share, 64), jnp.bfloat16),
        ],
        axis=1,
    )
    wide, early = lax.optimization_barrier((wide, early))
    half = lax.all_to_all(jnp.broadcast_to(wide[None], (8,) + wide.shape), ("x", "yl"), 0, 0)
    half = half.reshape(8 * share, wide.shape[1])
    return half, swap(half, "c"), early


def turn(values):
    moves = [(s * N_HEAD + h, h * N_HEAD + s) for s in range(N_SEQ) for h in range(N_HEAD)]
    return lax.ppermute(values, SEQ + HEAD, moves)


def shards(
    attn_out,
    out_weight,
    residual,
    norm_gain,
    latent_weight,
    index_proj,
    latent_gain,
    index_weight,
    index_keys,
    positions,
    cache_len,
):
    x, yl, c = (lax.axis_index(a) for a in SEQ)
    z, yh = (lax.axis_index(a) for a in HEAD)
    seq = (x * 2 + yl) * 2 + c
    head = z * 2 + yh
    rows = attn_out.shape[0]
    own = rows // N_HEAD
    local = latent_weight.shape[1]

    partial, half_weight = project(
        jnp.stack([head * 2 + c]).astype(jnp.int32), attn_out, out_weight, residual, index_weight
    )
    summed = lax.psum_scatter(partial, "z", scatter_dimension=0, tiled=False)

    weight_mine = swap(half_weight, "yh")
    down_mine, down_other, weight_mine = down_weight_rows(
        latent_weight, index_proj, c * 8 + x * 2 + yl, yh, weight_mine
    )
    weight_theirs = swap(weight_mine, "c")
    summed, index_keys, down_mine, down_other = lax.optimization_barrier(
        (summed, index_keys, down_mine, down_other)
    )
    all_keys = lax.all_gather(index_keys, SEQ, axis=0, tiled=True)
    kept, got = summed[0], swap(summed[1], "yh")
    gain = lax.dynamic_slice_in_dim(norm_gain, z * DZ, DZ).reshape(1, DZ)
    lifted = lift(jnp.stack([c]).astype(jnp.int32), kept, got, gain, down_mine, down_other)
    lifted, weight_theirs = lax.optimization_barrier((lifted, weight_theirs))
    parts = from_last(lifted.reshape(NZ, own, lifted.shape[1]))
    packed, give, hidden_rows = normalize(
        jnp.stack([yh]).astype(jnp.int32), parts, latent_gain.reshape(1, QL)
    )
    turned, beside = lax.optimization_barrier((turn(packed), swap(give, "yh")))
    everyone = lax.all_to_all(jnp.broadcast_to(turned[None, :, :QL], (NZ, own, QL)), "z", 0, 0)
    everyone = everyone.reshape(HALF, QL)
    place = jnp.stack([c, yh]).astype(jnp.int32)
    queries = make_queries(place, everyone, index_weight, weight_mine, weight_theirs, packed, beside)
    queries = from_last(queries)
    latent_out = queries[::-1, 8:, :, :local].reshape(rows, local)
    scores = make_scores(queries, turned[:, QL:], all_keys)
    scores = lax.all_to_all(scores, SEQ, 0, 0)

    own_positions = lax.dynamic_slice_in_dim(positions, head * rows, rows).reshape(rows, 1)
    numbers = jnp.stack([cache_len[0], seq * SLOTS]).astype(jnp.int32)
    return (hidden_rows, latent_out, finish(numbers, scores, own_positions))


def solution(mesh):
    fine = Mesh(mesh.devices.reshape(4, 2, 2, 8, 2), SEQ + HEAD)
    in_specs = (
        P(SEQ, HEAD),
        P(HEAD, None),
        P(SEQ + HEAD, None),
        P(),
        P(None, HEAD),
        P(None, HEAD),
        P(),
        P(None, HEAD),
        P(SEQ, None),
        P(),
        P(SEQ),
    )
    out_specs = (P(SEQ + HEAD, None), P(SEQ, HEAD), P(HEAD, SEQ))
    return jax.shard_map(shards, mesh=fine, in_specs=in_specs, out_specs=out_specs, check_vma=False)
```

```python
import functools

import jax
import jax.numpy as jnp
from jax import lax
from jax.experimental import pallas as pl
from jax.experimental.pallas import tpu as pltpu
from jax.sharding import Mesh
from jax.sharding import PartitionSpec as P

D = 7168
QL = 1536
IHEADS = 64
IDIM = 128
N_SEQ = 16
N_HEAD = 16
NZ = 8
DZ = D // NZ
EPSILON = 1e-06
SEQ = ("x", "yl", "c")
HEAD = ("z", "yh")
HALF = 128
SLOTS = 1024


def swap(values, axis):
    return lax.ppermute(values, axis, [(0, 1), (1, 0)])


def from_last(values):
    return lax.all_to_all(values, "z", 0, 0, axis_index_groups=[list(range(NZ))[::-1]])


def kernel_params():
    return pltpu.CompilerParams(vmem_limit_bytes=20 * 1024 * 1024)


def big_params():
    return pltpu.CompilerParams(vmem_limit_bytes=60 * 1024 * 1024)


def project_kernel(place_ref, a_ref, b_ref, res_ref, w_ref, o_ref, half_ref, b_held, o_held, in_sems, out_sems, half_sem):
    head, core = place_ref[0] // 2, place_ref[0] % 2
    own = pl.ds(pl.multiple_of((NZ - 1 - head // 2) * 16, 16), 16)
    depth = half_ref.shape[0]
    half_copy = pltpu.make_async_copy(
        w_ref.at[pl.ds(pl.multiple_of(core * depth, 16), depth), :], half_ref, half_sem
    )

    def fetch(i):
        columns = pl.ds(pl.multiple_of(i * DZ, 128), DZ)
        return pltpu.make_async_copy(b_ref.at[:, columns], b_held.at[i], in_sems.at[i])

    def store(i):
        return pltpu.make_async_copy(o_held.at[i], o_ref.at[i], out_sems.at[i])

    for i in range(NZ):
        fetch(i).start()
    half_copy.start()

    @pl.loop(0, NZ)
    def _(i):
        columns = pl.ds(pl.multiple_of(i * DZ, 128), DZ)
        fetch(i).wait()
        product = jnp.dot(a_ref[...], b_held[i], preferred_element_type=jnp.float32)
        product = product.astype(o_ref.dtype)
        for group in range(NZ):
            for half in range(2):
                at = (NZ - 1 - group) * 16
                o_held[i, half ^ (head % 2), at : at + 16, :] = product[
                    group * 32 + half * 16 : group * 32 + (half + 1) * 16, :
                ]
        added = o_held[i, 0, own, :].astype(jnp.float32) + res_ref[:, columns].astype(jnp.float32)
        o_held[i, 0, own, :] = added.astype(o_ref.dtype)
        store(i).start()

    for i in range(NZ):
        store(i).wait()
    half_copy.wait()


def project(place, attn_out, out_weight, residual, index_weight):
    rows, depth = attn_out.shape
    whole = pl.BlockSpec(memory_space=pltpu.VMEM)
    apart = pl.BlockSpec(memory_space=pl.ANY)
    shape = (NZ, 2, HALF, DZ)
    return pl.pallas_call(
        project_kernel,
        in_specs=[pl.BlockSpec(memory_space=pltpu.SMEM), whole, apart, whole, apart],
        out_specs=[apart, whole],
        out_shape=[
            jax.ShapeDtypeStruct(shape, jnp.bfloat16),
            jax.ShapeDtypeStruct((QL // 2, index_weight.shape[1]), jnp.bfloat16),
        ],
        scratch_shapes=[
            pltpu.VMEM((NZ, depth, DZ), jnp.bfloat16),
            pltpu.VMEM(shape, jnp.bfloat16),
            pltpu.SemaphoreType.DMA((NZ,)),
            pltpu.SemaphoreType.DMA((NZ,)),
            pltpu.SemaphoreType.DMA,
        ],
        compiler_params=big_params(),
    )(place, attn_out, out_weight, residual, index_weight)


def lift_kernel(core_ref, kept_ref, got_ref, gain_ref, mine_ref, other_ref, o_ref):
    hidden = (kept_ref[...].astype(jnp.float32) + got_ref[...].astype(jnp.float32)).astype(jnp.bfloat16)
    o_ref[:, QL + 128 :] = hidden
    wide = hidden.astype(jnp.float32)
    squares = jnp.sum(wide * wide, axis=1, keepdims=True)
    high = squares.astype(jnp.bfloat16).astype(jnp.float32)
    scaled = wide * gain_ref[...].astype(jnp.float32)
    first, second = scaled[:, : DZ // 2], scaled[:, DZ // 2 :]
    is_first = core_ref[0] == 0
    mine = jnp.where(is_first, first, second).astype(jnp.bfloat16)
    other = jnp.where(is_first, second, first).astype(jnp.bfloat16)
    lifted = jnp.dot(mine, mine_ref[...], preferred_element_type=jnp.float32) + jnp.dot(
        other, other_ref[...], preferred_element_type=jnp.float32
    )
    lane = lax.broadcasted_iota(jnp.int32, (HALF, 128), 1)
    tail = jnp.where(lane == IHEADS, high, jnp.where(lane == IHEADS + 1, squares - high, 0.0))
    o_ref[:, :QL] = lifted[:, :QL].astype(jnp.bfloat16)
    o_ref[:, QL : QL + 128] = jnp.where(lane < IHEADS, lifted[:, QL:], tail).astype(jnp.bfloat16)


def lift(core, kept, got, gain, mine, other):
    whole = pl.BlockSpec(memory_space=pltpu.VMEM)
    return pl.pallas_call(
        lift_kernel,
        in_specs=[pl.BlockSpec(memory_space=pltpu.SMEM)] + [whole] * 5,
        out_specs=whole,
        out_shape=jax.ShapeDtypeStruct((HALF, QL + 128 + DZ), jnp.bfloat16),
        compiler_params=kernel_params(),
    )(core, kept, got, gain, mine, other)


def norm_kernel(high_ref, parts_ref, gain_ref, o_ref, give_ref, hidden_ref):
    total = parts_ref[0, :, : QL + 128].astype(jnp.float32)
    for n in range(1, NZ):
        total = total + parts_ref[n, :, : QL + 128].astype(jnp.float32)
    for n in range(NZ):
        hidden_ref[:, n * DZ : (n + 1) * DZ] = parts_ref[NZ - 1 - n, :, QL + 128 :]
    mean = (total[:, 1600:1601] + total[:, 1601:1602]) / D
    inverse = lax.rsqrt(mean + EPSILON)
    raw = (total[:, :QL] * inverse).astype(jnp.bfloat16).astype(jnp.float32)
    level = lax.rsqrt(jnp.mean(raw * raw, axis=-1, keepdims=True) + EPSILON)
    latent = (raw * level * gain_ref[...].astype(jnp.float32)).astype(jnp.bfloat16)
    lane = lax.broadcasted_iota(jnp.int32, (16, 128), 1)
    weights = jnp.where(lane < IHEADS, total[:, QL:] * inverse * IHEADS ** (-0.5), 0.0)
    o_ref[:, :QL] = latent
    o_ref[:, QL:] = weights.astype(jnp.bfloat16)
    for block in range(NZ):
        low = latent[:, block * 192 : block * 192 + 96]
        top = latent[:, block * 192 + 96 : block * 192 + 192]
        give_ref[:, block * 96 : (block + 1) * 96] = jnp.where(high_ref[0] == 0, top, low)


def normalize(high, parts, gain):
    whole = pl.BlockSpec(memory_space=pltpu.VMEM)
    return pl.pallas_call(
        norm_kernel,
        in_specs=[pl.BlockSpec(memory_space=pltpu.SMEM), whole, whole],
        out_specs=[whole] * 3,
        out_shape=[
            jax.ShapeDtypeStruct((16, QL + 128), jnp.bfloat16),
            jax.ShapeDtypeStruct((16, QL // 2), jnp.bfloat16),
            jax.ShapeDtypeStruct((16, D), jnp.bfloat16),
        ],
        compiler_params=kernel_params(),
    )(high, parts, gain)


def query_kernel(place_ref, latent_ref, own_ref, mine_ref, theirs_ref, final_ref, beside_ref, o_ref):
    core, high = place_ref[0], place_ref[1]
    is_first = core == 0
    left, right = latent_ref[:, : QL // 2], latent_ref[:, QL // 2 : QL]
    here = jnp.where(is_first, left, right)
    there = jnp.where(is_first, right, left)
    own = jnp.dot(latent_ref[:, :QL], own_ref[...], preferred_element_type=jnp.float32)
    other = jnp.dot(here, mine_ref[...], preferred_element_type=jnp.float32) + jnp.dot(
        there, theirs_ref[...], preferred_element_type=jnp.float32
    )
    for at, part in ((high * 4, own), ((1 - high) * 4, other)):
        part = part.astype(jnp.bfloat16)
        for j in range(4):
            for block in range(NZ):
                o_ref[NZ - 1 - block, at + j] = part[block * 16 : (block + 1) * 16, j * IDIM : (j + 1) * IDIM]
    o_ref[:, 8:] = jnp.zeros((NZ, 2, 16, IDIM), jnp.bfloat16)
    for block in range(NZ):
        low = final_ref[:, block * 192 : block * 192 + 96]
        top = final_ref[:, block * 192 + 96 : block * 192 + 192]
        o_ref[NZ - 1 - block, 8 + high, :, :96] = jnp.where(high == 0, low, top)
        o_ref[NZ - 1 - block, 9 - high, :, :96] = beside_ref[:, block * 96 : (block + 1) * 96]


def make_queries(place, latent, own, mine, theirs, final, beside):
    whole = pl.BlockSpec(memory_space=pltpu.VMEM)
    return pl.pallas_call(
        query_kernel,
        in_specs=[pl.BlockSpec(memory_space=pltpu.SMEM)] + [whole] * 6,
        out_specs=whole,
        out_shape=jax.ShapeDtypeStruct((NZ, 10, 16, IDIM), jnp.bfloat16),
        compiler_params=kernel_params(),
    )(place, latent, own, mine, theirs, final, beside)


def score_kernel(q_ref, w_ref, k_ref, o_ref, wide_ref, rows_ref):
    scale = IDIM ** (-0.5)
    tile = 256

    @pl.when(pl.program_id(0) == 0)
    def _():
        weights = w_ref[...].astype(jnp.float32) * scale
        for j in range(IHEADS):
            wide_ref[j * 16 : (j + 1) * 16, :] = jnp.broadcast_to(weights[:, j : j + 1], (16, 128))
            rows_ref[j * 16 : (j + 1) * 16, :] = q_ref[NZ - 1 - j // 8, j % 8]

    blocks, _, slots = o_ref.shape
    for block in range(blocks):
        for slot in range(0, slots, tile):
            at = block * slots + slot
            logits = lax.dot_general(
                rows_ref[...],
                k_ref[at : at + tile, :],
                (((1,), (1,)), ((), ())),
                preferred_element_type=jnp.float32,
            )
            halves = [jnp.zeros((16, 128), jnp.float32), jnp.zeros((16, 128), jnp.float32)]
            for j in range(IHEADS):
                weight = wide_ref[j * 16 : (j + 1) * 16, :]
                for n in range(2):
                    halves[n] += (
                        jnp.maximum(logits[j * 16 : (j + 1) * 16, n * 128 : (n + 1) * 128], 0.0) * weight
                    )
            for n in range(2):
                o_ref[block, :, slot + n * 128 : slot + (n + 1) * 128] = halves[n].astype(o_ref.dtype)


def make_scores(queries, head_weights, keys):
    per_step = 4
    return pl.pallas_call(
        score_kernel,
        grid=(N_SEQ // per_step,),
        in_specs=[
            pl.BlockSpec(queries.shape, lambda i: (0, 0, 0, 0)),
            pl.BlockSpec((16, 128), lambda i: (0, 0)),
            pl.BlockSpec((per_step * SLOTS, IDIM), lambda i: (i, 0)),
        ],
        out_specs=pl.BlockSpec((per_step, 16, SLOTS), lambda i: (i, 0, 0)),
        out_shape=jax.ShapeDtypeStruct((N_SEQ, 16, SLOTS), jnp.bfloat16),
        scratch_shapes=[
            pltpu.VMEM((IHEADS * 16, 128), jnp.float32),
            pltpu.VMEM((IHEADS * 16, IDIM), jnp.bfloat16),
        ],
        compiler_params=big_params(),
        cost_estimate=pl.CostEstimate(
            flops=4 * IHEADS * 16 * keys.shape[0] * IDIM, bytes_accessed=2 * keys.size * 2, transcendentals=0
        ),
    )(queries, head_weights, keys)


def finish_kernel(numbers_ref, s_ref, pos_ref, o_ref):
    local = lax.broadcasted_iota(jnp.int32, (16, SLOTS), 1)
    filled, base = numbers_ref[0], numbers_ref[1]
    for group in range(N_SEQ):
        here = slice(group * 16, (group + 1) * 16)
        reach = jnp.minimum(filled, pos_ref[here, :] - base + 1)
        o_ref[here, :] = jnp.where(local < reach, s_ref[group].astype(jnp.float32), 0.0)


def finish(numbers, scores, own_positions):
    whole = pl.BlockSpec(memory_space=pltpu.VMEM)
    return pl.pallas_call(
        finish_kernel,
        in_specs=[pl.BlockSpec(memory_space=pltpu.SMEM), whole, whole],
        out_specs=whole,
        out_shape=jax.ShapeDtypeStruct((N_SEQ * 16, SLOTS), jnp.float32),
        compiler_params=kernel_params(),
    )(numbers, scores, own_positions)


def down_weight_rows(latent_weight, index_proj, piece, early):
    share = DZ // N_SEQ

    def own_rows(weight):
        return lax.dynamic_slice_in_dim(weight.reshape(NZ, DZ, weight.shape[1]), piece * share, share, 1)

    own = jnp.concatenate([own_rows(latent_weight), own_rows(index_proj)], axis=2)
    by_head = lax.all_to_all(jnp.repeat(own, 2, axis=0), HEAD, 0, 0).transpose(1, 0, 2)
    local = latent_weight.shape[1]
    wide = jnp.concatenate(
        [
            by_head[:, :, :local].reshape(share, QL),
            by_head[:, :, local:].reshape(share, IHEADS),
            jnp.zeros((share, 64), jnp.bfloat16),
        ],
        axis=1,
    )
    wide, early = lax.optimization_barrier((wide, early))
    half = lax.all_to_all(jnp.broadcast_to(wide[None], (8,) + wide.shape), ("x", "yl"), 0, 0)
    half = half.reshape(8 * share, wide.shape[1])
    return half, swap(half, "c"), early


def turn(values):
    moves = [(s * N_HEAD + h, h * N_HEAD + s) for s in range(N_SEQ) for h in range(N_HEAD)]
    return lax.ppermute(values, SEQ + HEAD, moves)


def shards(
    attn_out,
    out_weight,
    residual,
    norm_gain,
    latent_weight,
    index_proj,
    latent_gain,
    index_weight,
    index_keys,
    positions,
    cache_len,
):
    x, yl, c = (lax.axis_index(a) for a in SEQ)
    z, yh = (lax.axis_index(a) for a in HEAD)
    seq = (x * 2 + yl) * 2 + c
    head = z * 2 + yh
    rows = attn_out.shape[0]
    own = rows // N_HEAD
    local = latent_weight.shape[1]

    partial, half_weight = project(
        jnp.stack([head * 2 + c]).astype(jnp.int32), attn_out, out_weight, residual, index_weight
    )
    summed = lax.psum_scatter(partial, "z", scatter_dimension=0, tiled=False)

    weight_mine = swap(half_weight, "yh")
    down_mine, down_other, weight_mine = down_weight_rows(
        latent_weight, index_proj, c * 8 + x * 2 + yl, weight_mine
    )
    weight_theirs = swap(weight_mine, "c")
    summed, index_keys, down_mine, down_other = lax.optimization_barrier(
        (summed, index_keys, down_mine, down_other)
    )
    all_keys = lax.all_gather(index_keys, SEQ, axis=0, tiled=True)
    kept, got = summed[0], swap(summed[1], "yh")
    gain = lax.dynamic_slice_in_dim(norm_gain, z * DZ, DZ).reshape(1, DZ)
    lifted = lift(jnp.stack([c]).astype(jnp.int32), kept, got, gain, down_mine, down_other)
    lifted, weight_theirs = lax.optimization_barrier((lifted, weight_theirs))
    parts = from_last(lifted.reshape(NZ, own, lifted.shape[1]))
    packed, give, hidden_rows = normalize(
        jnp.stack([yh]).astype(jnp.int32), parts, latent_gain.reshape(1, QL)
    )
    turned, beside = lax.optimization_barrier((turn(packed), swap(give, "yh")))
    everyone = lax.all_to_all(jnp.broadcast_to(turned[None, :, :QL], (NZ, own, QL)), "z", 0, 0)
    everyone = everyone.reshape(HALF, QL)
    place = jnp.stack([c, yh]).astype(jnp.int32)
    queries = make_queries(place, everyone, index_weight, weight_mine, weight_theirs, packed, beside)
    queries = from_last(queries)
    latent_out = queries[::-1, 8:, :, :local].reshape(rows, local)
    scores = make_scores(queries, turned[:, QL:], all_keys)
    scores = lax.all_to_all(scores, SEQ, 0, 0)

    own_positions = lax.dynamic_slice_in_dim(positions, head * rows, rows).reshape(rows, 1)
    numbers = jnp.stack([cache_len[0], seq * SLOTS]).astype(jnp.int32)
    return (hidden_rows, latent_out, finish(numbers, scores, own_positions))


def solution(mesh):
    fine = Mesh(mesh.devices.reshape(4, 2, 2, 8, 2), SEQ + HEAD)
    in_specs = (
        P(SEQ, HEAD),
        P(HEAD, None),
        P(SEQ + HEAD, None),
        P(),
        P(None, HEAD),
        P(None, HEAD),
        P(),
        P(None, HEAD),
        P(SEQ, None),
        P(),
        P(SEQ),
    )
    out_specs = (P(SEQ + HEAD, None), P(SEQ, HEAD), P(HEAD, SEQ))
    return jax.shard_map(shards, mesh=fine, in_specs=in_specs, out_specs=out_specs, check_vma=False)
```

```python
import functools

import jax
import jax.numpy as jnp
from jax import lax
from jax.experimental import pallas as pl
from jax.experimental.pallas import tpu as pltpu
from jax.sharding import Mesh
from jax.sharding import PartitionSpec as P

D = 7168
QL = 1536
IHEADS = 64
IDIM = 128
N_SEQ = 16
N_HEAD = 16
NZ = 8
DZ = D // NZ
EPSILON = 1e-06
SEQ = ("x", "yl", "c")
HEAD = ("z", "yh")
HALF = 128
SLOTS = 1024


def swap(values, axis):
    return lax.ppermute(values, axis, [(0, 1), (1, 0)])


def from_last(values):
    return lax.all_to_all(values, "z", 0, 0, axis_index_groups=[list(range(NZ))[::-1]])


def kernel_params():
    return pltpu.CompilerParams(vmem_limit_bytes=20 * 1024 * 1024)


def big_params():
    return pltpu.CompilerParams(vmem_limit_bytes=60 * 1024 * 1024)


def project_kernel(place_ref, a_ref, b_ref, res_ref, w_ref, o_ref, half_ref, b_held, o_held, in_sems, out_sems, half_sem):
    head, core = place_ref[0] // 2, place_ref[0] % 2
    own = pl.ds(pl.multiple_of((NZ - 1 - head // 2) * 16, 16), 16)
    depth = half_ref.shape[0]
    half_copy = pltpu.make_async_copy(
        w_ref.at[pl.ds(pl.multiple_of(core * depth, 16), depth), :], half_ref, half_sem
    )

    def fetch(i):
        columns = pl.ds(pl.multiple_of(i * DZ, 128), DZ)
        return pltpu.make_async_copy(b_ref.at[:, columns], b_held.at[i], in_sems.at[i])

    def store(i):
        return pltpu.make_async_copy(o_held.at[i], o_ref.at[i], out_sems.at[i])

    for i in range(NZ):
        fetch(i).start()
    half_copy.start()

    @pl.loop(0, NZ)
    def _(i):
        columns = pl.ds(pl.multiple_of(i * DZ, 128), DZ)
        fetch(i).wait()
        product = jnp.dot(a_ref[...], b_held[i], preferred_element_type=jnp.float32)
        product = product.astype(o_ref.dtype)
        for group in range(NZ):
            for half in range(2):
                at = (NZ - 1 - group) * 16
                o_held[i, half ^ (head % 2), at : at + 16, :] = product[
                    group * 32 + half * 16 : group * 32 + (half + 1) * 16, :
                ]
        added = o_held[i, 0, own, :].astype(jnp.float32) + res_ref[:, columns].astype(jnp.float32)
        o_held[i, 0, own, :] = added.astype(o_ref.dtype)
        store(i).start()

    for i in range(NZ):
        store(i).wait()
    half_copy.wait()


def project(place, attn_out, out_weight, residual, index_weight):
    rows, depth = attn_out.shape
    whole = pl.BlockSpec(memory_space=pltpu.VMEM)
    apart = pl.BlockSpec(memory_space=pl.ANY)
    shape = (NZ, 2, HALF, DZ)
    return pl.pallas_call(
        project_kernel,
        in_specs=[pl.BlockSpec(memory_space=pltpu.SMEM), whole, apart, whole, apart],
        out_specs=[apart, whole],
        out_shape=[
            jax.ShapeDtypeStruct(shape, jnp.bfloat16),
            jax.ShapeDtypeStruct((QL // 2, index_weight.shape[1]), jnp.bfloat16),
        ],
        scratch_shapes=[
            pltpu.VMEM((NZ, depth, DZ), jnp.bfloat16),
            pltpu.VMEM(shape, jnp.bfloat16),
            pltpu.SemaphoreType.DMA((NZ,)),
            pltpu.SemaphoreType.DMA((NZ,)),
            pltpu.SemaphoreType.DMA,
        ],
        compiler_params=big_params(),
    )(place, attn_out, out_weight, residual, index_weight)


def lift_kernel(core_ref, kept_ref, got_ref, gain_ref, mine_ref, other_ref, o_ref):
    hidden = (kept_ref[...].astype(jnp.float32) + got_ref[...].astype(jnp.float32)).astype(jnp.bfloat16)
    o_ref[:, QL + 128 :] = hidden
    wide = hidden.astype(jnp.float32)
    squares = jnp.sum(wide * wide, axis=1, keepdims=True)
    high = squares.astype(jnp.bfloat16).astype(jnp.float32)
    scaled = wide * gain_ref[...].astype(jnp.float32)
    first, second = scaled[:, : DZ // 2], scaled[:, DZ // 2 :]
    is_first = core_ref[0] == 0
    mine = jnp.where(is_first, first, second).astype(jnp.bfloat16)
    other = jnp.where(is_first, second, first).astype(jnp.bfloat16)
    lifted = jnp.dot(mine, mine_ref[...], preferred_element_type=jnp.float32) + jnp.dot(
        other, other_ref[...], preferred_element_type=jnp.float32
    )
    lane = lax.broadcasted_iota(jnp.int32, (HALF, 128), 1)
    tail = jnp.where(lane == IHEADS, high, jnp.where(lane == IHEADS + 1, squares - high, 0.0))
    o_ref[:, :QL] = lifted[:, :QL].astype(jnp.bfloat16)
    o_ref[:, QL : QL + 128] = jnp.where(lane < IHEADS, lifted[:, QL:], tail).astype(jnp.bfloat16)


def lift(core, kept, got, gain, mine, other):
    whole = pl.BlockSpec(memory_space=pltpu.VMEM)
    return pl.pallas_call(
        lift_kernel,
        in_specs=[pl.BlockSpec(memory_space=pltpu.SMEM)] + [whole] * 5,
        out_specs=whole,
        out_shape=jax.ShapeDtypeStruct((HALF, QL + 128 + DZ), jnp.bfloat16),
        compiler_params=kernel_params(),
    )(core, kept, got, gain, mine, other)


def norm_kernel(high_ref, parts_ref, gain_ref, o_ref, give_ref, hidden_ref):
    total = parts_ref[0, :, : QL + 128].astype(jnp.float32)
    for n in range(1, NZ):
        total = total + parts_ref[n, :, : QL + 128].astype(jnp.float32)
    for n in range(NZ):
        hidden_ref[:, n * DZ : (n + 1) * DZ] = parts_ref[NZ - 1 - n, :, QL + 128 :]
    mean = (total[:, 1600:1601] + total[:, 1601:1602]) / D
    inverse = lax.rsqrt(mean + EPSILON)
    raw = (total[:, :QL] * inverse).astype(jnp.bfloat16).astype(jnp.float32)
    level = lax.rsqrt(jnp.mean(raw * raw, axis=-1, keepdims=True) + EPSILON)
    latent = (raw * level * gain_ref[...].astype(jnp.float32)).astype(jnp.bfloat16)
    lane = lax.broadcasted_iota(jnp.int32, (16, 128), 1)
    weights = jnp.where(lane < IHEADS, total[:, QL:] * inverse * IHEADS ** (-0.5), 0.0)
    o_ref[:, :QL] = latent
    o_ref[:, QL:] = weights.astype(jnp.bfloat16)
    for block in range(NZ):
        low = latent[:, block * 192 : block * 192 + 96]
        top = latent[:, block * 192 + 96 : block * 192 + 192]
        give_ref[:, block * 96 : (block + 1) * 96] = jnp.where(high_ref[0] == 0, top, low)


def normalize(high, parts, gain):
    whole = pl.BlockSpec(memory_space=pltpu.VMEM)
    return pl.pallas_call(
        norm_kernel,
        in_specs=[pl.BlockSpec(memory_space=pltpu.SMEM), whole, whole],
        out_specs=[whole] * 3,
        out_shape=[
            jax.ShapeDtypeStruct((16, QL + 128), jnp.bfloat16),
            jax.ShapeDtypeStruct((16, QL // 2), jnp.bfloat16),
            jax.ShapeDtypeStruct((16, D), jnp.bfloat16),
        ],
        compiler_params=kernel_params(),
    )(high, parts, gain)


def query_kernel(place_ref, latent_ref, own_ref, mine_ref, theirs_ref, final_ref, beside_ref, o_ref):
    core, high = place_ref[0], place_ref[1]
    is_first = core == 0
    left, right = latent_ref[:, : QL // 2], latent_ref[:, QL // 2 : QL]
    here = jnp.where(is_first, left, right)
    there = jnp.where(is_first, right, left)
    own = jnp.dot(latent_ref[:, :QL], own_ref[...], preferred_element_type=jnp.float32)
    other = jnp.dot(here, mine_ref[...], preferred_element_type=jnp.float32) + jnp.dot(
        there, theirs_ref[...], preferred_element_type=jnp.float32
    )
    for at, part in ((high * 4, own), ((1 - high) * 4, other)):
        part = part.astype(jnp.bfloat16)
        for j in range(4):
            for block in range(NZ):
                o_ref[block, at + j] = part[block * 16 : (block + 1) * 16, j * IDIM : (j + 1) * IDIM]
    o_ref[:, 8:] = jnp.zeros((NZ, 2, 16, IDIM), jnp.bfloat16)
    for block in range(NZ):
        low = final_ref[:, block * 192 : block * 192 + 96]
        top = final_ref[:, block * 192 + 96 : block * 192 + 192]
        o_ref[NZ - 1 - block, 8 + high, :, :96] = jnp.where(high == 0, low, top)
        o_ref[NZ - 1 - block, 9 - high, :, :96] = beside_ref[:, block * 96 : (block + 1) * 96]


def make_queries(place, latent, own, mine, theirs, final, beside):
    whole = pl.BlockSpec(memory_space=pltpu.VMEM)
    return pl.pallas_call(
        query_kernel,
        in_specs=[pl.BlockSpec(memory_space=pltpu.SMEM)] + [whole] * 6,
        out_specs=whole,
        out_shape=jax.ShapeDtypeStruct((NZ, 10, 16, IDIM), jnp.bfloat16),
        compiler_params=kernel_params(),
    )(place, latent, own, mine, theirs, final, beside)


def score_kernel(q_ref, w_ref, k_ref, o_ref, wide_ref, rows_ref):
    scale = IDIM ** (-0.5)
    tile = 256

    @pl.when(pl.program_id(0) == 0)
    def _():
        weights = w_ref[...].astype(jnp.float32) * scale
        for j in range(IHEADS):
            wide_ref[j * 16 : (j + 1) * 16, :] = jnp.broadcast_to(weights[:, j : j + 1], (16, 128))
            rows_ref[j * 16 : (j + 1) * 16, :] = q_ref[NZ - 1 - j // 8, j % 8]

    blocks, _, slots = o_ref.shape
    for block in range(blocks):
        for slot in range(0, slots, tile):
            at = block * slots + slot
            logits = lax.dot_general(
                rows_ref[...],
                k_ref[at : at + tile, :],
                (((1,), (1,)), ((), ())),
                preferred_element_type=jnp.float32,
            )
            halves = [jnp.zeros((16, 128), jnp.float32), jnp.zeros((16, 128), jnp.float32)]
            for j in range(IHEADS):
                weight = wide_ref[j * 16 : (j + 1) * 16, :]
                for n in range(2):
                    halves[n] += (
                        jnp.maximum(logits[j * 16 : (j + 1) * 16, n * 128 : (n + 1) * 128], 0.0) * weight
                    )
            for n in range(2):
                o_ref[blocks - 1 - block, :, slot + n * 128 : slot + (n + 1) * 128] = halves[n].astype(o_ref.dtype)


def make_scores(queries, head_weights, keys):
    per_step = 4
    return pl.pallas_call(
        score_kernel,
        grid=(N_SEQ // per_step,),
        in_specs=[
            pl.BlockSpec(queries.shape, lambda i: (0, 0, 0, 0)),
            pl.BlockSpec((16, 128), lambda i: (0, 0)),
            pl.BlockSpec((per_step * SLOTS, IDIM), lambda i: (i, 0)),
        ],
        out_specs=pl.BlockSpec((per_step, 16, SLOTS), lambda i: (N_SEQ // per_step - 1 - i, 0, 0)),
        out_shape=jax.ShapeDtypeStruct((N_SEQ, 16, SLOTS), jnp.bfloat16),
        scratch_shapes=[
            pltpu.VMEM((IHEADS * 16, 128), jnp.float32),
            pltpu.VMEM((IHEADS * 16, IDIM), jnp.bfloat16),
        ],
        compiler_params=big_params(),
        cost_estimate=pl.CostEstimate(
            flops=4 * IHEADS * 16 * keys.shape[0] * IDIM, bytes_accessed=2 * keys.size * 2, transcendentals=0
        ),
    )(queries, head_weights, keys)


def finish_kernel(numbers_ref, s_ref, pos_ref, o_ref):
    local = lax.broadcasted_iota(jnp.int32, (16, SLOTS), 1)
    filled, base = numbers_ref[0], numbers_ref[1]
    for group in range(N_SEQ):
        here = slice(group * 16, (group + 1) * 16)
        reach = jnp.minimum(filled, pos_ref[here, :] - base + 1)
        o_ref[here, :] = jnp.where(local < reach, s_ref[N_SEQ - 1 - group].astype(jnp.float32), 0.0)


def finish(numbers, scores, own_positions):
    whole = pl.BlockSpec(memory_space=pltpu.VMEM)
    return pl.pallas_call(
        finish_kernel,
        in_specs=[pl.BlockSpec(memory_space=pltpu.SMEM), whole, whole],
        out_specs=whole,
        out_shape=jax.ShapeDtypeStruct((N_SEQ * 16, SLOTS), jnp.float32),
        compiler_params=kernel_params(),
    )(numbers, scores, own_positions)


def down_weight_rows(latent_weight, index_proj, piece, early):
    share = DZ // N_SEQ

    def own_rows(weight):
        return lax.dynamic_slice_in_dim(weight.reshape(NZ, DZ, weight.shape[1]), piece * share, share, 1)

    own = jnp.concatenate([own_rows(latent_weight), own_rows(index_proj)], axis=2)
    by_head = lax.all_to_all(jnp.repeat(own, 2, axis=0), HEAD, 0, 0).transpose(1, 0, 2)
    local = latent_weight.shape[1]
    wide = jnp.concatenate(
        [
            by_head[:, :, :local].reshape(share, QL),
            by_head[:, :, local:].reshape(share, IHEADS),
            jnp.zeros((share, 64), jnp.bfloat16),
        ],
        axis=1,
    )
    wide, early = lax.optimization_barrier((wide, early))
    half = lax.all_to_all(jnp.broadcast_to(wide[None], (8,) + wide.shape), ("x", "yl"), 0, 0)
    half = half.reshape(8 * share, wide.shape[1])
    return half, swap(half, "c"), early


def turn(values):
    moves = [(s * N_HEAD + h, h * N_HEAD + s) for s in range(N_SEQ) for h in range(N_HEAD)]
    return lax.ppermute(values, SEQ + HEAD, moves)


def shards(
    attn_out,
    out_weight,
    residual,
    norm_gain,
    latent_weight,
    index_proj,
    latent_gain,
    index_weight,
    index_keys,
    positions,
    cache_len,
):
    x, yl, c = (lax.axis_index(a) for a in SEQ)
    z, yh = (lax.axis_index(a) for a in HEAD)
    seq = (x * 2 + yl) * 2 + c
    head = z * 2 + yh
    rows = attn_out.shape[0]
    own = rows // N_HEAD
    local = latent_weight.shape[1]

    partial, half_weight = project(
        jnp.stack([head * 2 + c]).astype(jnp.int32), attn_out, out_weight, residual, index_weight
    )
    summed = lax.psum_scatter(partial, "z", scatter_dimension=0, tiled=False)

    weight_mine = swap(half_weight, "yh")
    down_mine, down_other, weight_mine = down_weight_rows(
        latent_weight, index_proj, c * 8 + x * 2 + yl, weight_mine
    )
    weight_theirs = swap(weight_mine, "c")
    summed, index_keys, down_mine, down_other = lax.optimization_barrier(
        (summed, index_keys, down_mine, down_other)
    )
    all_keys = lax.all_gather(index_keys, SEQ, axis=0, tiled=True)
    kept, got = summed[0], swap(summed[1], "yh")
    gain = lax.dynamic_slice_in_dim(norm_gain, z * DZ, DZ).reshape(1, DZ)
    lifted = lift(jnp.stack([c]).astype(jnp.int32), kept, got, gain, down_mine, down_other)
    lifted, weight_theirs = lax.optimization_barrier((lifted, weight_theirs))
    parts = from_last(lifted.reshape(NZ, own, lifted.shape[1]))
    packed, give, hidden_rows = normalize(
        jnp.stack([yh]).astype(jnp.int32), parts, latent_gain.reshape(1, QL)
    )
    turned, beside = lax.optimization_barrier((turn(packed), swap(give, "yh")))
    everyone = from_last(jnp.broadcast_to(turned[None, :, :QL], (NZ, own, QL)))
    everyone = everyone.reshape(HALF, QL)
    place = jnp.stack([c, yh]).astype(jnp.int32)
    queries = make_queries(place, everyone, index_weight, weight_mine, weight_theirs, packed, beside)
    queries = from_last(queries)
    latent_out = queries[::-1, 8:, :, :local].reshape(rows, local)
    scores = make_scores(queries, turned[:, QL:], all_keys)
    scores = lax.all_to_all(scores, SEQ, 0, 0, axis_index_groups=[list(range(N_SEQ))[::-1]])

    own_positions = lax.dynamic_slice_in_dim(positions, head * rows, rows).reshape(rows, 1)
    numbers = jnp.stack([cache_len[0], seq * SLOTS]).astype(jnp.int32)
    return (hidden_rows, latent_out, finish(numbers, scores, own_positions))


def solution(mesh):
    fine = Mesh(mesh.devices.reshape(4, 2, 2, 8, 2), SEQ + HEAD)
    in_specs = (
        P(SEQ, HEAD),
        P(HEAD, None),
        P(SEQ + HEAD, None),
        P(),
        P(None, HEAD),
        P(None, HEAD),
        P(),
        P(None, HEAD),
        P(SEQ, None),
        P(),
        P(SEQ),
    )
    out_specs = (P(SEQ + HEAD, None), P(SEQ, HEAD), P(HEAD, SEQ))
    return jax.shard_map(shards, mesh=fine, in_specs=in_specs, out_specs=out_specs, check_vma=False)
```

```python
import functools

import jax
import jax.numpy as jnp
from jax import lax
from jax.experimental import pallas as pl
from jax.experimental.pallas import tpu as pltpu
from jax.sharding import Mesh
from jax.sharding import PartitionSpec as P

D = 7168
QL = 1536
IHEADS = 64
IDIM = 128
N_SEQ = 16
N_HEAD = 16
NZ = 8
DZ = D // NZ
EPSILON = 1e-06
SEQ = ("x", "yl", "c")
HEAD = ("z", "yh")
HALF = 128
SLOTS = 1024


def swap(values, axis):
    return lax.ppermute(values, axis, [(0, 1), (1, 0)])


def from_last(values):
    return lax.all_to_all(values, "z", 0, 0, axis_index_groups=[list(range(NZ))[::-1]])


def kernel_params():
    return pltpu.CompilerParams(vmem_limit_bytes=20 * 1024 * 1024)


def big_params():
    return pltpu.CompilerParams(vmem_limit_bytes=60 * 1024 * 1024)


def project_kernel(place_ref, a_ref, b_ref, res_ref, w_ref, o_ref, half_ref, b_held, o_held, in_sems, out_sems, half_sem):
    head, core = place_ref[0] // 2, place_ref[0] % 2
    own = pl.ds(pl.multiple_of((NZ - 1 - head // 2) * 16, 16), 16)
    depth = half_ref.shape[0]
    half_copy = pltpu.make_async_copy(
        w_ref.at[pl.ds(pl.multiple_of(core * depth, 16), depth), :], half_ref, half_sem
    )

    def fetch(i):
        columns = pl.ds(pl.multiple_of(i * DZ, 128), DZ)
        return pltpu.make_async_copy(b_ref.at[:, columns], b_held.at[i], in_sems.at[i])

    def store(i):
        return pltpu.make_async_copy(o_held.at[i], o_ref.at[i], out_sems.at[i])

    for i in range(NZ):
        fetch(i).start()
    half_copy.start()

    @pl.loop(0, NZ)
    def _(i):
        columns = pl.ds(pl.multiple_of(i * DZ, 128), DZ)
        fetch(i).wait()
        product = jnp.dot(a_ref[...], b_held[i], preferred_element_type=jnp.float32)
        product = product.astype(o_ref.dtype)
        for group in range(NZ):
            for half in range(2):
                at = (NZ - 1 - group) * 16
                o_held[i, half ^ (head % 2), at : at + 16, :] = product[
                    group * 32 + half * 16 : group * 32 + (half + 1) * 16, :
                ]
        added = o_held[i, 0, own, :].astype(jnp.float32) + res_ref[:, columns].astype(jnp.float32)
        o_held[i, 0, own, :] = added.astype(o_ref.dtype)
        store(i).start()

    for i in range(NZ):
        store(i).wait()
    half_copy.wait()


def project(place, attn_out, out_weight, residual, index_weight):
    rows, depth = attn_out.shape
    whole = pl.BlockSpec(memory_space=pltpu.VMEM)
    apart = pl.BlockSpec(memory_space=pl.ANY)
    shape = (NZ, 2, HALF, DZ)
    return pl.pallas_call(
        project_kernel,
        in_specs=[pl.BlockSpec(memory_space=pltpu.SMEM), whole, apart, whole, apart],
        out_specs=[apart, whole],
        out_shape=[
            jax.ShapeDtypeStruct(shape, jnp.bfloat16),
            jax.ShapeDtypeStruct((QL // 2, index_weight.shape[1]), jnp.bfloat16),
        ],
        scratch_shapes=[
            pltpu.VMEM((NZ, depth, DZ), jnp.bfloat16),
            pltpu.VMEM(shape, jnp.bfloat16),
            pltpu.SemaphoreType.DMA((NZ,)),
            pltpu.SemaphoreType.DMA((NZ,)),
            pltpu.SemaphoreType.DMA,
        ],
        compiler_params=big_params(),
    )(place, attn_out, out_weight, residual, index_weight)


def lift_kernel(core_ref, kept_ref, got_ref, gain_ref, mine_ref, other_ref, hidden_ref, o_ref):
    hidden = (kept_ref[...].astype(jnp.float32) + got_ref[...].astype(jnp.float32)).astype(jnp.bfloat16)
    hidden_ref[...] = hidden
    wide = hidden.astype(jnp.float32)
    squares = jnp.sum(wide * wide, axis=1, keepdims=True)
    high = squares.astype(jnp.bfloat16).astype(jnp.float32)
    scaled = wide * gain_ref[...].astype(jnp.float32)
    first, second = scaled[:, : DZ // 2], scaled[:, DZ // 2 :]
    is_first = core_ref[0] == 0
    mine = jnp.where(is_first, first, second).astype(jnp.bfloat16)
    other = jnp.where(is_first, second, first).astype(jnp.bfloat16)
    lifted = jnp.dot(mine, mine_ref[...], preferred_element_type=jnp.float32) + jnp.dot(
        other, other_ref[...], preferred_element_type=jnp.float32
    )
    lane = lax.broadcasted_iota(jnp.int32, (HALF, 128), 1)
    tail = jnp.where(lane == IHEADS, high, jnp.where(lane == IHEADS + 1, squares - high, 0.0))
    o_ref[:, :QL] = lifted[:, :QL].astype(jnp.bfloat16)
    o_ref[:, QL:] = jnp.where(lane < IHEADS, lifted[:, QL:], tail).astype(jnp.bfloat16)


def lift(core, kept, got, gain, mine, other):
    whole = pl.BlockSpec(memory_space=pltpu.VMEM)
    return pl.pallas_call(
        lift_kernel,
        in_specs=[pl.BlockSpec(memory_space=pltpu.SMEM)] + [whole] * 5,
        out_specs=[whole, whole],
        out_shape=[
            jax.ShapeDtypeStruct((HALF, DZ), jnp.bfloat16),
            jax.ShapeDtypeStruct((HALF, QL + 128), jnp.bfloat16),
        ],
        compiler_params=kernel_params(),
    )(core, kept, got, gain, mine, other)


def norm_kernel(high_ref, parts_ref, gain_ref, o_ref, give_ref):
    total = parts_ref[0].astype(jnp.float32)
    for n in range(1, NZ):
        total = total + parts_ref[n].astype(jnp.float32)
    mean = (total[:, 1600:1601] + total[:, 1601:1602]) / D
    inverse = lax.rsqrt(mean + EPSILON)
    raw = (total[:, :QL] * inverse).astype(jnp.bfloat16).astype(jnp.float32)
    level = lax.rsqrt(jnp.mean(raw * raw, axis=-1, keepdims=True) + EPSILON)
    latent = (raw * level * gain_ref[...].astype(jnp.float32)).astype(jnp.bfloat16)
    lane = lax.broadcasted_iota(jnp.int32, (16, 128), 1)
    weights = jnp.where(lane < IHEADS, total[:, QL:] * inverse * IHEADS ** (-0.5), 0.0)
    o_ref[:, :QL] = latent
    o_ref[:, QL:] = weights.astype(jnp.bfloat16)
    for block in range(NZ):
        low = latent[:, block * 192 : block * 192 + 96]
        top = latent[:, block * 192 + 96 : block * 192 + 192]
        give_ref[:, block * 96 : (block + 1) * 96] = jnp.where(high_ref[0] == 0, top, low)


def normalize(high, parts, gain):
    whole = pl.BlockSpec(memory_space=pltpu.VMEM)
    return pl.pallas_call(
        norm_kernel,
        in_specs=[pl.BlockSpec(memory_space=pltpu.SMEM), whole, whole],
        out_specs=[whole, whole],
        out_shape=[
            jax.ShapeDtypeStruct((16, QL + 128), jnp.bfloat16),
            jax.ShapeDtypeStruct((16, QL // 2), jnp.bfloat16),
        ],
        compiler_params=kernel_params(),
    )(high, parts, gain)


def query_kernel(place_ref, latent_ref, own_ref, mine_ref, theirs_ref, final_ref, beside_ref, o_ref):
    core, high = place_ref[0], place_ref[1]
    is_first = core == 0
    left, right = latent_ref[:, : QL // 2], latent_ref[:, QL // 2 : QL]
    here = jnp.where(is_first, left, right)
    there = jnp.where(is_first, right, left)
    own = jnp.dot(latent_ref[:, :QL], own_ref[...], preferred_element_type=jnp.float32)
    other = jnp.dot(here, mine_ref[...], preferred_element_type=jnp.float32) + jnp.dot(
        there, theirs_ref[...], preferred_element_type=jnp.float32
    )
    for at, part in ((high * 4, own), ((1 - high) * 4, other)):
        part = part.astype(jnp.bfloat16)
        for j in range(4):
            for block in range(NZ):
                o_ref[block, at + j] = part[block * 16 : (block + 1) * 16, j * IDIM : (j + 1) * IDIM]
    o_ref[:, 8:] = jnp.zeros((NZ, 2, 16, IDIM), jnp.bfloat16)
    for block in range(NZ):
        low = final_ref[:, block * 192 : block * 192 + 96]
        top = final_ref[:, block * 192 + 96 : block * 192 + 192]
        o_ref[NZ - 1 - block, 8 + high, :, :96] = jnp.where(high == 0, low, top)
        o_ref[NZ - 1 - block, 9 - high, :, :96] = beside_ref[:, block * 96 : (block + 1) * 96]


def make_queries(place, latent, own, mine, theirs, final, beside):
    whole = pl.BlockSpec(memory_space=pltpu.VMEM)
    return pl.pallas_call(
        query_kernel,
        in_specs=[pl.BlockSpec(memory_space=pltpu.SMEM)] + [whole] * 6,
        out_specs=whole,
        out_shape=jax.ShapeDtypeStruct((NZ, 10, 16, IDIM), jnp.bfloat16),
        compiler_params=kernel_params(),
    )(place, latent, own, mine, theirs, final, beside)


def score_kernel(q_ref, w_ref, k_ref, o_ref, wide_ref, rows_ref):
    scale = IDIM ** (-0.5)
    tile = 256

    @pl.when(pl.program_id(0) == 0)
    def _():
        weights = w_ref[...].astype(jnp.float32) * scale
        for j in range(IHEADS):
            wide_ref[j * 16 : (j + 1) * 16, :] = jnp.broadcast_to(weights[:, j : j + 1], (16, 128))
            rows_ref[j * 16 : (j + 1) * 16, :] = q_ref[NZ - 1 - j // 8, j % 8]

    blocks, _, slots = o_ref.shape
    for block in range(blocks):
        for slot in range(0, slots, tile):
            at = block * slots + slot
            logits = lax.dot_general(
                rows_ref[...],
                k_ref[at : at + tile, :],
                (((1,), (1,)), ((), ())),
                preferred_element_type=jnp.float32,
            )
            halves = [jnp.zeros((16, 128), jnp.float32), jnp.zeros((16, 128), jnp.float32)]
            for j in range(IHEADS):
                weight = wide_ref[j * 16 : (j + 1) * 16, :]
                for n in range(2):
                    halves[n] += (
                        jnp.maximum(logits[j * 16 : (j + 1) * 16, n * 128 : (n + 1) * 128], 0.0) * weight
                    )
            for n in range(2):
                o_ref[blocks - 1 - block, :, slot + n * 128 : slot + (n + 1) * 128] = halves[n].astype(o_ref.dtype)


def make_scores(queries, head_weights, keys):
    per_step = 4
    return pl.pallas_call(
        score_kernel,
        grid=(N_SEQ // per_step,),
        in_specs=[
            pl.BlockSpec(queries.shape, lambda i: (0, 0, 0, 0)),
            pl.BlockSpec((16, 128), lambda i: (0, 0)),
            pl.BlockSpec((per_step * SLOTS, IDIM), lambda i: (i, 0)),
        ],
        out_specs=pl.BlockSpec((per_step, 16, SLOTS), lambda i: (N_SEQ // per_step - 1 - i, 0, 0)),
        out_shape=jax.ShapeDtypeStruct((N_SEQ, 16, SLOTS), jnp.bfloat16),
        scratch_shapes=[
            pltpu.VMEM((IHEADS * 16, 128), jnp.float32),
            pltpu.VMEM((IHEADS * 16, IDIM), jnp.bfloat16),
        ],
        compiler_params=big_params(),
        cost_estimate=pl.CostEstimate(
            flops=4 * IHEADS * 16 * keys.shape[0] * IDIM, bytes_accessed=2 * keys.size * 2, transcendentals=0
        ),
    )(queries, head_weights, keys)


def finish_kernel(numbers_ref, s_ref, pos_ref, o_ref):
    groups = s_ref.shape[0]
    local = lax.broadcasted_iota(jnp.int32, (16, SLOTS), 1)
    filled, base = numbers_ref[0], numbers_ref[1]
    for group in range(groups):
        here = slice(group * 16, (group + 1) * 16)
        reach = jnp.minimum(filled, pos_ref[here, :] - base + 1)
        o_ref[here, :] = jnp.where(local < reach, s_ref[groups - 1 - group].astype(jnp.float32), 0.0)


def finish(numbers, scores, own_positions):
    steps = 4
    groups = N_SEQ // steps
    return pl.pallas_call(
        finish_kernel,
        grid=(steps,),
        in_specs=[
            pl.BlockSpec(memory_space=pltpu.SMEM),
            pl.BlockSpec((groups, 16, SLOTS), lambda i: (steps - 1 - i, 0, 0)),
            pl.BlockSpec((groups * 16, 1), lambda i: (i, 0)),
        ],
        out_specs=pl.BlockSpec((groups * 16, SLOTS), lambda i: (i, 0)),
        out_shape=jax.ShapeDtypeStruct((N_SEQ * 16, SLOTS), jnp.float32),
        compiler_params=kernel_params(),
    )(numbers, scores, own_positions)


def down_weight_rows(latent_weight, index_proj, piece, early):
    share = DZ // N_SEQ

    def own_rows(weight):
        return lax.dynamic_slice_in_dim(weight.reshape(NZ, DZ, weight.shape[1]), piece * share, share, 1)

    own = jnp.concatenate([own_rows(latent_weight), own_rows(index_proj)], axis=2)
    by_head = lax.all_to_all(jnp.repeat(own, 2, axis=0), HEAD, 0, 0).transpose(1, 0, 2)
    local = latent_weight.shape[1]
    wide = jnp.concatenate(
        [
            by_head[:, :, :local].reshape(share, QL),
            by_head[:, :, local:].reshape(share, IHEADS),
            jnp.zeros((share, 64), jnp.bfloat16),
        ],
        axis=1,
    )
    wide, early = lax.optimization_barrier((wide, early))
    half = lax.all_to_all(jnp.broadcast_to(wide[None], (8,) + wide.shape), ("x", "yl"), 0, 0)
    half = half.reshape(8 * share, wide.shape[1])
    return half, swap(half, "c"), early


def turn(values):
    moves = [(s * N_HEAD + h, h * N_HEAD + s) for s in range(N_SEQ) for h in range(N_HEAD)]
    return lax.ppermute(values, SEQ + HEAD, moves)


def shards(
    attn_out,
    out_weight,
    residual,
    norm_gain,
    latent_weight,
    index_proj,
    latent_gain,
    index_weight,
    index_keys,
    positions,
    cache_len,
):
    x, yl, c = (lax.axis_index(a) for a in SEQ)
    z, yh = (lax.axis_index(a) for a in HEAD)
    seq = (x * 2 + yl) * 2 + c
    head = z * 2 + yh
    rows = attn_out.shape[0]
    own = rows // N_HEAD
    local = latent_weight.shape[1]

    partial, half_weight = project(
        jnp.stack([head * 2 + c]).astype(jnp.int32), attn_out, out_weight, residual, index_weight
    )
    summed = lax.psum_scatter(partial, "z", scatter_dimension=0, tiled=False)

    weight_mine = swap(half_weight, "yh")
    down_mine, down_other, weight_mine = down_weight_rows(
        latent_weight, index_proj, c * 8 + x * 2 + yl, weight_mine
    )
    weight_theirs = swap(weight_mine, "c")
    summed, index_keys, down_mine, down_other = lax.optimization_barrier(
        (summed, index_keys, down_mine, down_other)
    )
    all_keys = lax.all_gather(index_keys, SEQ, axis=0, tiled=True)
    kept, got = summed[0], swap(summed[1], "yh")
    gain = lax.dynamic_slice_in_dim(norm_gain, z * DZ, DZ).reshape(1, DZ)
    hidden, lifted = lift(jnp.stack([c]).astype(jnp.int32), kept, got, gain, down_mine, down_other)
    lifted, weight_theirs = lax.optimization_barrier((lifted, weight_theirs))
    parts = from_last(lifted.reshape(NZ, own, lifted.shape[1]))
    packed, give = normalize(
        jnp.stack([yh]).astype(jnp.int32), parts, latent_gain.reshape(1, QL)
    )
    packed, hidden = lax.optimization_barrier((packed, hidden))
    hidden_cols = from_last(hidden.reshape(NZ, own, DZ))
    turned, beside = lax.optimization_barrier((turn(packed), swap(give, "yh")))
    everyone = from_last(jnp.broadcast_to(turned[None, :, :QL], (NZ, own, QL)))
    everyone, hidden_cols = lax.optimization_barrier((everyone.reshape(HALF, QL), hidden_cols))
    hidden_rows = hidden_cols[::-1].transpose(1, 0, 2).reshape(own, D)
    place = jnp.stack([c, yh]).astype(jnp.int32)
    queries = make_queries(place, everyone, index_weight, weight_mine, weight_theirs, packed, beside)
    queries = from_last(queries)
    latent_out = queries[::-1, 8:, :, :local].reshape(rows, local)
    scores = make_scores(queries, turned[:, QL:], all_keys)
    scores = lax.all_to_all(scores, SEQ, 0, 0, axis_index_groups=[list(range(N_SEQ))[::-1]])

    own_positions = lax.dynamic_slice_in_dim(positions, head * rows, rows).reshape(rows, 1)
    numbers = jnp.stack([cache_len[0], seq * SLOTS]).astype(jnp.int32)
    return (hidden_rows, latent_out, finish(numbers, scores, own_positions))


def solution(mesh):
    fine = Mesh(mesh.devices.reshape(4, 2, 2, 8, 2), SEQ + HEAD)
    in_specs = (
        P(SEQ, HEAD),
        P(HEAD, None),
        P(SEQ + HEAD, None),
        P(),
        P(None, HEAD),
        P(None, HEAD),
        P(),
        P(None, HEAD),
        P(SEQ, None),
        P(),
        P(SEQ),
    )
    out_specs = (P(SEQ + HEAD, None), P(SEQ, HEAD), P(HEAD, SEQ))
    return jax.shard_map(shards, mesh=fine, in_specs=in_specs, out_specs=out_specs, check_vma=False)
```

```python
import functools

import jax
import jax.numpy as jnp
from jax import lax
from jax.experimental import pallas as pl
from jax.experimental.pallas import tpu as pltpu
from jax.sharding import Mesh
from jax.sharding import PartitionSpec as P

D = 7168
QL = 1536
IHEADS = 64
IDIM = 128
N_SEQ = 16
N_HEAD = 16
NZ = 8
DZ = D // NZ
EPSILON = 1e-06
SEQ = ("x", "yl", "c")
HEAD = ("z", "yh")
HALF = 128
SLOTS = 1024


def swap(values, axis):
    return lax.ppermute(values, axis, [(0, 1), (1, 0)])


def from_last(values):
    return lax.all_to_all(values, "z", 0, 0, axis_index_groups=[list(range(NZ))[::-1]])


def kernel_params():
    return pltpu.CompilerParams(vmem_limit_bytes=20 * 1024 * 1024)


def big_params():
    return pltpu.CompilerParams(vmem_limit_bytes=60 * 1024 * 1024)


def project_kernel(place_ref, a_ref, b_ref, res_ref, w_ref, o_ref, half_ref, b_held, o_held, in_sems, out_sems, half_sem):
    head, core = place_ref[0] // 2, place_ref[0] % 2
    own = pl.ds(pl.multiple_of((NZ - 1 - head // 2) * 16, 16), 16)
    depth = half_ref.shape[0]
    half_copy = pltpu.make_async_copy(
        w_ref.at[pl.ds(pl.multiple_of(core * depth, 16), depth), :], half_ref, half_sem
    )

    def fetch(i):
        columns = pl.ds(pl.multiple_of(i * DZ, 128), DZ)
        return pltpu.make_async_copy(b_ref.at[:, columns], b_held.at[i], in_sems.at[i])

    def store(i):
        return pltpu.make_async_copy(o_held.at[i], o_ref.at[i], out_sems.at[i])

    for i in range(NZ):
        fetch(i).start()
    half_copy.start()

    @pl.loop(0, NZ)
    def _(i):
        columns = pl.ds(pl.multiple_of(i * DZ, 128), DZ)
        fetch(i).wait()
        product = jnp.dot(a_ref[...], b_held[i], preferred_element_type=jnp.float32)
        product = product.astype(o_ref.dtype)
        for group in range(NZ):
            for half in range(2):
                at = (NZ - 1 - group) * 16
                o_held[i, half ^ (head % 2), at : at + 16, :] = product[
                    group * 32 + half * 16 : group * 32 + (half + 1) * 16, :
                ]
        added = o_held[i, 0, own, :].astype(jnp.float32) + res_ref[:, columns].astype(jnp.float32)
        o_held[i, 0, own, :] = added.astype(o_ref.dtype)
        store(i).start()

    for i in range(NZ):
        store(i).wait()
    half_copy.wait()


def project(place, attn_out, out_weight, residual, index_weight):
    rows, depth = attn_out.shape
    whole = pl.BlockSpec(memory_space=pltpu.VMEM)
    apart = pl.BlockSpec(memory_space=pl.ANY)
    shape = (NZ, 2, HALF, DZ)
    return pl.pallas_call(
        project_kernel,
        in_specs=[pl.BlockSpec(memory_space=pltpu.SMEM), whole, apart, whole, apart],
        out_specs=[apart, whole],
        out_shape=[
            jax.ShapeDtypeStruct(shape, jnp.bfloat16),
            jax.ShapeDtypeStruct((QL // 2, index_weight.shape[1]), jnp.bfloat16),
        ],
        scratch_shapes=[
            pltpu.VMEM((NZ, depth, DZ), jnp.bfloat16),
            pltpu.VMEM(shape, jnp.bfloat16),
            pltpu.SemaphoreType.DMA((NZ,)),
            pltpu.SemaphoreType.DMA((NZ,)),
            pltpu.SemaphoreType.DMA,
        ],
        compiler_params=big_params(),
    )(place, attn_out, out_weight, residual, index_weight)


def lift_kernel(core_ref, kept_ref, got_ref, gain_ref, mine_ref, other_ref, hidden_ref, o_ref):
    hidden = (kept_ref[...].astype(jnp.float32) + got_ref[...].astype(jnp.float32)).astype(jnp.bfloat16)
    hidden_ref[...] = hidden
    wide = hidden.astype(jnp.float32)
    squares = jnp.sum(wide * wide, axis=1, keepdims=True)
    high = squares.astype(jnp.bfloat16).astype(jnp.float32)
    scaled = wide * gain_ref[...].astype(jnp.float32)
    first, second = scaled[:, : DZ // 2], scaled[:, DZ // 2 :]
    is_first = core_ref[0] == 0
    mine = jnp.where(is_first, first, second).astype(jnp.bfloat16)
    other = jnp.where(is_first, second, first).astype(jnp.bfloat16)
    lifted = jnp.dot(mine, mine_ref[...], preferred_element_type=jnp.float32) + jnp.dot(
        other, other_ref[...], preferred_element_type=jnp.float32
    )
    lane = lax.broadcasted_iota(jnp.int32, (HALF, 128), 1)
    tail = jnp.where(lane == IHEADS, high, jnp.where(lane == IHEADS + 1, squares - high, 0.0))
    o_ref[:, :QL] = lifted[:, :QL].astype(jnp.bfloat16)
    o_ref[:, QL:] = jnp.where(lane < IHEADS, lifted[:, QL:], tail).astype(jnp.bfloat16)


def lift(core, kept, got, gain, mine, other):
    whole = pl.BlockSpec(memory_space=pltpu.VMEM)
    return pl.pallas_call(
        lift_kernel,
        in_specs=[pl.BlockSpec(memory_space=pltpu.SMEM)] + [whole] * 5,
        out_specs=[whole, whole],
        out_shape=[
            jax.ShapeDtypeStruct((HALF, DZ), jnp.bfloat16),
            jax.ShapeDtypeStruct((HALF, QL + 128), jnp.bfloat16),
        ],
        compiler_params=kernel_params(),
    )(core, kept, got, gain, mine, other)


def norm_kernel(high_ref, parts_ref, gain_ref, o_ref, give_ref):
    total = parts_ref[0].astype(jnp.float32)
    for n in range(1, NZ):
        total = total + parts_ref[n].astype(jnp.float32)
    mean = (total[:, 1600:1601] + total[:, 1601:1602]) / D
    inverse = lax.rsqrt(mean + EPSILON)
    raw = (total[:, :QL] * inverse).astype(jnp.bfloat16).astype(jnp.float32)
    level = lax.rsqrt(jnp.mean(raw * raw, axis=-1, keepdims=True) + EPSILON)
    latent = (raw * level * gain_ref[...].astype(jnp.float32)).astype(jnp.bfloat16)
    lane = lax.broadcasted_iota(jnp.int32, (16, 128), 1)
    weights = jnp.where(lane < IHEADS, total[:, QL:] * inverse * IHEADS ** (-0.5), 0.0)
    o_ref[:, :QL] = latent
    o_ref[:, QL:] = weights.astype(jnp.bfloat16)
    for block in range(NZ):
        low = latent[:, block * 192 : block * 192 + 96]
        top = latent[:, block * 192 + 96 : block * 192 + 192]
        give_ref[:, block * 96 : (block + 1) * 96] = jnp.where(high_ref[0] == 0, top, low)


def normalize(high, parts, gain):
    whole = pl.BlockSpec(memory_space=pltpu.VMEM)
    return pl.pallas_call(
        norm_kernel,
        in_specs=[pl.BlockSpec(memory_space=pltpu.SMEM), whole, whole],
        out_specs=[whole, whole],
        out_shape=[
            jax.ShapeDtypeStruct((16, QL + 128), jnp.bfloat16),
            jax.ShapeDtypeStruct((16, QL // 2), jnp.bfloat16),
        ],
        compiler_params=kernel_params(),
    )(high, parts, gain)


def query_kernel(place_ref, latent_ref, own_ref, mine_ref, theirs_ref, final_ref, beside_ref, o_ref):
    core, high = place_ref[0], place_ref[1]
    is_first = core == 0
    left, right = latent_ref[:, : QL // 2], latent_ref[:, QL // 2 : QL]
    here = jnp.where(is_first, left, right)
    there = jnp.where(is_first, right, left)
    own = jnp.dot(latent_ref[:, :QL], own_ref[...], preferred_element_type=jnp.float32)
    other = jnp.dot(here, mine_ref[...], preferred_element_type=jnp.float32) + jnp.dot(
        there, theirs_ref[...], preferred_element_type=jnp.float32
    )
    for at, part in ((high * 4, own), ((1 - high) * 4, other)):
        part = part.astype(jnp.bfloat16)
        for j in range(4):
            for block in range(NZ):
                o_ref[block, at + j] = part[block * 16 : (block + 1) * 16, j * IDIM : (j + 1) * IDIM]
    o_ref[:, 8:] = jnp.zeros((NZ, 2, 16, IDIM), jnp.bfloat16)
    for block in range(NZ):
        low = final_ref[:, block * 192 : block * 192 + 96]
        top = final_ref[:, block * 192 + 96 : block * 192 + 192]
        o_ref[NZ - 1 - block, 8 + high, :, :96] = jnp.where(high == 0, low, top)
        o_ref[NZ - 1 - block, 9 - high, :, :96] = beside_ref[:, block * 96 : (block + 1) * 96]


def make_queries(place, latent, own, mine, theirs, final, beside):
    whole = pl.BlockSpec(memory_space=pltpu.VMEM)
    return pl.pallas_call(
        query_kernel,
        in_specs=[pl.BlockSpec(memory_space=pltpu.SMEM)] + [whole] * 6,
        out_specs=whole,
        out_shape=jax.ShapeDtypeStruct((NZ, 10, 16, IDIM), jnp.bfloat16),
        compiler_params=kernel_params(),
    )(place, latent, own, mine, theirs, final, beside)


def score_kernel(q_ref, w_ref, k_ref, o_ref, wide_ref, rows_ref):
    scale = IDIM ** (-0.5)
    tile = 256

    @pl.when(pl.program_id(0) == 0)
    def _():
        weights = w_ref[...].astype(jnp.float32) * scale
        for j in range(IHEADS):
            wide_ref[j * 16 : (j + 1) * 16, :] = jnp.broadcast_to(weights[:, j : j + 1], (16, 128))
            rows_ref[j * 16 : (j + 1) * 16, :] = q_ref[NZ - 1 - j // 8, j % 8]

    blocks, _, slots = o_ref.shape
    for block in range(blocks):
        for slot in range(0, slots, tile):
            at = block * slots + slot
            logits = lax.dot_general(
                rows_ref[...],
                k_ref[at : at + tile, :],
                (((1,), (1,)), ((), ())),
                preferred_element_type=jnp.float32,
            )
            halves = [jnp.zeros((16, 128), jnp.float32), jnp.zeros((16, 128), jnp.float32)]
            for j in range(IHEADS):
                weight = wide_ref[j * 16 : (j + 1) * 16, :]
                for n in range(2):
                    halves[n] += (
                        jnp.maximum(logits[j * 16 : (j + 1) * 16, n * 128 : (n + 1) * 128], 0.0) * weight
                    )
            for n in range(2):
                o_ref[blocks - 1 - block, :, slot + n * 128 : slot + (n + 1) * 128] = halves[n].astype(o_ref.dtype)


def make_scores(queries, head_weights, keys):
    per_step = 4
    return pl.pallas_call(
        score_kernel,
        grid=(N_SEQ // per_step,),
        in_specs=[
            pl.BlockSpec(queries.shape, lambda i: (0, 0, 0, 0)),
            pl.BlockSpec((16, 128), lambda i: (0, 0)),
            pl.BlockSpec((per_step * SLOTS, IDIM), lambda i: (i, 0)),
        ],
        out_specs=pl.BlockSpec((per_step, 16, SLOTS), lambda i: (N_SEQ // per_step - 1 - i, 0, 0)),
        out_shape=jax.ShapeDtypeStruct((N_SEQ, 16, SLOTS), jnp.bfloat16),
        scratch_shapes=[
            pltpu.VMEM((IHEADS * 16, 128), jnp.float32),
            pltpu.VMEM((IHEADS * 16, IDIM), jnp.bfloat16),
        ],
        compiler_params=big_params(),
        cost_estimate=pl.CostEstimate(
            flops=4 * IHEADS * 16 * keys.shape[0] * IDIM, bytes_accessed=2 * keys.size * 2, transcendentals=0
        ),
    )(queries, head_weights, keys)


def finish_kernel(numbers_ref, s_ref, pos_ref, o_ref):
    local = lax.broadcasted_iota(jnp.int32, (16, SLOTS), 1)
    filled, base = numbers_ref[0], numbers_ref[1]
    for group in range(N_SEQ):
        here = slice(group * 16, (group + 1) * 16)
        reach = jnp.minimum(filled, pos_ref[here, :] - base + 1)
        o_ref[here, :] = jnp.where(local < reach, s_ref[N_SEQ - 1 - group].astype(jnp.float32), 0.0)


def finish(numbers, scores, own_positions):
    whole = pl.BlockSpec(memory_space=pltpu.VMEM)
    return pl.pallas_call(
        finish_kernel,
        in_specs=[pl.BlockSpec(memory_space=pltpu.SMEM), whole, whole],
        out_specs=whole,
        out_shape=jax.ShapeDtypeStruct((N_SEQ * 16, SLOTS), jnp.float32),
        compiler_params=kernel_params(),
    )(numbers, scores, own_positions)


def down_weight_rows(latent_weight, index_proj, piece, early):
    share = DZ // N_SEQ

    def own_rows(weight):
        return lax.dynamic_slice_in_dim(weight.reshape(NZ, DZ, weight.shape[1]), piece * share, share, 1)

    own = jnp.concatenate([own_rows(latent_weight), own_rows(index_proj)], axis=2)
    by_head = lax.all_to_all(jnp.repeat(own, 2, axis=0), HEAD, 0, 0).transpose(1, 0, 2)
    local = latent_weight.shape[1]
    wide = jnp.concatenate(
        [
            by_head[:, :, :local].reshape(share, QL),
            by_head[:, :, local:].reshape(share, IHEADS),
            jnp.zeros((share, 64), jnp.bfloat16),
        ],
        axis=1,
    )
    wide, early = lax.optimization_barrier((wide, early))
    half = lax.all_to_all(jnp.broadcast_to(wide[None], (8,) + wide.shape), ("x", "yl"), 0, 0)
    half = half.reshape(8 * share, wide.shape[1])
    return half, swap(half, "c"), early


def turn(values):
    moves = [(s * N_HEAD + h, h * N_HEAD + s) for s in range(N_SEQ) for h in range(N_HEAD)]
    return lax.ppermute(values, SEQ + HEAD, moves)


def shards(
    attn_out,
    out_weight,
    residual,
    norm_gain,
    latent_weight,
    index_proj,
    latent_gain,
    index_weight,
    index_keys,
    positions,
    cache_len,
):
    x, yl, c = (lax.axis_index(a) for a in SEQ)
    z, yh = (lax.axis_index(a) for a in HEAD)
    seq = (x * 2 + yl) * 2 + c
    head = z * 2 + yh
    rows = attn_out.shape[0]
    own = rows // N_HEAD
    local = latent_weight.shape[1]

    partial, half_weight = project(
        jnp.stack([head * 2 + c]).astype(jnp.int32), attn_out, out_weight, residual, index_weight
    )
    summed = lax.psum_scatter(partial, "z", scatter_dimension=0, tiled=False)

    weight_mine = swap(half_weight, "yh")
    down_mine, down_other, weight_mine = down_weight_rows(
        latent_weight, index_proj, c * 8 + x * 2 + yl, weight_mine
    )
    summed, index_keys, down_mine, down_other = lax.optimization_barrier(
        (summed, index_keys, down_mine, down_other)
    )
    all_keys = lax.all_gather(index_keys, SEQ, axis=0, tiled=True)
    kept, got = summed[0], swap(summed[1], "yh")
    gain = lax.dynamic_slice_in_dim(norm_gain, z * DZ, DZ).reshape(1, DZ)
    hidden, lifted = lift(jnp.stack([c]).astype(jnp.int32), kept, got, gain, down_mine, down_other)
    parts = from_last(lifted.reshape(NZ, own, lifted.shape[1]))
    packed, give = normalize(
        jnp.stack([yh]).astype(jnp.int32), parts, latent_gain.reshape(1, QL)
    )
    packed, weight_mine = lax.optimization_barrier((packed, weight_mine))
    weight_theirs = swap(weight_mine, "c")
    weight_theirs, hidden = lax.optimization_barrier((weight_theirs, hidden))
    hidden_cols = from_last(hidden.reshape(NZ, own, DZ))
    turned, beside = lax.optimization_barrier((turn(packed), swap(give, "yh")))
    everyone = from_last(jnp.broadcast_to(turned[None, :, :QL], (NZ, own, QL)))
    everyone, hidden_cols = lax.optimization_barrier((everyone.reshape(HALF, QL), hidden_cols))
    hidden_rows = hidden_cols[::-1].transpose(1, 0, 2).reshape(own, D)
    place = jnp.stack([c, yh]).astype(jnp.int32)
    queries = make_queries(place, everyone, index_weight, weight_mine, weight_theirs, packed, beside)
    queries = from_last(queries)
    latent_out = queries[::-1, 8:, :, :local].reshape(rows, local)
    scores = make_scores(queries, turned[:, QL:], all_keys)
    scores = lax.all_to_all(scores, SEQ, 0, 0, axis_index_groups=[list(range(N_SEQ))[::-1]])

    own_positions = lax.dynamic_slice_in_dim(positions, head * rows, rows).reshape(rows, 1)
    numbers = jnp.stack([cache_len[0], seq * SLOTS]).astype(jnp.int32)
    return (hidden_rows, latent_out, finish(numbers, scores, own_positions))


def solution(mesh):
    fine = Mesh(mesh.devices.reshape(4, 2, 2, 8, 2), SEQ + HEAD)
    in_specs = (
        P(SEQ, HEAD),
        P(HEAD, None),
        P(SEQ + HEAD, None),
        P(),
        P(None, HEAD),
        P(None, HEAD),
        P(),
        P(None, HEAD),
        P(SEQ, None),
        P(),
        P(SEQ),
    )
    out_specs = (P(SEQ + HEAD, None), P(SEQ, HEAD), P(HEAD, SEQ))
    return jax.shard_map(shards, mesh=fine, in_specs=in_specs, out_specs=out_specs, check_vma=False)
```

```python
import functools

import jax
import jax.numpy as jnp
from jax import lax
from jax.experimental import pallas as pl
from jax.experimental.layout import Layout, with_layout_constraint
from jax.experimental.pallas import tpu as pltpu
from jax.sharding import Mesh
from jax.sharding import PartitionSpec as P

D = 7168
QL = 1536
IHEADS = 64
IDIM = 128
N_SEQ = 16
N_HEAD = 16
NZ = 8
DZ = D // NZ
EPSILON = 1e-06
SEQ = ("x", "yl", "c")
HEAD = ("z", "yh")
HALF = 128
SLOTS = 1024


def swap(values, axis):
    return lax.ppermute(values, axis, [(0, 1), (1, 0)])


def from_last(values):
    return lax.all_to_all(values, "z", 0, 0, axis_index_groups=[list(range(NZ))[::-1]])


def kernel_params():
    return pltpu.CompilerParams(vmem_limit_bytes=20 * 1024 * 1024)


def big_params():
    return pltpu.CompilerParams(vmem_limit_bytes=60 * 1024 * 1024)


def project_kernel(place_ref, a_ref, b_ref, res_ref, w_ref, o_ref, half_ref, b_held, o_held, in_sems, out_sems, half_sem):
    head, core = place_ref[0] // 2, place_ref[0] % 2
    own = pl.ds(pl.multiple_of((NZ - 1 - head // 2) * 16, 16), 16)
    depth = half_ref.shape[0]
    half_copy = pltpu.make_async_copy(
        w_ref.at[pl.ds(pl.multiple_of(core * depth, 16), depth), :], half_ref, half_sem
    )

    def fetch(i):
        columns = pl.ds(pl.multiple_of(i * DZ, 128), DZ)
        return pltpu.make_async_copy(b_ref.at[:, columns], b_held.at[i], in_sems.at[i])

    def store(i):
        return pltpu.make_async_copy(o_held.at[i], o_ref.at[i], out_sems.at[i])

    for i in range(NZ):
        fetch(i).start()
    half_copy.start()

    @pl.loop(0, NZ)
    def _(i):
        columns = pl.ds(pl.multiple_of(i * DZ, 128), DZ)
        fetch(i).wait()
        product = jnp.dot(a_ref[...], b_held[i], preferred_element_type=jnp.float32)
        product = product.astype(o_ref.dtype)
        for group in range(NZ):
            for half in range(2):
                at = (NZ - 1 - group) * 16
                o_held[i, half ^ (head % 2), at : at + 16, :] = product[
                    group * 32 + half * 16 : group * 32 + (half + 1) * 16, :
                ]
        added = o_held[i, 0, own, :].astype(jnp.float32) + res_ref[:, columns].astype(jnp.float32)
        o_held[i, 0, own, :] = added.astype(o_ref.dtype)
        store(i).start()

    for i in range(NZ):
        store(i).wait()
    half_copy.wait()


def project(place, attn_out, out_weight, residual, index_weight):
    rows, depth = attn_out.shape
    whole = pl.BlockSpec(memory_space=pltpu.VMEM)
    apart = pl.BlockSpec(memory_space=pl.ANY)
    shape = (NZ, 2, HALF, DZ)
    return pl.pallas_call(
        project_kernel,
        in_specs=[pl.BlockSpec(memory_space=pltpu.SMEM), whole, apart, whole, apart],
        out_specs=[apart, whole],
        out_shape=[
            jax.ShapeDtypeStruct(shape, jnp.bfloat16),
            jax.ShapeDtypeStruct((QL // 2, index_weight.shape[1]), jnp.bfloat16),
        ],
        scratch_shapes=[
            pltpu.VMEM((NZ, depth, DZ), jnp.bfloat16),
            pltpu.VMEM(shape, jnp.bfloat16),
            pltpu.SemaphoreType.DMA((NZ,)),
            pltpu.SemaphoreType.DMA((NZ,)),
            pltpu.SemaphoreType.DMA,
        ],
        compiler_params=big_params(),
    )(place, attn_out, out_weight, residual, index_weight)


def lift_kernel(core_ref, kept_ref, got_ref, gain_ref, mine_ref, other_ref, o_ref):
    hidden = (kept_ref[...].astype(jnp.float32) + got_ref[...].astype(jnp.float32)).astype(jnp.bfloat16)
    o_ref[:, QL + 128 :] = hidden
    wide = hidden.astype(jnp.float32)
    squares = jnp.sum(wide * wide, axis=1, keepdims=True)
    high = squares.astype(jnp.bfloat16).astype(jnp.float32)
    scaled = wide * gain_ref[...].astype(jnp.float32)
    first, second = scaled[:, : DZ // 2], scaled[:, DZ // 2 :]
    is_first = core_ref[0] == 0
    mine = jnp.where(is_first, first, second).astype(jnp.bfloat16)
    other = jnp.where(is_first, second, first).astype(jnp.bfloat16)
    lifted = jnp.dot(mine, mine_ref[...], preferred_element_type=jnp.float32) + jnp.dot(
        other, other_ref[...], preferred_element_type=jnp.float32
    )
    lane = lax.broadcasted_iota(jnp.int32, (HALF, 128), 1)
    tail = jnp.where(lane == IHEADS, high, jnp.where(lane == IHEADS + 1, squares - high, 0.0))
    o_ref[:, :QL] = lifted[:, :QL].astype(jnp.bfloat16)
    o_ref[:, QL : QL + 128] = jnp.where(lane < IHEADS, lifted[:, QL:], tail).astype(jnp.bfloat16)


def lift(core, kept, got, gain, mine, other):
    whole = pl.BlockSpec(memory_space=pltpu.VMEM)
    return pl.pallas_call(
        lift_kernel,
        in_specs=[pl.BlockSpec(memory_space=pltpu.SMEM)] + [whole] * 5,
        out_specs=whole,
        out_shape=jax.ShapeDtypeStruct((HALF, QL + 128 + DZ), jnp.bfloat16),
        compiler_params=kernel_params(),
    )(core, kept, got, gain, mine, other)


def norm_kernel(high_ref, parts_ref, gain_ref, o_ref, give_ref, hidden_ref):
    total = parts_ref[0, :, : QL + 128].astype(jnp.float32)
    for n in range(1, NZ):
        total = total + parts_ref[n, :, : QL + 128].astype(jnp.float32)
    for n in range(NZ):
        hidden_ref[:, n * DZ : (n + 1) * DZ] = parts_ref[NZ - 1 - n, :, QL + 128 :]
    mean = (total[:, 1600:1601] + total[:, 1601:1602]) / D
    inverse = lax.rsqrt(mean + EPSILON)
    raw = (total[:, :QL] * inverse).astype(jnp.bfloat16).astype(jnp.float32)
    level = lax.rsqrt(jnp.mean(raw * raw, axis=-1, keepdims=True) + EPSILON)
    latent = (raw * level * gain_ref[...].astype(jnp.float32)).astype(jnp.bfloat16)
    lane = lax.broadcasted_iota(jnp.int32, (16, 128), 1)
    weights = jnp.where(lane < IHEADS, total[:, QL:] * inverse * IHEADS ** (-0.5), 0.0)
    o_ref[:, :QL] = latent
    o_ref[:, QL:] = weights.astype(jnp.bfloat16)
    for block in range(NZ):
        low = latent[:, block * 192 : block * 192 + 96]
        top = latent[:, block * 192 + 96 : block * 192 + 192]
        give_ref[:, block * 96 : (block + 1) * 96] = jnp.where(high_ref[0] == 0, top, low)


def normalize(high, parts, gain):
    whole = pl.BlockSpec(memory_space=pltpu.VMEM)
    return pl.pallas_call(
        norm_kernel,
        in_specs=[pl.BlockSpec(memory_space=pltpu.SMEM), whole, whole],
        out_specs=[whole] * 3,
        out_shape=[
            jax.ShapeDtypeStruct((16, QL + 128), jnp.bfloat16),
            jax.ShapeDtypeStruct((16, QL // 2), jnp.bfloat16),
            jax.ShapeDtypeStruct((16, D), jnp.bfloat16),
        ],
        compiler_params=kernel_params(),
    )(high, parts, gain)


def query_kernel(place_ref, latent_ref, own_ref, mine_ref, theirs_ref, final_ref, beside_ref, o_ref):
    core, high = place_ref[0], place_ref[1]
    is_first = core == 0
    left, right = latent_ref[:, : QL // 2], latent_ref[:, QL // 2 : QL]
    here = jnp.where(is_first, left, right)
    there = jnp.where(is_first, right, left)
    own = jnp.dot(latent_ref[:, :QL], own_ref[...], preferred_element_type=jnp.float32)
    other = jnp.dot(here, mine_ref[...], preferred_element_type=jnp.float32) + jnp.dot(
        there, theirs_ref[...], preferred_element_type=jnp.float32
    )
    for at, part in ((high * 4, own), ((1 - high) * 4, other)):
        part = part.astype(jnp.bfloat16)
        for j in range(4):
            for block in range(NZ):
                o_ref[block, at + j] = part[block * 16 : (block + 1) * 16, j * IDIM : (j + 1) * IDIM]
    o_ref[:, 8:] = jnp.zeros((NZ, 2, 16, IDIM), jnp.bfloat16)
    for block in range(NZ):
        low = final_ref[:, block * 192 : block * 192 + 96]
        top = final_ref[:, block * 192 + 96 : block * 192 + 192]
        o_ref[NZ - 1 - block, 8 + high, :, :96] = jnp.where(high == 0, low, top)
        o_ref[NZ - 1 - block, 9 - high, :, :96] = beside_ref[:, block * 96 : (block + 1) * 96]


def make_queries(place, latent, own, mine, theirs, final, beside):
    whole = pl.BlockSpec(memory_space=pltpu.VMEM)
    return pl.pallas_call(
        query_kernel,
        in_specs=[pl.BlockSpec(memory_space=pltpu.SMEM)] + [whole] * 6,
        out_specs=whole,
        out_shape=jax.ShapeDtypeStruct((NZ, 10, 16, IDIM), jnp.bfloat16),
        compiler_params=kernel_params(),
    )(place, latent, own, mine, theirs, final, beside)


def score_kernel(q_ref, w_ref, k_ref, o_ref, wide_ref, rows_ref):
    scale = IDIM ** (-0.5)
    tile = 256

    @pl.when(pl.program_id(0) == 0)
    def _():
        weights = w_ref[...].astype(jnp.float32) * scale
        for j in range(IHEADS):
            wide_ref[j * 16 : (j + 1) * 16, :] = jnp.broadcast_to(weights[:, j : j + 1], (16, 128))
            rows_ref[j * 16 : (j + 1) * 16, :] = q_ref[NZ - 1 - j // 8, j % 8]

    blocks, _, slots = o_ref.shape
    for block in range(blocks):
        for slot in range(0, slots, tile):
            at = block * slots + slot
            logits = lax.dot_general(
                rows_ref[...],
                k_ref[at : at + tile, :],
                (((1,), (1,)), ((), ())),
                preferred_element_type=jnp.float32,
            )
            halves = [jnp.zeros((16, 128), jnp.float32), jnp.zeros((16, 128), jnp.float32)]
            for j in range(IHEADS):
                weight = wide_ref[j * 16 : (j + 1) * 16, :]
                for n in range(2):
                    halves[n] += (
                        jnp.maximum(logits[j * 16 : (j + 1) * 16, n * 128 : (n + 1) * 128], 0.0) * weight
                    )
            for n in range(2):
                o_ref[blocks - 1 - block, :, slot + n * 128 : slot + (n + 1) * 128] = halves[n].astype(o_ref.dtype)


def make_scores(queries, head_weights, keys):
    per_step = 4
    return pl.pallas_call(
        score_kernel,
        grid=(N_SEQ // per_step,),
        in_specs=[
            pl.BlockSpec(queries.shape, lambda i: (0, 0, 0, 0)),
            pl.BlockSpec((16, 128), lambda i: (0, 0)),
            pl.BlockSpec((per_step * SLOTS, IDIM), lambda i: (i, 0)),
        ],
        out_specs=pl.BlockSpec((per_step, 16, SLOTS), lambda i: (N_SEQ // per_step - 1 - i, 0, 0)),
        out_shape=jax.ShapeDtypeStruct((N_SEQ, 16, SLOTS), jnp.bfloat16),
        scratch_shapes=[
            pltpu.VMEM((IHEADS * 16, 128), jnp.float32),
            pltpu.VMEM((IHEADS * 16, IDIM), jnp.bfloat16),
        ],
        compiler_params=big_params(),
        cost_estimate=pl.CostEstimate(
            flops=4 * IHEADS * 16 * keys.shape[0] * IDIM, bytes_accessed=2 * keys.size * 2, transcendentals=0
        ),
    )(queries, head_weights, keys)


def finish_kernel(numbers_ref, s_ref, pos_ref, o_ref):
    local = lax.broadcasted_iota(jnp.int32, (16, SLOTS), 1)
    filled, base = numbers_ref[0], numbers_ref[1]
    for group in range(N_SEQ):
        here = slice(group * 16, (group + 1) * 16)
        reach = jnp.minimum(filled, pos_ref[here, :] - base + 1)
        o_ref[here, :] = jnp.where(local < reach, s_ref[N_SEQ - 1 - group].astype(jnp.float32), 0.0)


def finish(numbers, scores, own_positions):
    whole = pl.BlockSpec(memory_space=pltpu.VMEM)
    return pl.pallas_call(
        finish_kernel,
        in_specs=[pl.BlockSpec(memory_space=pltpu.SMEM), whole, whole],
        out_specs=whole,
        out_shape=jax.ShapeDtypeStruct((N_SEQ * 16, SLOTS), jnp.float32),
        compiler_params=kernel_params(),
    )(numbers, scores, own_positions)


def down_weight_rows(latent_weight, index_proj, piece, high, early):
    share = DZ // N_SEQ

    def own_rows(weight):
        columns = weight.T.reshape(weight.shape[1], NZ, DZ)
        return lax.dynamic_slice_in_dim(columns, piece * share, share, 2)

    own = jnp.concatenate([own_rows(latent_weight), own_rows(index_proj)], axis=0)
    own = with_layout_constraint(own, Layout(major_to_minor=(0, 1, 2)))
    mine = lax.all_to_all(own.transpose(1, 2, 0), "z", 0, 0)
    theirs = swap(mine, "yh")
    pair = [jnp.where(high == 0, mine, theirs), jnp.where(high == 0, theirs, mine)]
    by_head = jnp.stack(pair, axis=1).reshape(N_HEAD, share, own.shape[0]).transpose(1, 0, 2)
    local = latent_weight.shape[1]
    wide = jnp.concatenate(
        [
            by_head[:, :, :local].reshape(share, QL),
            by_head[:, :, local:].reshape(share, IHEADS),
            jnp.zeros((share, 64), jnp.bfloat16),
        ],
        axis=1,
    )
    wide, early = lax.optimization_barrier((wide, early))
    half = lax.all_to_all(jnp.broadcast_to(wide[None], (8,) + wide.shape), ("x", "yl"), 0, 0)
    half = half.reshape(8 * share, wide.shape[1])
    return half, swap(half, "c"), early


def turn(values):
    moves = [(s * N_HEAD + h, h * N_HEAD + s) for s in range(N_SEQ) for h in range(N_HEAD)]
    return lax.ppermute(values, SEQ + HEAD, moves)


def shards(
    attn_out,
    out_weight,
    residual,
    norm_gain,
    latent_weight,
    index_proj,
    latent_gain,
    index_weight,
    index_keys,
    positions,
    cache_len,
):
    x, yl, c = (lax.axis_index(a) for a in SEQ)
    z, yh = (lax.axis_index(a) for a in HEAD)
    seq = (x * 2 + yl) * 2 + c
    head = z * 2 + yh
    rows = attn_out.shape[0]
    own = rows // N_HEAD
    local = latent_weight.shape[1]

    partial, half_weight = project(
        jnp.stack([head * 2 + c]).astype(jnp.int32), attn_out, out_weight, residual, index_weight
    )
    summed = lax.psum_scatter(partial, "z", scatter_dimension=0, tiled=False)

    weight_mine = swap(half_weight, "yh")
    down_mine, down_other, weight_mine = down_weight_rows(
        latent_weight, index_proj, c * 8 + x * 2 + yl, yh, weight_mine
    )
    weight_theirs = swap(weight_mine, "c")
    summed, index_keys, down_mine, down_other = lax.optimization_barrier(
        (summed, index_keys, down_mine, down_other)
    )
    all_keys = lax.all_gather(index_keys, SEQ, axis=0, tiled=True)
    kept, got = summed[0], swap(summed[1], "yh")
    gain = lax.dynamic_slice_in_dim(norm_gain, z * DZ, DZ).reshape(1, DZ)
    lifted = lift(jnp.stack([c]).astype(jnp.int32), kept, got, gain, down_mine, down_other)
    lifted, weight_theirs = lax.optimization_barrier((lifted, weight_theirs))
    parts = from_last(lifted.reshape(NZ, own, lifted.shape[1]))
    packed, give, hidden_rows = normalize(
        jnp.stack([yh]).astype(jnp.int32), parts, latent_gain.reshape(1, QL)
    )
    turned, beside = lax.optimization_barrier((turn(packed), swap(give, "yh")))
    everyone = from_last(jnp.broadcast_to(turned[None, :, :QL], (NZ, own, QL)))
    everyone = everyone.reshape(HALF, QL)
    place = jnp.stack([c, yh]).astype(jnp.int32)
    queries = make_queries(place, everyone, index_weight, weight_mine, weight_theirs, packed, beside)
    queries = from_last(queries)
    latent_out = queries[::-1, 8:, :, :local].reshape(rows, local)
    scores = make_scores(queries, turned[:, QL:], all_keys)
    scores = lax.all_to_all(scores, SEQ, 0, 0, axis_index_groups=[list(range(N_SEQ))[::-1]])

    own_positions = lax.dynamic_slice_in_dim(positions, head * rows, rows).reshape(rows, 1)
    numbers = jnp.stack([cache_len[0], seq * SLOTS]).astype(jnp.int32)
    return (hidden_rows, latent_out, finish(numbers, scores, own_positions))


def solution(mesh):
    fine = Mesh(mesh.devices.reshape(4, 2, 2, 8, 2), SEQ + HEAD)
    in_specs = (
        P(SEQ, HEAD),
        P(HEAD, None),
        P(SEQ + HEAD, None),
        P(),
        P(None, HEAD),
        P(None, HEAD),
        P(),
        P(None, HEAD),
        P(SEQ, None),
        P(),
        P(SEQ),
    )
    out_specs = (P(SEQ + HEAD, None), P(SEQ, HEAD), P(HEAD, SEQ))
    return jax.shard_map(shards, mesh=fine, in_specs=in_specs, out_specs=out_specs, check_vma=False)
```

```python
import functools

import jax
import jax.numpy as jnp
from jax import lax
from jax.experimental import pallas as pl
from jax.experimental.layout import Layout, with_layout_constraint
from jax.experimental.pallas import tpu as pltpu
from jax.sharding import Mesh
from jax.sharding import PartitionSpec as P

D = 7168
QL = 1536
IHEADS = 64
IDIM = 128
N_SEQ = 16
N_HEAD = 16
NZ = 8
DZ = D // NZ
EPSILON = 1e-06
SEQ = ("x", "yl", "c")
HEAD = ("z", "yh")
HALF = 128
SLOTS = 1024


def swap(values, axis):
    return lax.ppermute(values, axis, [(0, 1), (1, 0)])


def from_last(values):
    return lax.all_to_all(values, "z", 0, 0, axis_index_groups=[list(range(NZ))[::-1]])


def kernel_params():
    return pltpu.CompilerParams(vmem_limit_bytes=20 * 1024 * 1024)


def big_params():
    return pltpu.CompilerParams(vmem_limit_bytes=60 * 1024 * 1024)


def project_kernel(place_ref, a_ref, b_ref, res_ref, w_ref, o_ref, half_ref, b_held, o_held, in_sems, out_sems, half_sem):
    head, core = place_ref[0] // 2, place_ref[0] % 2
    own = pl.ds(pl.multiple_of((NZ - 1 - head // 2) * 16, 16), 16)
    depth = half_ref.shape[0]
    half_copy = pltpu.make_async_copy(
        w_ref.at[pl.ds(pl.multiple_of(core * depth, 16), depth), :], half_ref, half_sem
    )

    def fetch(i):
        columns = pl.ds(pl.multiple_of(i * DZ, 128), DZ)
        return pltpu.make_async_copy(b_ref.at[:, columns], b_held.at[i], in_sems.at[i])

    def store(i):
        return pltpu.make_async_copy(o_held.at[i], o_ref.at[i], out_sems.at[i])

    for i in range(NZ):
        fetch(i).start()
    half_copy.start()

    @pl.loop(0, NZ)
    def _(i):
        columns = pl.ds(pl.multiple_of(i * DZ, 128), DZ)
        fetch(i).wait()
        product = jnp.dot(a_ref[...], b_held[i], preferred_element_type=jnp.float32)
        product = product.astype(o_ref.dtype)
        for group in range(NZ):
            for half in range(2):
                at = (NZ - 1 - group) * 16
                o_held[i, half ^ (head % 2), at : at + 16, :] = product[
                    group * 32 + half * 16 : group * 32 + (half + 1) * 16, :
                ]
        added = o_held[i, 0, own, :].astype(jnp.float32) + res_ref[:, columns].astype(jnp.float32)
        o_held[i, 0, own, :] = added.astype(o_ref.dtype)
        store(i).start()

    for i in range(NZ):
        store(i).wait()
    half_copy.wait()


def project(place, attn_out, out_weight, residual, index_weight):
    rows, depth = attn_out.shape
    whole = pl.BlockSpec(memory_space=pltpu.VMEM)
    apart = pl.BlockSpec(memory_space=pl.ANY)
    shape = (NZ, 2, HALF, DZ)
    return pl.pallas_call(
        project_kernel,
        in_specs=[pl.BlockSpec(memory_space=pltpu.SMEM), whole, apart, whole, apart],
        out_specs=[apart, whole],
        out_shape=[
            jax.ShapeDtypeStruct(shape, jnp.bfloat16),
            jax.ShapeDtypeStruct((QL // 2, index_weight.shape[1]), jnp.bfloat16),
        ],
        scratch_shapes=[
            pltpu.VMEM((NZ, depth, DZ), jnp.bfloat16),
            pltpu.VMEM(shape, jnp.bfloat16),
            pltpu.SemaphoreType.DMA((NZ,)),
            pltpu.SemaphoreType.DMA((NZ,)),
            pltpu.SemaphoreType.DMA,
        ],
        compiler_params=big_params(),
    )(place, attn_out, out_weight, residual, index_weight)


def lift_kernel(core_ref, kept_ref, got_ref, gain_ref, mine_ref, other_ref, hidden_ref, o_ref):
    hidden = (kept_ref[...].astype(jnp.float32) + got_ref[...].astype(jnp.float32)).astype(jnp.bfloat16)
    hidden_ref[...] = hidden
    wide = hidden.astype(jnp.float32)
    squares = jnp.sum(wide * wide, axis=1, keepdims=True)
    high = squares.astype(jnp.bfloat16).astype(jnp.float32)
    scaled = wide * gain_ref[...].astype(jnp.float32)
    first, second = scaled[:, : DZ // 2], scaled[:, DZ // 2 :]
    is_first = core_ref[0] == 0
    mine = jnp.where(is_first, first, second).astype(jnp.bfloat16)
    other = jnp.where(is_first, second, first).astype(jnp.bfloat16)
    lifted = jnp.dot(mine, mine_ref[...], preferred_element_type=jnp.float32) + jnp.dot(
        other, other_ref[...], preferred_element_type=jnp.float32
    )
    lane = lax.broadcasted_iota(jnp.int32, (HALF, 128), 1)
    tail = jnp.where(lane == IHEADS, high, jnp.where(lane == IHEADS + 1, squares - high, 0.0))
    o_ref[:, :QL] = lifted[:, :QL].astype(jnp.bfloat16)
    o_ref[:, QL:] = jnp.where(lane < IHEADS, lifted[:, QL:], tail).astype(jnp.bfloat16)


def lift(core, kept, got, gain, mine, other):
    whole = pl.BlockSpec(memory_space=pltpu.VMEM)
    return pl.pallas_call(
        lift_kernel,
        in_specs=[pl.BlockSpec(memory_space=pltpu.SMEM)] + [whole] * 5,
        out_specs=[whole, whole],
        out_shape=[
            jax.ShapeDtypeStruct((HALF, DZ), jnp.bfloat16),
            jax.ShapeDtypeStruct((HALF, QL + 128), jnp.bfloat16),
        ],
        compiler_params=kernel_params(),
    )(core, kept, got, gain, mine, other)


def norm_kernel(high_ref, parts_ref, gain_ref, o_ref, give_ref):
    total = parts_ref[0].astype(jnp.float32)
    for n in range(1, NZ):
        total = total + parts_ref[n].astype(jnp.float32)
    mean = (total[:, 1600:1601] + total[:, 1601:1602]) / D
    inverse = lax.rsqrt(mean + EPSILON)
    raw = (total[:, :QL] * inverse).astype(jnp.bfloat16).astype(jnp.float32)
    level = lax.rsqrt(jnp.mean(raw * raw, axis=-1, keepdims=True) + EPSILON)
    latent = (raw * level * gain_ref[...].astype(jnp.float32)).astype(jnp.bfloat16)
    lane = lax.broadcasted_iota(jnp.int32, (16, 128), 1)
    weights = jnp.where(lane < IHEADS, total[:, QL:] * inverse * IHEADS ** (-0.5), 0.0)
    o_ref[:, :QL] = latent
    o_ref[:, QL:] = weights.astype(jnp.bfloat16)
    for block in range(NZ):
        low = latent[:, block * 192 : block * 192 + 96]
        top = latent[:, block * 192 + 96 : block * 192 + 192]
        give_ref[:, block * 96 : (block + 1) * 96] = jnp.where(high_ref[0] == 0, top, low)


def normalize(high, parts, gain):
    whole = pl.BlockSpec(memory_space=pltpu.VMEM)
    return pl.pallas_call(
        norm_kernel,
        in_specs=[pl.BlockSpec(memory_space=pltpu.SMEM), whole, whole],
        out_specs=[whole, whole],
        out_shape=[
            jax.ShapeDtypeStruct((16, QL + 128), jnp.bfloat16),
            jax.ShapeDtypeStruct((16, QL // 2), jnp.bfloat16),
        ],
        compiler_params=kernel_params(),
    )(high, parts, gain)


def query_kernel(place_ref, latent_ref, own_ref, mine_ref, theirs_ref, final_ref, beside_ref, o_ref):
    core, high = place_ref[0], place_ref[1]
    is_first = core == 0
    left, right = latent_ref[:, : QL // 2], latent_ref[:, QL // 2 : QL]
    here = jnp.where(is_first, left, right)
    there = jnp.where(is_first, right, left)
    own = jnp.dot(latent_ref[:, :QL], own_ref[...], preferred_element_type=jnp.float32)
    other = jnp.dot(here, mine_ref[...], preferred_element_type=jnp.float32) + jnp.dot(
        there, theirs_ref[...], preferred_element_type=jnp.float32
    )
    for at, part in ((high * 4, own), ((1 - high) * 4, other)):
        part = part.astype(jnp.bfloat16)
        for j in range(4):
            for block in range(NZ):
                o_ref[block, at + j] = part[block * 16 : (block + 1) * 16, j * IDIM : (j + 1) * IDIM]
    o_ref[:, 8:] = jnp.zeros((NZ, 2, 16, IDIM), jnp.bfloat16)
    for block in range(NZ):
        low = final_ref[:, block * 192 : block * 192 + 96]
        top = final_ref[:, block * 192 + 96 : block * 192 + 192]
        o_ref[NZ - 1 - block, 8 + high, :, :96] = jnp.where(high == 0, low, top)
        o_ref[NZ - 1 - block, 9 - high, :, :96] = beside_ref[:, block * 96 : (block + 1) * 96]


def make_queries(place, latent, own, mine, theirs, final, beside):
    whole = pl.BlockSpec(memory_space=pltpu.VMEM)
    return pl.pallas_call(
        query_kernel,
        in_specs=[pl.BlockSpec(memory_space=pltpu.SMEM)] + [whole] * 6,
        out_specs=whole,
        out_shape=jax.ShapeDtypeStruct((NZ, 10, 16, IDIM), jnp.bfloat16),
        compiler_params=kernel_params(),
    )(place, latent, own, mine, theirs, final, beside)


def score_kernel(q_ref, w_ref, k_ref, o_ref, wide_ref, rows_ref):
    scale = IDIM ** (-0.5)
    tile = 256

    @pl.when(pl.program_id(0) == 0)
    def _():
        weights = w_ref[...].astype(jnp.float32) * scale
        for j in range(IHEADS):
            wide_ref[j * 16 : (j + 1) * 16, :] = jnp.broadcast_to(weights[:, j : j + 1], (16, 128))
            rows_ref[j * 16 : (j + 1) * 16, :] = q_ref[NZ - 1 - j // 8, j % 8]

    blocks, _, slots = o_ref.shape
    for block in range(blocks):
        for slot in range(0, slots, tile):
            at = block * slots + slot
            logits = lax.dot_general(
                rows_ref[...],
                k_ref[at : at + tile, :],
                (((1,), (1,)), ((), ())),
                preferred_element_type=jnp.float32,
            )
            halves = [jnp.zeros((16, 128), jnp.float32), jnp.zeros((16, 128), jnp.float32)]
            for j in range(IHEADS):
                weight = wide_ref[j * 16 : (j + 1) * 16, :]
                for n in range(2):
                    halves[n] += (
                        jnp.maximum(logits[j * 16 : (j + 1) * 16, n * 128 : (n + 1) * 128], 0.0) * weight
                    )
            for n in range(2):
                o_ref[blocks - 1 - block, :, slot + n * 128 : slot + (n + 1) * 128] = halves[n].astype(o_ref.dtype)


def make_scores(queries, head_weights, keys):
    per_step = 4
    return pl.pallas_call(
        score_kernel,
        grid=(N_SEQ // per_step,),
        in_specs=[
            pl.BlockSpec(queries.shape, lambda i: (0, 0, 0, 0)),
            pl.BlockSpec((16, 128), lambda i: (0, 0)),
            pl.BlockSpec((per_step * SLOTS, IDIM), lambda i: (i, 0)),
        ],
        out_specs=pl.BlockSpec((per_step, 16, SLOTS), lambda i: (N_SEQ // per_step - 1 - i, 0, 0)),
        out_shape=jax.ShapeDtypeStruct((N_SEQ, 16, SLOTS), jnp.bfloat16),
        scratch_shapes=[
            pltpu.VMEM((IHEADS * 16, 128), jnp.float32),
            pltpu.VMEM((IHEADS * 16, IDIM), jnp.bfloat16),
        ],
        compiler_params=big_params(),
        cost_estimate=pl.CostEstimate(
            flops=4 * IHEADS * 16 * keys.shape[0] * IDIM, bytes_accessed=2 * keys.size * 2, transcendentals=0
        ),
    )(queries, head_weights, keys)


def finish_kernel(numbers_ref, s_ref, pos_ref, o_ref):
    local = lax.broadcasted_iota(jnp.int32, (16, SLOTS), 1)
    filled, base = numbers_ref[0], numbers_ref[1]
    for group in range(N_SEQ):
        here = slice(group * 16, (group + 1) * 16)
        reach = jnp.minimum(filled, pos_ref[here, :] - base + 1)
        o_ref[here, :] = jnp.where(local < reach, s_ref[N_SEQ - 1 - group].astype(jnp.float32), 0.0)


def finish(numbers, scores, own_positions):
    whole = pl.BlockSpec(memory_space=pltpu.VMEM)
    return pl.pallas_call(
        finish_kernel,
        in_specs=[pl.BlockSpec(memory_space=pltpu.SMEM), whole, whole],
        out_specs=whole,
        out_shape=jax.ShapeDtypeStruct((N_SEQ * 16, SLOTS), jnp.float32),
        compiler_params=kernel_params(),
    )(numbers, scores, own_positions)


def down_weight_rows(latent_weight, index_proj, piece, high, early):
    share = DZ // N_SEQ

    def own_rows(weight):
        columns = weight.T.reshape(weight.shape[1], NZ, DZ)
        return lax.dynamic_slice_in_dim(columns, piece * share, share, 2)

    own = jnp.concatenate([own_rows(latent_weight), own_rows(index_proj)], axis=0)
    own = with_layout_constraint(own, Layout(major_to_minor=(0, 1, 2)))
    mine = lax.all_to_all(own.transpose(1, 2, 0), "z", 0, 0)
    theirs = swap(mine, "yh")
    pair = [jnp.where(high == 0, mine, theirs), jnp.where(high == 0, theirs, mine)]
    by_head = jnp.stack(pair, axis=1).reshape(N_HEAD, share, own.shape[0]).transpose(1, 0, 2)
    local = latent_weight.shape[1]
    wide = jnp.concatenate(
        [
            by_head[:, :, :local].reshape(share, QL),
            by_head[:, :, local:].reshape(share, IHEADS),
            jnp.zeros((share, 64), jnp.bfloat16),
        ],
        axis=1,
    )
    wide, early = lax.optimization_barrier((wide, early))
    half = lax.all_to_all(jnp.broadcast_to(wide[None], (8,) + wide.shape), ("x", "yl"), 0, 0)
    half = half.reshape(8 * share, wide.shape[1])
    return half, swap(half, "c"), early


def turn(values):
    moves = [(s * N_HEAD + h, h * N_HEAD + s) for s in range(N_SEQ) for h in range(N_HEAD)]
    return lax.ppermute(values, SEQ + HEAD, moves)


def shards(
    attn_out,
    out_weight,
    residual,
    norm_gain,
    latent_weight,
    index_proj,
    latent_gain,
    index_weight,
    index_keys,
    positions,
    cache_len,
):
    x, yl, c = (lax.axis_index(a) for a in SEQ)
    z, yh = (lax.axis_index(a) for a in HEAD)
    seq = (x * 2 + yl) * 2 + c
    head = z * 2 + yh
    rows = attn_out.shape[0]
    own = rows // N_HEAD
    local = latent_weight.shape[1]

    partial, half_weight = project(
        jnp.stack([head * 2 + c]).astype(jnp.int32), attn_out, out_weight, residual, index_weight
    )
    summed = lax.psum_scatter(partial, "z", scatter_dimension=0, tiled=False)

    weight_mine = swap(half_weight, "yh")
    down_mine, down_other, weight_mine = down_weight_rows(
        latent_weight, index_proj, c * 8 + x * 2 + yl, yh, weight_mine
    )
    weight_theirs = swap(weight_mine, "c")
    summed, index_keys, down_mine, down_other = lax.optimization_barrier(
        (summed, index_keys, down_mine, down_other)
    )
    all_keys = lax.all_gather(index_keys, SEQ, axis=0, tiled=True)
    kept, got = summed[0], swap(summed[1], "yh")
    gain = lax.dynamic_slice_in_dim(norm_gain, z * DZ, DZ).reshape(1, DZ)
    hidden, lifted = lift(jnp.stack([c]).astype(jnp.int32), kept, got, gain, down_mine, down_other)
    lifted, weight_theirs = lax.optimization_barrier((lifted, weight_theirs))
    parts = from_last(lifted.reshape(NZ, own, lifted.shape[1]))
    packed, give = normalize(
        jnp.stack([yh]).astype(jnp.int32), parts, latent_gain.reshape(1, QL)
    )
    turned, beside = lax.optimization_barrier((turn(packed), swap(give, "yh")))
    everyone = from_last(jnp.broadcast_to(turned[None, :, :QL], (NZ, own, QL)))
    everyone, hidden = lax.optimization_barrier((everyone.reshape(HALF, QL), hidden))
    all_hidden = lax.all_gather(hidden, "z", axis=0, tiled=False)
    hidden_rows = lax.dynamic_slice_in_dim(all_hidden, (NZ - 1 - z) * own, own, 1)
    hidden_rows = hidden_rows.transpose(1, 0, 2).reshape(own, D)
    place = jnp.stack([c, yh]).astype(jnp.int32)
    queries = make_queries(place, everyone, index_weight, weight_mine, weight_theirs, packed, beside)
    queries = from_last(queries)
    latent_out = queries[::-1, 8:, :, :local].reshape(rows, local)
    scores = make_scores(queries, turned[:, QL:], all_keys)
    scores = lax.all_to_all(scores, SEQ, 0, 0, axis_index_groups=[list(range(N_SEQ))[::-1]])

    own_positions = lax.dynamic_slice_in_dim(positions, head * rows, rows).reshape(rows, 1)
    numbers = jnp.stack([cache_len[0], seq * SLOTS]).astype(jnp.int32)
    return (hidden_rows, latent_out, finish(numbers, scores, own_positions))


def solution(mesh):
    fine = Mesh(mesh.devices.reshape(4, 2, 2, 8, 2), SEQ + HEAD)
    in_specs = (
        P(SEQ, HEAD),
        P(HEAD, None),
        P(SEQ + HEAD, None),
        P(),
        P(None, HEAD),
        P(None, HEAD),
        P(),
        P(None, HEAD),
        P(SEQ, None),
        P(),
        P(SEQ),
    )
    out_specs = (P(SEQ + HEAD, None), P(SEQ, HEAD), P(HEAD, SEQ))
    return jax.shard_map(shards, mesh=fine, in_specs=in_specs, out_specs=out_specs, check_vma=False)
```

```python
import functools

import jax
import jax.numpy as jnp
from jax import lax
from jax.experimental import pallas as pl
from jax.experimental.layout import Layout, with_layout_constraint
from jax.experimental.pallas import tpu as pltpu
from jax.sharding import Mesh
from jax.sharding import PartitionSpec as P

D = 7168
QL = 1536
IHEADS = 64
IDIM = 128
N_SEQ = 16
N_HEAD = 16
NZ = 8
DZ = D // NZ
EPSILON = 1e-06
SEQ = ("x", "yl", "c")
HEAD = ("z", "yh")
HALF = 128
SLOTS = 1024


def swap(values, axis):
    return lax.ppermute(values, axis, [(0, 1), (1, 0)])


def from_last(values):
    return lax.all_to_all(values, "z", 0, 0, axis_index_groups=[list(range(NZ))[::-1]])


def kernel_params():
    return pltpu.CompilerParams(vmem_limit_bytes=20 * 1024 * 1024)


def big_params():
    return pltpu.CompilerParams(vmem_limit_bytes=60 * 1024 * 1024)


def project_kernel(place_ref, a_ref, b_ref, res_ref, w_ref, o_ref, half_ref, b_held, o_held, in_sems, out_sems, half_sem):
    head, core = place_ref[0] // 2, place_ref[0] % 2
    own = pl.ds(pl.multiple_of((NZ - 1 - head // 2) * 16, 16), 16)
    depth = half_ref.shape[0]
    half_copy = pltpu.make_async_copy(
        w_ref.at[pl.ds(pl.multiple_of(core * depth, 16), depth), :], half_ref, half_sem
    )

    def fetch(i):
        columns = pl.ds(pl.multiple_of(i * DZ, 128), DZ)
        return pltpu.make_async_copy(b_ref.at[:, columns], b_held.at[i], in_sems.at[i])

    def store(i):
        return pltpu.make_async_copy(o_held.at[i], o_ref.at[i], out_sems.at[i])

    for i in range(NZ):
        fetch(i).start()
    half_copy.start()

    @pl.loop(0, NZ)
    def _(i):
        columns = pl.ds(pl.multiple_of(i * DZ, 128), DZ)
        fetch(i).wait()
        product = jnp.dot(a_ref[...], b_held[i], preferred_element_type=jnp.float32)
        product = product.astype(o_ref.dtype)
        for group in range(NZ):
            for half in range(2):
                at = (NZ - 1 - group) * 16
                o_held[i, half ^ (head % 2), at : at + 16, :] = product[
                    group * 32 + half * 16 : group * 32 + (half + 1) * 16, :
                ]
        added = o_held[i, 0, own, :].astype(jnp.float32) + res_ref[:, columns].astype(jnp.float32)
        o_held[i, 0, own, :] = added.astype(o_ref.dtype)
        store(i).start()

    for i in range(NZ):
        store(i).wait()
    half_copy.wait()


def project(place, attn_out, out_weight, residual, index_weight):
    rows, depth = attn_out.shape
    whole = pl.BlockSpec(memory_space=pltpu.VMEM)
    apart = pl.BlockSpec(memory_space=pl.ANY)
    shape = (NZ, 2, HALF, DZ)
    return pl.pallas_call(
        project_kernel,
        in_specs=[pl.BlockSpec(memory_space=pltpu.SMEM), whole, apart, whole, apart],
        out_specs=[apart, whole],
        out_shape=[
            jax.ShapeDtypeStruct(shape, jnp.bfloat16),
            jax.ShapeDtypeStruct((QL // 2, index_weight.shape[1]), jnp.bfloat16),
        ],
        scratch_shapes=[
            pltpu.VMEM((NZ, depth, DZ), jnp.bfloat16),
            pltpu.VMEM(shape, jnp.bfloat16),
            pltpu.SemaphoreType.DMA((NZ,)),
            pltpu.SemaphoreType.DMA((NZ,)),
            pltpu.SemaphoreType.DMA,
        ],
        compiler_params=big_params(),
    )(place, attn_out, out_weight, residual, index_weight)


def lift_kernel(core_ref, kept_ref, got_ref, gain_ref, mine_ref, other_ref, hidden_ref, o_ref):
    hidden = (kept_ref[...].astype(jnp.float32) + got_ref[...].astype(jnp.float32)).astype(jnp.bfloat16)
    hidden_ref[...] = hidden
    wide = hidden.astype(jnp.float32)
    squares = jnp.sum(wide * wide, axis=1, keepdims=True)
    high = squares.astype(jnp.bfloat16).astype(jnp.float32)
    scaled = wide * gain_ref[...].astype(jnp.float32)
    first, second = scaled[:, : DZ // 2], scaled[:, DZ // 2 :]
    is_first = core_ref[0] == 0
    mine = jnp.where(is_first, first, second).astype(jnp.bfloat16)
    other = jnp.where(is_first, second, first).astype(jnp.bfloat16)
    lifted = jnp.dot(mine, mine_ref[...], preferred_element_type=jnp.float32) + jnp.dot(
        other, other_ref[...], preferred_element_type=jnp.float32
    )
    lane = lax.broadcasted_iota(jnp.int32, (HALF, 128), 1)
    tail = jnp.where(lane == IHEADS, high, jnp.where(lane == IHEADS + 1, squares - high, 0.0))
    o_ref[:, :QL] = lifted[:, :QL].astype(jnp.bfloat16)
    o_ref[:, QL:] = jnp.where(lane < IHEADS, lifted[:, QL:], tail).astype(jnp.bfloat16)


def lift(core, kept, got, gain, mine, other):
    whole = pl.BlockSpec(memory_space=pltpu.VMEM)
    return pl.pallas_call(
        lift_kernel,
        in_specs=[pl.BlockSpec(memory_space=pltpu.SMEM)] + [whole] * 5,
        out_specs=[whole, whole],
        out_shape=[
            jax.ShapeDtypeStruct((HALF, DZ), jnp.bfloat16),
            jax.ShapeDtypeStruct((HALF, QL + 128), jnp.bfloat16),
        ],
        compiler_params=kernel_params(),
    )(core, kept, got, gain, mine, other)


def norm_kernel(high_ref, parts_ref, gain_ref, o_ref, give_ref):
    total = parts_ref[0].astype(jnp.float32)
    for n in range(1, NZ):
        total = total + parts_ref[n].astype(jnp.float32)
    mean = (total[:, 1600:1601] + total[:, 1601:1602]) / D
    inverse = lax.rsqrt(mean + EPSILON)
    raw = (total[:, :QL] * inverse).astype(jnp.bfloat16).astype(jnp.float32)
    level = lax.rsqrt(jnp.mean(raw * raw, axis=-1, keepdims=True) + EPSILON)
    latent = (raw * level * gain_ref[...].astype(jnp.float32)).astype(jnp.bfloat16)
    lane = lax.broadcasted_iota(jnp.int32, (16, 128), 1)
    weights = jnp.where(lane < IHEADS, total[:, QL:] * inverse * IHEADS ** (-0.5), 0.0)
    o_ref[:, :QL] = latent
    o_ref[:, QL:] = weights.astype(jnp.bfloat16)
    for block in range(NZ):
        low = latent[:, block * 192 : block * 192 + 96]
        top = latent[:, block * 192 + 96 : block * 192 + 192]
        give_ref[:, block * 96 : (block + 1) * 96] = jnp.where(high_ref[0] == 0, top, low)


def normalize(high, parts, gain):
    whole = pl.BlockSpec(memory_space=pltpu.VMEM)
    return pl.pallas_call(
        norm_kernel,
        in_specs=[pl.BlockSpec(memory_space=pltpu.SMEM), whole, whole],
        out_specs=[whole, whole],
        out_shape=[
            jax.ShapeDtypeStruct((16, QL + 128), jnp.bfloat16),
            jax.ShapeDtypeStruct((16, QL // 2), jnp.bfloat16),
        ],
        compiler_params=kernel_params(),
    )(high, parts, gain)


def query_kernel(place_ref, latent_ref, own_ref, mine_ref, theirs_ref, final_ref, beside_ref, o_ref):
    core, high = place_ref[0], place_ref[1]
    is_first = core == 0
    left, right = latent_ref[:, : QL // 2], latent_ref[:, QL // 2 : QL]
    here = jnp.where(is_first, left, right)
    there = jnp.where(is_first, right, left)
    own = jnp.dot(latent_ref[:, :QL], own_ref[...], preferred_element_type=jnp.float32)
    other = jnp.dot(here, mine_ref[...], preferred_element_type=jnp.float32) + jnp.dot(
        there, theirs_ref[...], preferred_element_type=jnp.float32
    )
    for at, part in ((high * 4, own), ((1 - high) * 4, other)):
        part = part.astype(jnp.bfloat16)
        for j in range(4):
            for block in range(NZ):
                o_ref[block, at + j] = part[block * 16 : (block + 1) * 16, j * IDIM : (j + 1) * IDIM]
    o_ref[:, 8:] = jnp.zeros((NZ, 2, 16, IDIM), jnp.bfloat16)
    for block in range(NZ):
        low = final_ref[:, block * 192 : block * 192 + 96]
        top = final_ref[:, block * 192 + 96 : block * 192 + 192]
        o_ref[NZ - 1 - block, 8 + high, :, :96] = jnp.where(high == 0, low, top)
        o_ref[NZ - 1 - block, 9 - high, :, :96] = beside_ref[:, block * 96 : (block + 1) * 96]


def make_queries(place, latent, own, mine, theirs, final, beside):
    whole = pl.BlockSpec(memory_space=pltpu.VMEM)
    return pl.pallas_call(
        query_kernel,
        in_specs=[pl.BlockSpec(memory_space=pltpu.SMEM)] + [whole] * 6,
        out_specs=whole,
        out_shape=jax.ShapeDtypeStruct((NZ, 10, 16, IDIM), jnp.bfloat16),
        compiler_params=kernel_params(),
    )(place, latent, own, mine, theirs, final, beside)


def score_kernel(q_ref, w_ref, k_ref, o_ref, wide_ref, rows_ref):
    scale = IDIM ** (-0.5)
    tile = 256

    @pl.when(pl.program_id(0) == 0)
    def _():
        weights = w_ref[...].astype(jnp.float32) * scale
        for j in range(IHEADS):
            wide_ref[j * 16 : (j + 1) * 16, :] = jnp.broadcast_to(weights[:, j : j + 1], (16, 128))
            rows_ref[j * 16 : (j + 1) * 16, :] = q_ref[NZ - 1 - j // 8, j % 8]

    blocks, _, slots = o_ref.shape
    for block in range(blocks):
        for slot in range(0, slots, tile):
            at = block * slots + slot
            logits = lax.dot_general(
                rows_ref[...],
                k_ref[at : at + tile, :],
                (((1,), (1,)), ((), ())),
                preferred_element_type=jnp.float32,
            )
            halves = [jnp.zeros((16, 128), jnp.float32), jnp.zeros((16, 128), jnp.float32)]
            for j in range(IHEADS):
                weight = wide_ref[j * 16 : (j + 1) * 16, :]
                for n in range(2):
                    halves[n] += (
                        jnp.maximum(logits[j * 16 : (j + 1) * 16, n * 128 : (n + 1) * 128], 0.0) * weight
                    )
            for n in range(2):
                o_ref[blocks - 1 - block, :, slot + n * 128 : slot + (n + 1) * 128] = halves[n].astype(o_ref.dtype)


def make_scores(queries, head_weights, keys):
    per_step = 4
    return pl.pallas_call(
        score_kernel,
        grid=(N_SEQ // per_step,),
        in_specs=[
            pl.BlockSpec(queries.shape, lambda i: (0, 0, 0, 0)),
            pl.BlockSpec((16, 128), lambda i: (0, 0)),
            pl.BlockSpec((per_step * SLOTS, IDIM), lambda i: (i, 0)),
        ],
        out_specs=pl.BlockSpec((per_step, 16, SLOTS), lambda i: (N_SEQ // per_step - 1 - i, 0, 0)),
        out_shape=jax.ShapeDtypeStruct((N_SEQ, 16, SLOTS), jnp.bfloat16),
        scratch_shapes=[
            pltpu.VMEM((IHEADS * 16, 128), jnp.float32),
            pltpu.VMEM((IHEADS * 16, IDIM), jnp.bfloat16),
        ],
        compiler_params=pltpu.CompilerParams(vmem_limit_bytes=59 * 1024 * 1024),
        cost_estimate=pl.CostEstimate(
            flops=4 * IHEADS * 16 * keys.shape[0] * IDIM, bytes_accessed=2 * keys.size * 2, transcendentals=0
        ),
    )(queries, head_weights, keys)


def finish_kernel(numbers_ref, s_ref, pos_ref, o_ref):
    local = lax.broadcasted_iota(jnp.int32, (16, SLOTS), 1)
    filled, base = numbers_ref[0], numbers_ref[1]
    for group in range(N_SEQ):
        here = slice(group * 16, (group + 1) * 16)
        reach = jnp.minimum(filled, pos_ref[here, :] - base + 1)
        o_ref[here, :] = jnp.where(local < reach, s_ref[N_SEQ - 1 - group].astype(jnp.float32), 0.0)


def finish(numbers, scores, own_positions):
    whole = pl.BlockSpec(memory_space=pltpu.VMEM)
    return pl.pallas_call(
        finish_kernel,
        in_specs=[pl.BlockSpec(memory_space=pltpu.SMEM), whole, whole],
        out_specs=whole,
        out_shape=jax.ShapeDtypeStruct((N_SEQ * 16, SLOTS), jnp.float32),
        compiler_params=kernel_params(),
    )(numbers, scores, own_positions)


def down_weight_rows(latent_weight, index_proj, piece, high, early):
    share = DZ // N_SEQ

    def own_rows(weight):
        columns = weight.T.reshape(weight.shape[1], NZ, DZ)
        return lax.dynamic_slice_in_dim(columns, piece * share, share, 2)

    own = jnp.concatenate([own_rows(latent_weight), own_rows(index_proj)], axis=0)
    own = with_layout_constraint(own, Layout(major_to_minor=(0, 1, 2)))
    mine = lax.all_to_all(own.transpose(1, 2, 0), "z", 0, 0)
    theirs = swap(mine, "yh")
    pair = [jnp.where(high == 0, mine, theirs), jnp.where(high == 0, theirs, mine)]
    by_head = jnp.stack(pair, axis=1).reshape(N_HEAD, share, own.shape[0]).transpose(1, 0, 2)
    local = latent_weight.shape[1]
    wide = jnp.concatenate(
        [
            by_head[:, :, :local].reshape(share, QL),
            by_head[:, :, local:].reshape(share, IHEADS),
            jnp.zeros((share, 64), jnp.bfloat16),
        ],
        axis=1,
    )
    wide, early = lax.optimization_barrier((wide, early))
    half = lax.all_to_all(jnp.broadcast_to(wide[None], (8,) + wide.shape), ("x", "yl"), 0, 0)
    half = half.reshape(8 * share, wide.shape[1])
    return half, swap(half, "c"), early


def turn(values):
    moves = [(s * N_HEAD + h, h * N_HEAD + s) for s in range(N_SEQ) for h in range(N_HEAD)]
    return lax.ppermute(values, SEQ + HEAD, moves)


def shards(
    attn_out,
    out_weight,
    residual,
    norm_gain,
    latent_weight,
    index_proj,
    latent_gain,
    index_weight,
    index_keys,
    positions,
    cache_len,
):
    x, yl, c = (lax.axis_index(a) for a in SEQ)
    z, yh = (lax.axis_index(a) for a in HEAD)
    seq = (x * 2 + yl) * 2 + c
    head = z * 2 + yh
    rows = attn_out.shape[0]
    own = rows // N_HEAD
    local = latent_weight.shape[1]

    partial, half_weight = project(
        jnp.stack([head * 2 + c]).astype(jnp.int32), attn_out, out_weight, residual, index_weight
    )
    summed = lax.psum_scatter(partial, "z", scatter_dimension=0, tiled=False)

    weight_mine = swap(half_weight, "yh")
    down_mine, down_other, weight_mine = down_weight_rows(
        latent_weight, index_proj, c * 8 + x * 2 + yl, yh, weight_mine
    )
    weight_theirs = swap(weight_mine, "c")
    summed, index_keys, down_mine, down_other = lax.optimization_barrier(
        (summed, index_keys, down_mine, down_other)
    )
    all_keys = lax.all_gather(index_keys, SEQ, axis=0, tiled=True)
    kept, got = summed[0], swap(summed[1], "yh")
    gain = lax.dynamic_slice_in_dim(norm_gain, z * DZ, DZ).reshape(1, DZ)
    hidden, lifted = lift(jnp.stack([c]).astype(jnp.int32), kept, got, gain, down_mine, down_other)
    lifted, weight_theirs = lax.optimization_barrier((lifted, weight_theirs))
    parts = from_last(lifted.reshape(NZ, own, lifted.shape[1]))
    packed, give = normalize(
        jnp.stack([yh]).astype(jnp.int32), parts, latent_gain.reshape(1, QL)
    )
    turned, beside = lax.optimization_barrier((turn(packed), swap(give, "yh")))
    everyone = from_last(jnp.broadcast_to(turned[None, :, :QL], (NZ, own, QL)))
    everyone, hidden = lax.optimization_barrier((everyone.reshape(HALF, QL), hidden))
    all_hidden = lax.all_gather(hidden, "z", axis=0, tiled=False)
    hidden_rows = lax.dynamic_slice_in_dim(all_hidden, (NZ - 1 - z) * own, own, 1)
    hidden_rows = hidden_rows.transpose(1, 0, 2).reshape(own, D)
    place = jnp.stack([c, yh]).astype(jnp.int32)
    queries = make_queries(place, everyone, index_weight, weight_mine, weight_theirs, packed, beside)
    queries = from_last(queries)
    latent_out = queries[::-1, 8:, :, :local].reshape(rows, local)
    scores = make_scores(queries, turned[:, QL:], all_keys)
    scores = lax.all_to_all(scores, SEQ, 0, 0, axis_index_groups=[list(range(N_SEQ))[::-1]])

    own_positions = lax.dynamic_slice_in_dim(positions, head * rows, rows).reshape(rows, 1)
    numbers = jnp.stack([cache_len[0], seq * SLOTS]).astype(jnp.int32)
    return (hidden_rows, latent_out, finish(numbers, scores, own_positions))


def solution(mesh):
    fine = Mesh(mesh.devices.reshape(4, 2, 2, 8, 2), SEQ + HEAD)
    in_specs = (
        P(SEQ, HEAD),
        P(HEAD, None),
        P(SEQ + HEAD, None),
        P(),
        P(None, HEAD),
        P(None, HEAD),
        P(),
        P(None, HEAD),
        P(SEQ, None),
        P(),
        P(SEQ),
    )
    out_specs = (P(SEQ + HEAD, None), P(SEQ, HEAD), P(HEAD, SEQ))
    return jax.shard_map(shards, mesh=fine, in_specs=in_specs, out_specs=out_specs, check_vma=False)
```
